128 devices in a mesh: tm: 2 (over z_hi), clip: 64 (over z_lo, x, y, core).
Axes of the slice: x: 4, y: 4, z: 4 (z_hi: 2, z_lo: 2; z = z_hi * 2 + z_lo), core: 2. Of those that a mesh axis runs over, the one named last changes fastest.
Arguments:
- frames: bfloat16 [16384, 16, 1408], P('clip', 'tm'), may hold values from -32 to 32
- key_proj: bfloat16 [1408, 16], replicated, may hold values from -2 to 2
- value_weight: bfloat16 [1408, 1408], replicated, may hold values from -0.15625 to 0.15625
- out_weight: bfloat16 [1408, 512], replicated, may hold values from -0.15625 to 0.15625
- texts: bfloat16 [16384, 512], P(('tm', 'clip')), may hold values from -6 to 6
- logit_scale: float32 [1], replicated, may hold values from 4 to 12
- logit_bias: float32 [1], replicated, may hold values from -8 to -4
Outputs:
- grad_frames: bfloat16 [16384, 16, 1408], P('clip', 'tm')
- grad_texts: float32 [16384, 512], P(('tm', 'clip'))
The draws below stay inside these ranges and needn't reach their ends.
All inputs are finite; a program needn't handle non-finite values.
Results may differ from the reference program's by a relative error of at most 0.02.
Values may be sent and summed in bfloat16 or wider, within the bound.
A program may use at most 192 MiB of HBM per device.

```python
import math
import jax
import jax.numpy as jnp
from jax import lax

D = 1408
H = 16
HD = 88
E = 512
FRAMES = 16
CLIP_DEV = 256
CLIPS = 16384


def key_columns(key):
    column_key = jax.random.fold_in(key, 101)
    sign_key, size_key = jax.random.split(column_key)
    signs_table = jnp.where(jax.random.bernoulli(sign_key, 0.5, (D, H)), 1.0, -1.0).astype(jnp.float32)
    magnitude = jax.random.uniform(size_key, (D, H), jnp.float32, 0.5, 2.0)
    return (signs_table, magnitude)


def draw_key_proj(key, part):
    signs_table, magnitude = key_columns(key)
    return (signs_table * magnitude).astype(jnp.bfloat16)


def align_rows(plain_part, noise_part, signs_table):
    clip_index = jnp.arange(CLIPS)
    chosen = clip_index % 5 == 0
    amplitude = min(30.0, 260.0 / (1.25 * math.sqrt(D)))
    strength = amplitude * (0.7 + 0.15 * (clip_index % 3).astype(jnp.float32))
    aligned = signs_table.T[clip_index % H]
    frame_factor = jnp.where(jnp.arange(FRAMES) == 0, 1.0, 0.993)
    target = strength[:, None, None] * frame_factor[None, :, None] * aligned[:, None, :] + 0.1 * noise_part
    target = jnp.clip(target, -32.0, 32.0)
    align_mask = chosen[:, None, None] & (jnp.arange(FRAMES) < 2)[None, :, None]
    return jnp.where(align_mask, target, plain_part).astype(jnp.bfloat16)


def draw_frames(key, part):
    signs_table, magnitude = key_columns(key)
    key = jax.random.fold_in(key, 2)
    noise_key = jax.random.fold_in(key, 0)
    full_shape = (CLIPS, FRAMES, D)
    noise_part = jax.random.truncated_normal(noise_key, -8.0, 8.0, full_shape, jnp.float32)
    return align_rows(noise_part, noise_part, signs_table)


def level_of(stream_key, shape, pieces, low, top_value):
    loudness, own = 1.0, jax.random.fold_in(stream_key, 6)
    for axis_at, blocks in pieces:
        draws = jnp.exp(jax.random.uniform(jax.random.fold_in(own, axis_at), (blocks,), jnp.float32, low / len(pieces), top_value / len(pieces)))
        loudness = loudness * jnp.repeat(draws, shape[axis_at] // blocks).reshape([-1 if axis == axis_at else 1 for axis in range(len(shape))])
    return loudness


def noise(stream_key, extent, deviation, reach, cuts=(), kind=jnp.bfloat16):
    drawn = deviation * jax.random.normal(stream_key, extent, jnp.float32)
    if cuts:
        drawn = drawn * level_of(stream_key, extent, cuts, -0.22, 0.18)
    return jnp.clip(drawn, -reach, reach).astype(kind)


def setup_inputs(seed: int = 0) -> dict:
    seeds = jax.random.split(jax.random.key(seed), 8)
    return {
        "frames": draw_frames(jax.random.fold_in(seeds[7], 71), 0),
        "key_proj": draw_key_proj(jax.random.fold_in(seeds[7], 71), 0),
        "value_weight": noise(seeds[2], (D, D), D ** -0.5, 0.15625),
        "out_weight": noise(seeds[3], (D, E), D ** -0.5, 0.15625),
        "texts": noise(seeds[4], (CLIPS, E), 1.0, 6.0, ((0, 128),)),
        "logit_scale": jnp.clip(jax.random.uniform(seeds[5], (1,), jnp.float32, 4.0, 12.0), 4.0, 12.0),
        "logit_bias": jnp.clip(jax.random.uniform(seeds[6], (1,), jnp.float32, -8.0, -4.0), -8.0, -4.0),
    }


EPSILON = 1e-06

def pool_block(clip_block, key_proj, value_weight):
    block_clips, frame_count, model_width = clip_block.shape
    head_count = key_proj.shape[1]
    head_size = model_width // head_count
    frame_rows = clip_block.reshape(block_clips * frame_count, model_width)
    scores = jnp.dot(frame_rows, key_proj, preferred_element_type=jnp.float32).reshape(block_clips, frame_count, head_count) * (1.0 / math.sqrt(model_width))
    values = jnp.dot(frame_rows, value_weight, preferred_element_type=jnp.float32).astype(jnp.bfloat16)
    values = values.reshape(block_clips, frame_count, head_count, head_size)
    weights = jax.nn.softmax(scores, axis=1)
    pooled_sum = jnp.einsum('bfh,bfhk->bhk', weights, values.astype(jnp.float32)).reshape(block_clips, model_width)
    return (weights, values, pooled_sum)

def reference(frames, key_proj, value_weight, out_weight, texts, logit_scale, logit_bias):
    block_count = CLIPS // CLIP_DEV
    clip_blocks = frames.reshape(block_count, CLIP_DEV, FRAMES, D)
    pooled_sum = lax.map(lambda clip_block: pool_block(clip_block, key_proj, value_weight)[2], clip_blocks).reshape(CLIPS, D)
    pooled = pooled_sum.astype(jnp.bfloat16)
    embedding = jnp.dot(pooled, out_weight, preferred_element_type=jnp.float32)
    vis_norm = jnp.sqrt(lax.optimization_barrier(jnp.sum(embedding * embedding, axis=1, keepdims=True)) + EPSILON)
    vis_unit = embedding / vis_norm
    vis_half = vis_unit.astype(jnp.bfloat16)
    text_full = texts.astype(jnp.float32)
    text_norm = jnp.sqrt(lax.optimization_barrier(jnp.sum(text_full * text_full, axis=1, keepdims=True)) + EPSILON)
    text_unit = text_full / text_norm
    text_half = text_unit.astype(jnp.bfloat16)
    inverse = 1.0 / CLIPS
    text_ids = jnp.arange(CLIPS, dtype=jnp.int32)

    def loss_step(text_grad, inputs):
        vis_block, first_row = inputs
        logits = lax.dot_general(vis_block, text_half, (((1,), (1,)), ((), ())), preferred_element_type=jnp.float32) * logit_scale[0] + logit_bias[0]
        clip_ids = first_row + jnp.arange(CLIP_DEV, dtype=jnp.int32)
        target_sign = jnp.where(clip_ids[:, None] == text_ids[None, :], 1.0, -1.0)
        logit_grad = (logit_scale[0] * (-inverse * target_sign * jax.nn.sigmoid(-target_sign * logits))).astype(jnp.bfloat16)
        vis_grad = jnp.dot(logit_grad, text_half, preferred_element_type=jnp.float32)
        text_grad = text_grad + lax.dot_general(logit_grad, vis_block, (((0,), (0,)), ((), ())), preferred_element_type=jnp.float32)
        return (text_grad, vis_grad)
    first_rows = (jnp.arange(block_count) * CLIP_DEV).astype(jnp.int32)
    start_state = jnp.zeros((CLIPS, E), jnp.float32)
    text_grad, vis_grad = lax.scan(loss_step, start_state, (vis_half.reshape(block_count, CLIP_DEV, E), first_rows))
    vis_grad = vis_grad.reshape(CLIPS, E)
    grad_texts = (text_grad - text_unit * lax.optimization_barrier(jnp.sum(text_grad * text_unit, axis=1, keepdims=True))) / text_norm
    emb_grad = ((vis_grad - vis_unit * lax.optimization_barrier(jnp.sum(vis_grad * vis_unit, axis=1, keepdims=True))) / vis_norm).astype(jnp.bfloat16)
    pooled_grad = lax.dot_general(emb_grad, out_weight, (((1,), (1,)), ((), ())), preferred_element_type=jnp.float32)

    def back_block(inputs):
        clip_block, grad_block = inputs
        weights, values, block_pooled = pool_block(clip_block, key_proj, value_weight)
        block_clips = clip_block.shape[0]
        split_grad = grad_block.reshape(block_clips, 1, H, HD)
        value_grad = (weights[:, :, :, None] * split_grad).astype(jnp.bfloat16).reshape(block_clips * FRAMES, D)
        spread = split_grad * (values.astype(jnp.float32) - block_pooled.reshape(block_clips, 1, H, HD))
        inner_sum = lax.optimization_barrier(jnp.sum(spread, axis=3))
        score_grad = (weights * inner_sum * (1.0 / math.sqrt(D))).astype(jnp.bfloat16).reshape(block_clips * FRAMES, H)
        total = lax.dot_general(value_grad, value_weight, (((1,), (1,)), ((), ())), preferred_element_type=jnp.float32)
        total = total + lax.dot_general(score_grad, key_proj, (((1,), (1,)), ((), ())), preferred_element_type=jnp.float32)
        return total.astype(jnp.bfloat16).reshape(block_clips, FRAMES, D)
    grad_frames = lax.map(back_block, (clip_blocks, pooled_grad.reshape(block_count, CLIP_DEV, D))).reshape(CLIPS, FRAMES, D)
    return (grad_frames, grad_texts)
```

```python
import functools
import math

import jax
import jax.numpy as jnp
from jax import lax
from jax.experimental import pallas as pl
from jax.experimental.pallas import tpu as pltpu
from jax.sharding import PartitionSpec as P

EPSILON = 1e-06
MESH = pl.DeviceIdType.MESH
BF = jnp.bfloat16
F32 = jnp.float32
NT = (((1,), (1,)), ((), ()))
TN = (((0,), (0,)), ((), ()))
HEADS = 16
GROUP = 16


def nt(a, b):
    return lax.dot_general(a, b, NT, preferred_element_type=F32)


def tn(a, b):
    return lax.dot_general(a, b, TN, preferred_element_type=F32)


def nn(a, b):
    return jnp.dot(a, b, preferred_element_type=F32)


def split_nn(a, b):
    high = a.astype(BF)
    low = (a - high.astype(F32)).astype(BF)
    return nn(high, b) + nn(low, b)


def own_clip_mask(rows_per_clip):
    shape = (GROUP * rows_per_clip, HEADS * GROUP)
    row = lax.broadcasted_iota(jnp.int32, shape, 0)
    lane = lax.broadcasted_iota(jnp.int32, shape, 1) & (GROUP - 1)
    start = lane * rows_per_clip
    return jnp.where((row >= start) & (row < start + rows_per_clip), 1.0, 0.0)


def repeat_heads(key_ref, out_ref):
    for h in range(HEADS):
        row = key_ref[h : h + 1, :].astype(F32)
        wide = jnp.broadcast_to(row, (GROUP, row.shape[1])).astype(BF)
        out_ref[h * GROUP : (h + 1) * GROUP, :] = wide


def main_kernel(
    dims,
    frames_hbm, key_hbm, value_hbm, out_hbm, texts_hbm, scale_ref, bias_ref,
    vp_hbm, sg_hbm, gt_hbm,
    key_ref, texts_ref, gt_ref,
    x_s, w_s, ow_s, key_s, pq_s, e_s, ms_send, ms_recv, alpha_s, acc_s, a_s, sg_s, t_s,
    tt_s, tg_s, rsib_s, r1_s, r2_s, tr_s, q1_s, q2_s, g_s,
    embp_s, embr_s, vu_s, vn_s, v_s, vg_s, vgb_s, g1_s, g2_s, eg_s, egr_s, pg_s, u_send, u_recv,
    load_sem, out_sem, send_sem, recv_sem,
):
    clips, width, head, emb, all_clips = dims
    frames_here = 8
    rows = clips * frames_here
    groups = clips // GROUP
    half_clips = clips // 2
    root = 1.0 / math.sqrt(width)

    tm = lax.axis_index("tm")
    ci = lax.axis_index("clip")
    core = lax.rem(ci, 2)
    y = lax.rem(ci // 2, 4)
    x = lax.rem(ci // 8, 4)
    z_lo = ci // 32
    z = tm * 2 + z_lo

    def at(xx, yy, zz, cc):
        return (zz // 2, ((lax.rem(zz, 2) * 4 + xx) * 4 + yy) * 2 + cc)

    def up(a, n):
        return lax.rem(a + n, 4)

    p1 = x * (1 - core) + y * core
    p2 = y * (1 - core) + x * core

    def plane(a1, a2):
        return at(a1 * (1 - core) + a2 * core, a2 * (1 - core) + a1 * core, z, core)

    n1p, n1m = plane(up(p1, 1), p2), plane(up(p1, 3), p2)
    n2p, n2m = plane(p1, up(p2, 1)), plane(p1, up(p2, 3))
    zp, zm = at(x, y, up(z, 1), core), at(x, y, up(z, 3), core)
    partner = (1 - tm, ci)
    sibling = at(x, y, z, 1 - core)

    counter = [0]

    def remote(src, dst, device):
        k = counter[0]
        counter[0] += 1
        return pltpu.make_async_remote_copy(
            src_ref=src, dst_ref=dst, send_sem=send_sem.at[k], recv_sem=recv_sem.at[k],
            device_id=device, device_id_type=MESH,
        )

    chunk = rows // 4
    loads = [
        pltpu.make_async_copy(
            frames_hbm.at[pl.ds(i * chunk, chunk)], x_s.at[pl.ds(i * chunk, chunk)], load_sem.at[i]
        )
        for i in range(4)
    ]
    load_w = pltpu.make_async_copy(value_hbm, w_s, load_sem.at[4])
    load_ow = pltpu.make_async_copy(out_hbm, ow_s, load_sem.at[5])
    load_key = pltpu.make_async_copy(key_hbm, key_ref, load_sem.at[6])
    load_texts = pltpu.make_async_copy(texts_hbm, texts_ref, load_sem.at[7])
    load_texts.start()
    load_key.start()
    for load in loads:
        load.start()
    load_w.start()
    load_ow.start()

    barrier = pltpu.get_barrier_semaphore()
    greet = (n1p, n1m, n2p, n2m, zp, zm, partner, sibling)
    for device in greet:
        pl.semaphore_signal(barrier, inc=1, device_id=device, device_id_type=MESH)

    load_texts.wait()
    text_full = texts_ref[...].astype(F32)
    text_norm = jnp.sqrt(jnp.sum(text_full * text_full, axis=1, keepdims=True) + EPSILON)
    tt_s[1, p2, p1] = (text_full / text_norm).astype(BF)
    load_key.wait()
    repeat_heads(key_ref, key_s)

    pl.semaphore_wait(barrier, len(greet))

    sent = []

    def go(*copies):
        for copy in copies:
            copy.start()
            sent.append(copy)

    own = tt_s.at[1]
    a0p = remote(own.at[p2, p1], own.at[p2, p1], n1p)
    a0m = remote(own.at[p2, p1], own.at[p2, p1], n1m)
    go(a0p, a0m)

    mask = own_clip_mask(frames_here)
    clip_mask = own_clip_mask(1)
    lanes = HEADS * GROUP

    def own_lane(per_clip):
        picked = per_clip.reshape(per_clip.shape[0] // GROUP, GROUP, lanes) * clip_mask[None]
        return jnp.sum(picked, axis=1)

    for i in range(4):
        loads[i].wait()
        part = pl.ds(i * chunk, chunk)
        s = nt(x_s[part, :], key_s[...]) * root
        s3 = s.reshape(chunk // frames_here, frames_here, lanes)
        top = jnp.max(s3, axis=1)
        e3 = jnp.exp(s3 - top[:, None, :])
        e_s[part, :] = e3.reshape(chunk, lanes)
        group_part = pl.ds(i * groups // 4, groups // 4)
        ms_send[0, group_part, :] = own_lane(top)
        ms_send[1, group_part, :] = own_lane(jnp.sum(e3, axis=1))
    ms = remote(ms_send, ms_recv, partner)
    go(ms)

    def a1():
        a0p.wait_recv()
        a0m.wait_recv()
        low, high = pl.ds(0, 64), pl.ds(64, 64)
        b1, b3 = up(p1, 3), up(p1, 1)
        cp = remote(own.at[p2, b1, low], own.at[p2, b1, low], n1p)
        cm = remote(own.at[p2, b3, high], own.at[p2, b3, high], n1m)
        go(cp, cm)
        return cp, cm

    def sib_row(row):
        copy = remote(own.at[row], tt_s.at[0, row], sibling)
        go(copy)
        return copy

    fwd1 = a1()

    columns = [slice(at, min(at + 256, width)) for at in range(0, width, 256)]

    def pool_group(g, carry):
        frame_part = pl.ds(pl.multiple_of(g * 128, 128), 128)
        clip_part = pl.ds(pl.multiple_of(g * GROUP, GROUP), GROUP)
        weight = jnp.transpose(e_s[frame_part, :] * mask).astype(BF)
        for cols in columns:
            pooled = nn(weight, x_s[frame_part, cols]).astype(BF)
            pq_s[:, clip_part, cols] = pooled.reshape(HEADS, GROUP, pooled.shape[1])
        return carry

    lax.fori_loop(0, groups // 2, pool_group, 0, unroll=4)

    for copy in fwd1:
        copy.wait_recv()
    row_p = remote(own.at[p2], own.at[p2], n2p)
    row_m = remote(own.at[p2], own.at[p2], n2m)
    go(row_p, row_m)
    sib0 = sib_row(p2)

    lax.fori_loop(groups // 2, groups, pool_group, 0, unroll=4)

    load_w.wait()
    load_ow.wait()
    acc_s[...] = jnp.zeros_like(acc_s)

    pairs = []
    for h in range(0, HEADS, 2):
        first = min(h * head // 128, width // 128 - 2) * 128
        wide = 256 if (h + 2) * head <= first + 256 else 384
        pairs.append((h, first, wide))

    def window_mask(h, first, wide):
        lane = lax.broadcasted_iota(jnp.int32, (1, wide), 1)
        offset = h * head - first
        return (lane >= offset) & (lane < offset + head)

    for h, first, wide in pairs:
        cols = slice(first, first + wide)
        part = nn(pq_s[h : h + 2].reshape(2 * clips, width), w_s[:, cols])
        acc_s[:, cols] += jnp.where(window_mask(h, first, wide), part[:clips], 0.0) + jnp.where(
            window_mask(h + 1, first, wide), part[clips:], 0.0
        )

    ms.wait_recv()
    mine, theirs = ms_send[0], ms_recv[0]
    top = jnp.maximum(mine, theirs)
    mine_f, theirs_f = jnp.exp(mine - top), jnp.exp(theirs - top)
    alpha = mine_f / (ms_send[1] * mine_f + ms_recv[1] * theirs_f)
    alpha_s[...] = alpha
    spread = (alpha[:, None, :] * clip_mask[None]).reshape(clips, lanes)
    head_start = (lax.broadcasted_iota(jnp.int32, (lanes, width), 0) // GROUP) * head
    head_lane = lax.broadcasted_iota(jnp.int32, (lanes, width), 1)
    in_head = (head_lane >= head_start) & (head_lane < head_start + head)
    pooled = (acc_s[...] * split_nn(spread, jnp.where(in_head, 1.0, 0.0).astype(BF))).astype(BF)
    embp_s[...] = nn(pooled, ow_s[...]).astype(BF).reshape(2, half_clips, emb)
    er_p = remote(embp_s.at[up(z, 1) // 2], embr_s.at[0], zp)
    er_m = remote(embp_s.at[up(z, 3) // 2], embr_s.at[1], zm)
    go(er_p, er_m)

    row_p.wait_recv()
    row_m.wait_recv()
    r1, r3 = up(p2, 3), up(p2, 1)
    low, high = pl.ds(0, 2), pl.ds(2, 2)
    fwd_p = remote(own.at[r1, low], own.at[r1, low], n2p)
    fwd_m = remote(own.at[r3, high], own.at[r3, high], n2m)
    go(fwd_p, fwd_m)
    sib1 = sib_row(r3)
    sib2 = sib_row(r1)

    def weights(g, carry):
        frame_part = pl.ds(pl.multiple_of(g * 128, 128), 128)
        wide = e_s[frame_part, :] * mask * alpha_s[pl.ds(g, 1), :]
        e_s[frame_part, :] = wide
        a_s[frame_part, :] = wide.astype(BF)
        return carry

    lax.fori_loop(0, groups // 2, weights, 0, unroll=4)

    er_p.wait_recv()
    er_m.wait_recv()
    embedding = embr_s[0].astype(F32) + embr_s[1].astype(F32)
    vis_norm = jnp.sqrt(jnp.sum(embedding * embedding, axis=1, keepdims=True) + EPSILON)
    vis_unit = embedding / vis_norm
    vu_s[...] = vis_unit
    vn_s[...] = jnp.broadcast_to(vis_norm, vn_s.shape)
    v_s[z] = vis_unit.astype(BF)
    v_p = remote(v_s.at[z], v_s.at[z], zp)
    v_m = remote(v_s.at[z], v_s.at[z], zm)
    go(v_p, v_m)
    lax.fori_loop(groups // 2, groups, weights, 0, unroll=4)
    v_p.wait_recv()
    v_m.wait_recv()
    z1, z2, z3 = up(z, 1), up(z, 2), up(z, 3)
    hlow, hhigh = pl.ds(0, half_clips // 2), pl.ds(half_clips // 2, half_clips // 2)
    v_fp = remote(v_s.at[z3, hlow], v_s.at[z3, hlow], zp)
    v_fm = remote(v_s.at[z1, hhigh], v_s.at[z1, hhigh], zm)
    go(v_fp, v_fm)

    fwd_p.wait_recv()
    fwd_m.wait_recv()
    sib3 = sib_row(up(p2, 2))
    v_fp.wait_recv()
    v_fm.wait_recv()

    vg_s[...] = jnp.zeros_like(vg_s)
    slope = 0.5 * scale_ref[0]
    shift = 0.5 * bias_ref[0]
    diff = lax.broadcasted_iota(jnp.int32, (128, 128), 0) - lax.broadcasted_iota(
        jnp.int32, (128, 128), 1
    )
    vis_base = [
        (((1 - zz % 2) * 4 + x) * 4 + y) * 2 * clips + core * clips + (zz // 2) * half_clips
        for zz in range(4)
    ]

    def text_base(whose, a2, a1):
        c = core * whose + (1 - core) * (1 - whose)
        xx = a1 * (1 - c) + a2 * c
        yy = a2 * (1 - c) + a1 * c
        return (tm * 64 + ((z_lo * 4 + xx) * 4 + yy) * 2 + c) * 128

    def pair_row(whose, row):
        vis = v_s[...].reshape(4 * half_clips, emb)
        total = None
        for hh in range(2):
            texts = tt_s[whose, row, pl.ds(2 * hh, 2)].reshape(256, emb)
            curve = jnp.tanh(nt(vis, texts) * slope + shift) * 0.5
            tall = []
            for zz in range(4):
                wide = []
                for b in range(2):
                    gap = text_base(whose, row, 2 * hh + b) - vis_base[zz]
                    block = curve[zz * 128 : (zz + 1) * 128, b * 128 : (b + 1) * 128]
                    wide.append(block + jnp.where(diff == gap, -0.5, 0.5))
                tall.append(jnp.concatenate(wide, axis=1))
            grad = jnp.concatenate(tall, axis=0).astype(BF)
            g_s[whose, row, hh] = grad
            part = nn(grad, texts)
            total = part if total is None else total + part
        vg_s[...] += total

    def pair_rows(whose):
        def body(row, carry):
            pair_row(whose, row)
            return carry

        lax.fori_loop(0, 4, body, 0)

    pair_rows(1)
    for copy in (sib0, sib1, sib2, sib3):
        copy.wait_recv()
    pair_rows(0)

    vgb_s[...] = vg_s[...].astype(BF).reshape(4, half_clips, emb)
    g1p = remote(vgb_s.at[z2, hlow], g1_s.at[0], zp)
    g1m = remote(vgb_s.at[z2, hhigh], g1_s.at[1], zm)
    g2p = remote(vgb_s.at[z1, hhigh], g2_s.at[0, hhigh], zp)
    g2m = remote(vgb_s.at[z3, hlow], g2_s.at[1, hlow], zm)
    go(g1p, g1m, g2p, g2m)

    sib_base = counter[0]
    counter[0] += 4

    def sib_copy(rr, row):
        return pltpu.make_async_remote_copy(
            src_ref=tg_s.at[0, row], dst_ref=rsib_s.at[row],
            send_sem=send_sem.at[sib_base + rr], recv_sem=recv_sem.at[sib_base + rr],
            device_id=sibling, device_id_type=MESH,
        )

    def ordered(p, rr):
        return lax.rem(p + 2 + 3 * rr + 3 * (rr // 2) + 2 * (rr // 3), 4)

    def text_terms(whose, row):
        vis = v_s[...].reshape(4 * half_clips, emb)
        grad = jnp.concatenate([g_s[whose, row, 0], g_s[whose, row, 1]], axis=1)
        return tn(grad, vis).reshape(4, 128, emb)

    def sib_rows(rr, carry):
        row = ordered(p1, rr)
        tg_s[0, row] = text_terms(0, row).astype(BF)
        sib_copy(rr, row).start()
        return carry

    lax.fori_loop(0, 4, sib_rows, 0)

    g1p.wait_recv()
    g1m.wait_recv()
    vgb_s[z1, hlow] = (vgb_s[z1, hlow].astype(F32) + g1_s[0].astype(F32)).astype(BF)
    g3p = remote(vgb_s.at[z1, hlow], g2_s.at[0, hlow], zp)
    vgb_s[z3, hhigh] = (vgb_s[z3, hhigh].astype(F32) + g1_s[1].astype(F32)).astype(BF)
    g3m = remote(vgb_s.at[z3, hhigh], g2_s.at[1, hhigh], zm)
    go(g3p, g3m)

    def own_rows(rr, carry):
        row = ordered(p2, rr)
        sib_copy(rr, row).wait_recv()
        tg_s[1, row] = (text_terms(1, row) + rsib_s[row].astype(F32)).astype(BF)
        return carry

    tg = tg_s.at[1]
    lax.fori_loop(0, 1, own_rows, 0)
    s1p = remote(tg.at[up(p2, 2), low], r1_s.at[0], n2p)
    s1m = remote(tg.at[up(p2, 2), high], r1_s.at[1], n2m)
    go(s1p, s1m)
    lax.fori_loop(1, 2, own_rows, 0)
    s2p = remote(tg.at[r3, high], r2_s.at[0, high], n2p)
    go(s2p)
    lax.fori_loop(2, 3, own_rows, 0)
    s2m = remote(tg.at[r1, low], r2_s.at[1, low], n2m)
    go(s2m)

    for copy in (g2p, g2m, g3p, g3m):
        copy.wait_recv()
    out_scale = scale_ref[0] * (1.0 / all_clips)
    vis_grad = (
        vg_s[pl.ds(pl.multiple_of(z * half_clips, 128), half_clips), :]
        + g2_s[0].astype(F32)
        + g2_s[1].astype(F32)
    ) * out_scale
    unit = vu_s[...]
    inner = jnp.sum(vis_grad * unit, axis=1, keepdims=True)
    eg_s[...] = ((vis_grad - unit * inner) / vn_s[:, :1]).astype(BF)
    eg_p = remote(eg_s, egr_s.at[tm], zp)
    eg_m = remote(eg_s, egr_s.at[tm], zm)
    go(eg_p, eg_m)

    lax.fori_loop(3, 4, own_rows, 0)
    s1p.wait_recv()
    s1m.wait_recv()
    tg_s[1, r3, low] = (tg_s[1, r3, low].astype(F32) + r1_s[0].astype(F32)).astype(BF)
    s3p = remote(tg.at[r3, low], r2_s.at[0, low], n2p)
    go(s3p)
    tg_s[1, r1, high] = (tg_s[1, r1, high].astype(F32) + r1_s[1].astype(F32)).astype(BF)
    s3m = remote(tg.at[r1, high], r2_s.at[1, high], n2m)
    go(s3m)

    eg_p.wait_recv()
    eg_m.wait_recv()
    pg_s[...] = nt(egr_s[...].reshape(clips, emb), ow_s[...]).astype(BF)

    for h, first, wide in pairs:
        grads = pg_s[:, first : first + wide].astype(F32)
        part = jnp.concatenate(
            [jnp.where(window_mask(h + i, first, wide), grads, 0.0).astype(BF) for i in range(2)],
            axis=0,
        )
        for cols in columns:
            q = nt(part, w_s[cols, first : first + wide]).astype(BF)
            pq_s[h : h + 2, :, cols] = q.reshape(2, clips, q.shape[1])

    def score_terms(g, carry):
        frame_part = pl.ds(pl.multiple_of(g * 128, 128), 128)
        clip_part = pl.ds(pl.multiple_of(g * GROUP, GROUP), GROUP)
        q = pq_s[:, clip_part, :].reshape(lanes, width)
        prod = jnp.transpose(nt(q, x_s[frame_part, :]))
        t_s[frame_part, :] = prod
        u_send[pl.ds(g, 1), :] = jnp.sum(prod * e_s[frame_part, :], axis=0, keepdims=True)
        return carry

    lax.fori_loop(0, groups, score_terms, 0, unroll=4)
    uc = remote(u_send, u_recv, partner)
    uc.start()

    for copy in (s2p, s2m, s3p, s3m):
        copy.wait_recv()
    for b in range(4):
        total = tg_s[1, p2, b].astype(F32) + r2_s[0, b].astype(F32) + r2_s[1, b].astype(F32)
        tr_s[b] = total.astype(BF)
    b1, b2, b3 = up(p1, 1), up(p1, 2), up(p1, 3)
    tlow, thigh = pl.ds(0, 64), pl.ds(64, 64)
    u1p = remote(tr_s.at[b2, tlow], q1_s.at[0], n1p)
    u1m = remote(tr_s.at[b2, thigh], q1_s.at[1], n1m)
    u2p = remote(tr_s.at[b1, thigh], q2_s.at[0, thigh], n1p)
    u2m = remote(tr_s.at[b3, tlow], q2_s.at[1, tlow], n1m)
    go(u1p, u1m, u2p, u2m)

    def vp_copy(g):
        frame_part = pl.ds(pl.multiple_of(g * 128, 128), 128)
        return pltpu.make_async_copy(
            x_s.at[frame_part], vp_hbm.at[frame_part], out_sem.at[g]
        )

    def value_part(g, carry):
        frame_part = pl.ds(pl.multiple_of(g * 128, 128), 128)
        clip_part = pl.ds(pl.multiple_of(g * GROUP, GROUP), GROUP)
        for cols in columns:
            q = pq_s[:, clip_part, cols]
            q = q.reshape(lanes, q.shape[2])
            x_s[frame_part, cols] = nn(a_s[frame_part, :], q).astype(BF)
        vp_copy(g).start()
        return carry

    lax.fori_loop(0, groups // 2, value_part, 0, unroll=4)
    u1p.wait_recv()
    u1m.wait_recv()
    tr_s[b1, tlow] = (tr_s[b1, tlow].astype(F32) + q1_s[0].astype(F32)).astype(BF)
    u3p = remote(tr_s.at[b1, tlow], q2_s.at[0, tlow], n1p)
    tr_s[b3, thigh] = (tr_s[b3, thigh].astype(F32) + q1_s[1].astype(F32)).astype(BF)
    u3m = remote(tr_s.at[b3, thigh], q2_s.at[1, thigh], n1m)
    go(u3p, u3m)

    lax.fori_loop(groups // 2, groups, value_part, 0, unroll=4)

    for copy in (u2p, u2m, u3p, u3m):
        copy.wait_recv()
    gt_ref[...] = (
        tr_s[p1].astype(F32) + q2_s[0].astype(F32) + q2_s[1].astype(F32)
    ) * out_scale
    gt_out = pltpu.make_async_copy(gt_ref, gt_hbm, load_sem.at[8])
    gt_out.start()

    uc.wait()
    u_send[...] = u_send[...] + u_recv[...]

    def score_grads(g, carry):
        frame_part = pl.ds(pl.multiple_of(g * 128, 128), 128)
        centred = t_s[frame_part, :] - u_send[pl.ds(g, 1), :]
        sg_s[frame_part, :] = (e_s[frame_part, :] * centred * root).astype(BF)
        return carry

    sg_out = []
    for i in range(2):
        lax.fori_loop(i * groups // 2, (i + 1) * groups // 2, score_grads, 0, unroll=4)
        part = pl.ds(i * rows // 2, rows // 2)
        sg_out.append(pltpu.make_async_copy(sg_s.at[part], sg_hbm.at[part], load_sem.at[9 + i]))
        sg_out[i].start()

    for copy in sent:
        copy.wait_send()

    def drain(rr, carry):
        sib_copy(rr, ordered(p1, rr)).wait_send()
        return carry

    lax.fori_loop(0, 4, drain, 0)

    def drain_vp(g, carry):
        vp_copy(g).wait()
        return carry

    lax.fori_loop(0, groups, drain_vp, 0)
    for copy in sg_out:
        copy.wait()
    gt_out.wait()


def final_kernel(
    vp_hbm, sg_hbm, key_hbm, texts_hbm, tg_hbm, out_hbm, gt_hbm,
    vp_s, sg_s, key_in, key_s, texts_s, tg_s, gt_s, vp_sem, sg_sem, out_sem, small_sem,
):
    rows, width = vp_s.shape
    steps = 8
    step = rows // steps
    parts = [pl.ds(i * step, step) for i in range(steps)]
    load_key = pltpu.make_async_copy(key_hbm, key_in, small_sem.at[0])
    load_texts = pltpu.make_async_copy(texts_hbm, texts_s, small_sem.at[1])
    load_tg = pltpu.make_async_copy(tg_hbm, tg_s, small_sem.at[2])
    load_key.start()
    load_vp, load_sg, outs = [], [], []
    for i, part in enumerate(parts):
        load_sg.append(pltpu.make_async_copy(sg_hbm.at[part], sg_s.at[part], sg_sem.at[i]))
        load_vp.append(pltpu.make_async_copy(vp_hbm.at[part], vp_s.at[part], vp_sem.at[i]))
        outs.append(pltpu.make_async_copy(vp_s.at[part], out_hbm.at[part], out_sem.at[i]))
        load_sg[i].start()
        load_vp[i].start()
        if i == 1:
            load_texts.start()
            load_tg.start()
    load_key.wait()
    repeat_heads(key_in, key_s)
    for i, part in enumerate(parts):
        load_sg[i].wait()
        load_vp[i].wait()
        for start in range(0, width, 256):
            cols = slice(start, min(start + 256, width))
            total = vp_s[part, cols].astype(F32) + nn(sg_s[part, :], key_s[:, cols])
            vp_s[part, cols] = total.astype(BF)
        outs[i].start()
        if i == 2:
            load_texts.wait()
            load_tg.wait()
            text_full = texts_s[...].astype(F32)
            text_norm = jnp.sqrt(jnp.sum(text_full * text_full, axis=1, keepdims=True) + EPSILON)
            text_unit = text_full / text_norm
            text_grad = tg_s[...]
            inner = jnp.sum(text_grad * text_unit, axis=1, keepdims=True)
            gt_s[...] = (text_grad - text_unit * inner) / text_norm
            gt_out = pltpu.make_async_copy(gt_s, gt_hbm, small_sem.at[3])
            gt_out.start()
    for copy in outs:
        copy.wait()
    gt_out.wait()


def local(frames, key_proj, value_weight, out_weight, texts, logit_scale, logit_bias):
    clips, frames_here, width = frames.shape
    heads = key_proj.shape[1]
    head = width // heads
    emb = out_weight.shape[1]
    all_clips = clips * lax.axis_size("clip")
    rows = clips * frames_here
    half = clips // 2
    frame_rows = frames.reshape(rows, width)
    key_t = key_proj.T
    V = pltpu.VMEM
    copies = 48
    scratch = [
        V((heads, width), BF),
        V((128, emb), BF),
        V((128, emb), F32),
        V((rows, width), BF),
        V((width, width), BF),
        V((width, emb), BF),
        V((heads * GROUP, width), BF),
        V((heads, clips, width), BF),
        V((rows, heads * GROUP), F32),
        V((2, clips // GROUP, heads * GROUP), F32),
        V((2, clips // GROUP, heads * GROUP), F32),
        V((clips // GROUP, heads * GROUP), F32),
        V((clips, width), F32),
        V((rows, heads * GROUP), BF),
        V((rows, heads * GROUP), BF),
        V((rows, heads * GROUP), F32),
        V((2, 4, 4, 128, emb), BF),
        V((2, 4, 4, 128, emb), BF),
        V((4, 4, 128, emb), BF),
        V((2, 2, 128, emb), BF),
        V((2, 4, 128, emb), BF),
        V((4, 128, emb), BF),
        V((2, 64, emb), BF),
        V((2, 128, emb), BF),
        V((2, 4, 2, 4 * half, 256), BF),
        V((2, half, emb), BF),
        V((2, half, emb), BF),
        V((half, emb), F32),
        V((half, 128), F32),
        V((4, half, emb), BF),
        V((4 * half, emb), F32),
        V((4, half, emb), BF),
        V((2, half // 2, emb), BF),
        V((2, half, emb), BF),
        V((half, emb), BF),
        V((2, half, emb), BF),
        V((clips, width), BF),
        V((clips // GROUP, heads * GROUP), F32),
        V((clips // GROUP, heads * GROUP), F32),
        pltpu.SemaphoreType.DMA((11,)),
        pltpu.SemaphoreType.DMA((clips // GROUP,)),
        pltpu.SemaphoreType.DMA((copies,)),
        pltpu.SemaphoreType.DMA((copies,)),
    ]
    anywhere = pl.BlockSpec(memory_space=pl.ANY)
    smem = pl.BlockSpec(memory_space=pltpu.SMEM)
    value_part, score_grad, text_grad = pl.pallas_call(
        functools.partial(main_kernel, (clips, width, head, emb, all_clips)),
        out_shape=(
            jax.ShapeDtypeStruct((rows, width), BF),
            jax.ShapeDtypeStruct((rows, heads * GROUP), BF),
            jax.ShapeDtypeStruct((128, emb), F32),
        ),
        in_specs=[anywhere] * 5 + [smem] * 2,
        out_specs=(anywhere, anywhere, anywhere),
        scratch_shapes=scratch,
        compiler_params=pltpu.CompilerParams(
            collective_id=0, has_side_effects=True, vmem_limit_bytes=60 * 1024 * 1024
        ),
        name="pool_pair_back",
    )(frame_rows, key_t, value_weight, out_weight, texts, logit_scale, logit_bias)
    steps = 8
    grad_frames, grad_texts = pl.pallas_call(
        final_kernel,
        in_specs=[anywhere] * 5,
        out_specs=(anywhere, anywhere),
        out_shape=(
            jax.ShapeDtypeStruct((rows, width), BF),
            jax.ShapeDtypeStruct((128, emb), F32),
        ),
        scratch_shapes=[
            V((rows, width), BF),
            V((rows, heads * GROUP), BF),
            V((heads, width), BF),
            V((heads * GROUP, width), BF),
            V((128, emb), BF),
            V((128, emb), F32),
            V((128, emb), F32),
            pltpu.SemaphoreType.DMA((steps,)),
            pltpu.SemaphoreType.DMA((steps,)),
            pltpu.SemaphoreType.DMA((steps,)),
            pltpu.SemaphoreType.DMA((4,)),
        ],
        compiler_params=pltpu.CompilerParams(vmem_limit_bytes=60 * 1024 * 1024),
        name="frame_grads",
    )(value_part, score_grad, key_t, texts, text_grad)
    return (grad_frames.reshape(clips, frames_here, width), grad_texts)


def solution(mesh):
    in_specs = (P("clip", "tm", None), P(), P(), P(), P(("tm", "clip"), None), P(), P())
    out_specs = (P("clip", "tm", None), P(("tm", "clip"), None))
    return jax.shard_map(local, mesh=mesh, in_specs=in_specs, out_specs=out_specs, check_vma=False)
```

```python
import functools
import math

import jax
import jax.numpy as jnp
from jax import lax
from jax.experimental import pallas as pl
from jax.experimental.pallas import tpu as pltpu
from jax.sharding import PartitionSpec as P

EPSILON = 1e-06
MESH = pl.DeviceIdType.MESH
BF = jnp.bfloat16
F32 = jnp.float32
NT = (((1,), (1,)), ((), ()))
TN = (((0,), (0,)), ((), ()))
HEADS = 16
GROUP = 16


def nt(a, b):
    return lax.dot_general(a, b, NT, preferred_element_type=F32)


def tn(a, b):
    return lax.dot_general(a, b, TN, preferred_element_type=F32)


def nn(a, b):
    return jnp.dot(a, b, preferred_element_type=F32)


def split_nn(a, b):
    high = a.astype(BF)
    low = (a - high.astype(F32)).astype(BF)
    return nn(high, b) + nn(low, b)


def own_clip_mask(rows_per_clip):
    shape = (GROUP * rows_per_clip, HEADS * GROUP)
    row = lax.broadcasted_iota(jnp.int32, shape, 0)
    lane = lax.broadcasted_iota(jnp.int32, shape, 1) & (GROUP - 1)
    start = lane * rows_per_clip
    return jnp.where((row >= start) & (row < start + rows_per_clip), 1.0, 0.0)


def repeat_heads(key_ref, out_ref):
    for h in range(HEADS):
        row = key_ref[h : h + 1, :].astype(F32)
        wide = jnp.broadcast_to(row, (GROUP, row.shape[1])).astype(BF)
        out_ref[h * GROUP : (h + 1) * GROUP, :] = wide


def main_kernel(
    dims,
    frames_hbm, key_hbm, value_hbm, out_hbm, texts_hbm, scale_ref, bias_ref,
    vp_hbm, sg_hbm, gt_hbm,
    key_ref, texts_ref, gt_ref,
    x_s, w_s, ow_s, key_s, pq_s, e_s, ms_send, ms_recv, alpha_s, acc_s, a_s, sg_s, t_s,
    tt_s, tg_s, rsib_s, r1_s, r2_s, tr_s, q1_s, q2_s, g_s,
    embp_s, embr_s, vu_s, vn_s, v_s, vg_s, vgb_s, g1_s, g2_s, eg_s, egr_s, pg_s, u_send, u_recv,
    load_sem, out_sem, send_sem, recv_sem,
):
    clips, width, head, emb, all_clips = dims
    frames_here = 8
    rows = clips * frames_here
    groups = clips // GROUP
    half_clips = clips // 2
    root = 1.0 / math.sqrt(width)

    tm = lax.axis_index("tm")
    ci = lax.axis_index("clip")
    core = lax.rem(ci, 2)
    y = lax.rem(ci // 2, 4)
    x = lax.rem(ci // 8, 4)
    z_lo = ci // 32
    z = tm * 2 + z_lo

    def at(xx, yy, zz, cc):
        return (zz // 2, ((lax.rem(zz, 2) * 4 + xx) * 4 + yy) * 2 + cc)

    def up(a, n):
        return lax.rem(a + n, 4)

    p1, p2 = y, x

    def plane(a1, a2):
        return at(a2, a1, z, core)

    n1p, n1m = plane(up(p1, 1), p2), plane(up(p1, 3), p2)
    n2p, n2m = plane(p1, up(p2, 1)), plane(p1, up(p2, 3))
    zp, zm = at(x, y, up(z, 1), core), at(x, y, up(z, 3), core)
    partner = (1 - tm, ci)
    sibling = at(x, y, z, 1 - core)

    counter = [0]

    def remote(src, dst, device):
        k = counter[0]
        counter[0] += 1
        return pltpu.make_async_remote_copy(
            src_ref=src, dst_ref=dst, send_sem=send_sem.at[k], recv_sem=recv_sem.at[k],
            device_id=device, device_id_type=MESH,
        )

    chunk = rows // 4
    loads = [
        pltpu.make_async_copy(
            frames_hbm.at[pl.ds(i * chunk, chunk)], x_s.at[pl.ds(i * chunk, chunk)], load_sem.at[i]
        )
        for i in range(4)
    ]
    load_w = pltpu.make_async_copy(value_hbm, w_s, load_sem.at[4])
    load_ow = pltpu.make_async_copy(out_hbm, ow_s, load_sem.at[5])
    load_key = pltpu.make_async_copy(key_hbm, key_ref, load_sem.at[6])
    load_texts = pltpu.make_async_copy(texts_hbm, texts_ref, load_sem.at[7])
    load_texts.start()
    load_key.start()
    for load in loads:
        load.start()
    load_w.start()
    load_ow.start()

    barrier = pltpu.get_barrier_semaphore()
    greet = (n1p, n1m, n2p, n2m, zp, zm, partner, sibling)
    for device in greet:
        pl.semaphore_signal(barrier, inc=1, device_id=device, device_id_type=MESH)

    load_texts.wait()
    text_full = texts_ref[...].astype(F32)
    text_norm = jnp.sqrt(jnp.sum(text_full * text_full, axis=1, keepdims=True) + EPSILON)
    tt_s[1, p2, p1] = (text_full / text_norm).astype(BF)
    load_key.wait()
    repeat_heads(key_ref, key_s)

    pl.semaphore_wait(barrier, len(greet))

    sent = []

    def go(*copies):
        for copy in copies:
            copy.start()
            sent.append(copy)

    own = tt_s.at[1]
    a0p = remote(own.at[p2, p1], own.at[p2, p1], n1p)
    a0m = remote(own.at[p2, p1], own.at[p2, p1], n1m)
    go(a0p, a0m)

    mask = own_clip_mask(frames_here)
    clip_mask = own_clip_mask(1)
    lanes = HEADS * GROUP

    def own_lane(per_clip):
        picked = per_clip.reshape(per_clip.shape[0] // GROUP, GROUP, lanes) * clip_mask[None]
        return jnp.sum(picked, axis=1)

    for i in range(4):
        loads[i].wait()
        part = pl.ds(i * chunk, chunk)
        s = nt(x_s[part, :], key_s[...]) * root
        s3 = s.reshape(chunk // frames_here, frames_here, lanes)
        top = jnp.max(s3, axis=1)
        e3 = jnp.exp(s3 - top[:, None, :])
        e_s[part, :] = e3.reshape(chunk, lanes)
        group_part = pl.ds(i * groups // 4, groups // 4)
        ms_send[0, group_part, :] = own_lane(top)
        ms_send[1, group_part, :] = own_lane(jnp.sum(e3, axis=1))
    ms = remote(ms_send, ms_recv, partner)
    go(ms)

    def a1():
        a0p.wait_recv()
        a0m.wait_recv()
        low, high = pl.ds(0, 64), pl.ds(64, 64)
        b1, b3 = up(p1, 3), up(p1, 1)
        cp = remote(own.at[p2, b1, low], own.at[p2, b1, low], n1p)
        cm = remote(own.at[p2, b3, high], own.at[p2, b3, high], n1m)
        go(cp, cm)
        return cp, cm

    def sib_row(row):
        copy = remote(own.at[row], tt_s.at[0, row], sibling)
        go(copy)
        return copy

    fwd1 = a1()

    columns = [slice(at, min(at + 256, width)) for at in range(0, width, 256)]

    def pool_group(g, carry):
        frame_part = pl.ds(pl.multiple_of(g * 128, 128), 128)
        clip_part = pl.ds(pl.multiple_of(g * GROUP, GROUP), GROUP)
        weight = jnp.transpose(e_s[frame_part, :] * mask).astype(BF)
        for cols in columns:
            pooled = nn(weight, x_s[frame_part, cols]).astype(BF)
            pq_s[:, clip_part, cols] = pooled.reshape(HEADS, GROUP, pooled.shape[1])
        return carry

    lax.fori_loop(0, groups // 2, pool_group, 0, unroll=4)

    for copy in fwd1:
        copy.wait_recv()
    row_p = remote(own.at[p2], own.at[p2], n2p)
    row_m = remote(own.at[p2], own.at[p2], n2m)
    go(row_p, row_m)
    sib0 = sib_row(p2)

    lax.fori_loop(groups // 2, groups, pool_group, 0, unroll=4)

    load_w.wait()
    load_ow.wait()
    acc_s[...] = jnp.zeros_like(acc_s)

    pairs = []
    for h in range(0, HEADS, 2):
        first = min(h * head // 128, width // 128 - 2) * 128
        wide = 256 if (h + 2) * head <= first + 256 else 384
        pairs.append((h, first, wide))

    def window_mask(h, first, wide):
        lane = lax.broadcasted_iota(jnp.int32, (1, wide), 1)
        offset = h * head - first
        return (lane >= offset) & (lane < offset + head)

    for h, first, wide in pairs:
        cols = slice(first, first + wide)
        part = nn(pq_s[h : h + 2].reshape(2 * clips, width), w_s[:, cols])
        acc_s[:, cols] += jnp.where(window_mask(h, first, wide), part[:clips], 0.0) + jnp.where(
            window_mask(h + 1, first, wide), part[clips:], 0.0
        )

    ms.wait_recv()
    mine, theirs = ms_send[0], ms_recv[0]
    top = jnp.maximum(mine, theirs)
    mine_f, theirs_f = jnp.exp(mine - top), jnp.exp(theirs - top)
    alpha = mine_f / (ms_send[1] * mine_f + ms_recv[1] * theirs_f)
    alpha_s[...] = alpha
    spread = (alpha[:, None, :] * clip_mask[None]).reshape(clips, lanes)
    head_start = (lax.broadcasted_iota(jnp.int32, (lanes, width), 0) // GROUP) * head
    head_lane = lax.broadcasted_iota(jnp.int32, (lanes, width), 1)
    in_head = (head_lane >= head_start) & (head_lane < head_start + head)
    pooled = (acc_s[...] * split_nn(spread, jnp.where(in_head, 1.0, 0.0).astype(BF))).astype(BF)
    embp_s[...] = nn(pooled, ow_s[...]).astype(BF).reshape(2, half_clips, emb)
    er_p = remote(embp_s.at[up(z, 1) // 2], embr_s.at[0], zp)
    er_m = remote(embp_s.at[up(z, 3) // 2], embr_s.at[1], zm)
    go(er_p, er_m)

    row_p.wait_recv()
    row_m.wait_recv()
    r1, r3 = up(p2, 3), up(p2, 1)
    low, high = pl.ds(0, 2), pl.ds(2, 2)
    fwd_p = remote(own.at[r1, low], own.at[r1, low], n2p)
    fwd_m = remote(own.at[r3, high], own.at[r3, high], n2m)
    go(fwd_p, fwd_m)
    sib1 = sib_row(r3)
    sib2 = sib_row(r1)

    def weights(g, carry):
        frame_part = pl.ds(pl.multiple_of(g * 128, 128), 128)
        wide = e_s[frame_part, :] * mask * alpha_s[pl.ds(g, 1), :]
        e_s[frame_part, :] = wide
        a_s[frame_part, :] = wide.astype(BF)
        return carry

    lax.fori_loop(0, groups // 2, weights, 0, unroll=4)

    er_p.wait_recv()
    er_m.wait_recv()
    embedding = embr_s[0].astype(F32) + embr_s[1].astype(F32)
    vis_norm = jnp.sqrt(jnp.sum(embedding * embedding, axis=1, keepdims=True) + EPSILON)
    vis_unit = embedding / vis_norm
    vu_s[...] = vis_unit
    vn_s[...] = jnp.broadcast_to(vis_norm, vn_s.shape)
    v_s[z] = vis_unit.astype(BF)
    hlow, hhigh = pl.ds(0, half_clips // 2), pl.ds(half_clips // 2, half_clips // 2)

    def send_vis(at_z, half, device):
        copy = remote(v_s.at[at_z, half], v_s.at[at_z, half], device)
        go(copy)
        return copy

    v_first = send_vis(z, hlow, zp), send_vis(z, hhigh, zm)
    v_second = send_vis(z, hhigh, zp), send_vis(z, hlow, zm)
    lax.fori_loop(groups // 2, groups, weights, 0, unroll=4)
    z1, z2, z3 = up(z, 1), up(z, 2), up(z, 3)
    for copy in v_first:
        copy.wait_recv()
    v_far = send_vis(z3, hlow, zp), send_vis(z1, hhigh, zm)

    fwd_p.wait_recv()
    fwd_m.wait_recv()
    sib3 = sib_row(up(p2, 2))
    for copy in v_second + v_far:
        copy.wait_recv()

    vg_s[...] = jnp.zeros_like(vg_s)
    slope = 0.5 * scale_ref[0]
    shift = 0.5 * bias_ref[0]
    diff = lax.broadcasted_iota(jnp.int32, (128, 128), 0) - lax.broadcasted_iota(
        jnp.int32, (128, 128), 1
    )
    vis_base = [
        (((1 - zz % 2) * 4 + x) * 4 + y) * 2 * clips + core * clips + (zz // 2) * half_clips
        for zz in range(4)
    ]

    def text_base(whose, a2, a1):
        c = core * whose + (1 - core) * (1 - whose)
        return (tm * 64 + ((z_lo * 4 + a2) * 4 + a1) * 2 + c) * 128

    def pair_row(whose, row):
        vis = v_s[...].reshape(4 * half_clips, emb)
        total = None
        for hh in range(2):
            texts = tt_s[whose, row, pl.ds(2 * hh, 2)].reshape(256, emb)
            curve = jnp.tanh(nt(vis, texts) * slope + shift) * 0.5
            tall = []
            for zz in range(4):
                wide = []
                for b in range(2):
                    gap = text_base(whose, row, 2 * hh + b) - vis_base[zz]
                    block = curve[zz * 128 : (zz + 1) * 128, b * 128 : (b + 1) * 128]
                    wide.append(block + jnp.where(diff == gap, -0.5, 0.5))
                tall.append(jnp.concatenate(wide, axis=1))
            grad = jnp.concatenate(tall, axis=0).astype(BF)
            g_s[whose, row, hh] = grad
            part = nn(grad, texts)
            total = part if total is None else total + part
        vg_s[...] += total

    def pair_rows(whose):
        def body(row, carry):
            pair_row(whose, row)
            return carry

        lax.fori_loop(0, 4, body, 0)

    pair_rows(1)
    for copy in (sib0, sib1, sib2, sib3):
        copy.wait_recv()
    pair_rows(0)

    vgb_s[...] = vg_s[...].astype(BF).reshape(4, half_clips, emb)
    g1p = remote(vgb_s.at[z2, hlow], g1_s.at[0], zp)
    g1m = remote(vgb_s.at[z2, hhigh], g1_s.at[1], zm)
    g2p = remote(vgb_s.at[z1, hhigh], g2_s.at[0, hhigh], zp)
    g2m = remote(vgb_s.at[z3, hlow], g2_s.at[1, hlow], zm)
    go(g1p, g1m, g2p, g2m)

    sib_base = counter[0]
    counter[0] += 4

    def sib_copy(rr, row):
        return pltpu.make_async_remote_copy(
            src_ref=tg_s.at[0, row], dst_ref=rsib_s.at[row],
            send_sem=send_sem.at[sib_base + rr], recv_sem=recv_sem.at[sib_base + rr],
            device_id=sibling, device_id_type=MESH,
        )

    def ordered(p, rr):
        return lax.rem(p + 2 + 3 * rr + 3 * (rr // 2) + 2 * (rr // 3), 4)

    def text_terms(whose, row):
        vis = v_s[...].reshape(4 * half_clips, emb)
        grad = jnp.concatenate([g_s[whose, row, 0], g_s[whose, row, 1]], axis=1)
        return tn(grad, vis).reshape(4, 128, emb)

    def sib_rows(rr, carry):
        row = ordered(p2, rr)
        tg_s[0, row] = text_terms(0, row).astype(BF)
        sib_copy(rr, row).start()
        return carry

    lax.fori_loop(0, 4, sib_rows, 0)

    g1p.wait_recv()
    g1m.wait_recv()
    vgb_s[z1, hlow] = (vgb_s[z1, hlow].astype(F32) + g1_s[0].astype(F32)).astype(BF)
    g3p = remote(vgb_s.at[z1, hlow], g2_s.at[0, hlow], zp)
    vgb_s[z3, hhigh] = (vgb_s[z3, hhigh].astype(F32) + g1_s[1].astype(F32)).astype(BF)
    g3m = remote(vgb_s.at[z3, hhigh], g2_s.at[1, hhigh], zm)
    go(g3p, g3m)

    def own_rows(rr, carry):
        row = ordered(p2, rr)
        sib_copy(rr, row).wait_recv()
        tg_s[1, row] = (text_terms(1, row) + rsib_s[row].astype(F32)).astype(BF)
        return carry

    tg = tg_s.at[1]
    lax.fori_loop(0, 1, own_rows, 0)
    s1p = remote(tg.at[up(p2, 2), low], r1_s.at[0], n2p)
    s1m = remote(tg.at[up(p2, 2), high], r1_s.at[1], n2m)
    go(s1p, s1m)
    lax.fori_loop(1, 2, own_rows, 0)
    s2p = remote(tg.at[r3, high], r2_s.at[0, high], n2p)
    go(s2p)
    lax.fori_loop(2, 3, own_rows, 0)
    s2m = remote(tg.at[r1, low], r2_s.at[1, low], n2m)
    go(s2m)

    for copy in (g2p, g2m, g3p, g3m):
        copy.wait_recv()
    out_scale = scale_ref[0] * (1.0 / all_clips)
    vis_grad = (
        vg_s[pl.ds(pl.multiple_of(z * half_clips, 128), half_clips), :]
        + g2_s[0].astype(F32)
        + g2_s[1].astype(F32)
    ) * out_scale
    unit = vu_s[...]
    inner = jnp.sum(vis_grad * unit, axis=1, keepdims=True)
    eg_s[...] = ((vis_grad - unit * inner) / vn_s[:, :1]).astype(BF)
    eg_p = remote(eg_s, egr_s.at[tm], zp)
    eg_m = remote(eg_s, egr_s.at[tm], zm)
    go(eg_p, eg_m)

    lax.fori_loop(3, 4, own_rows, 0)
    s1p.wait_recv()
    s1m.wait_recv()
    tg_s[1, r3, low] = (tg_s[1, r3, low].astype(F32) + r1_s[0].astype(F32)).astype(BF)
    s3p = remote(tg.at[r3, low], r2_s.at[0, low], n2p)
    go(s3p)
    tg_s[1, r1, high] = (tg_s[1, r1, high].astype(F32) + r1_s[1].astype(F32)).astype(BF)
    s3m = remote(tg.at[r1, high], r2_s.at[1, high], n2m)
    go(s3m)

    eg_p.wait_recv()
    eg_m.wait_recv()
    pg_s[...] = nt(egr_s[...].reshape(clips, emb), ow_s[...]).astype(BF)

    for h, first, wide in pairs:
        grads = pg_s[:, first : first + wide].astype(F32)
        part = jnp.concatenate(
            [jnp.where(window_mask(h + i, first, wide), grads, 0.0).astype(BF) for i in range(2)],
            axis=0,
        )
        for cols in columns:
            q = nt(part, w_s[cols, first : first + wide]).astype(BF)
            pq_s[h : h + 2, :, cols] = q.reshape(2, clips, q.shape[1])

    def score_terms(g, carry):
        frame_part = pl.ds(pl.multiple_of(g * 128, 128), 128)
        clip_part = pl.ds(pl.multiple_of(g * GROUP, GROUP), GROUP)
        q = pq_s[:, clip_part, :].reshape(lanes, width)
        prod = jnp.transpose(nt(q, x_s[frame_part, :]))
        t_s[frame_part, :] = prod
        u_send[pl.ds(g, 1), :] = jnp.sum(prod * e_s[frame_part, :], axis=0, keepdims=True)
        return carry

    lax.fori_loop(0, groups, score_terms, 0, unroll=4)
    uc = remote(u_send, u_recv, partner)
    uc.start()

    for copy in (s2p, s2m, s3p, s3m):
        copy.wait_recv()
    for b in range(4):
        total = tg_s[1, p2, b].astype(F32) + r2_s[0, b].astype(F32) + r2_s[1, b].astype(F32)
        tr_s[b] = total.astype(BF)
    b1, b2, b3 = up(p1, 1), up(p1, 2), up(p1, 3)
    tlow, thigh = pl.ds(0, 64), pl.ds(64, 64)
    u1p = remote(tr_s.at[b2, tlow], q1_s.at[0], n1p)
    u1m = remote(tr_s.at[b2, thigh], q1_s.at[1], n1m)
    u2p = remote(tr_s.at[b1, thigh], q2_s.at[0, thigh], n1p)
    u2m = remote(tr_s.at[b3, tlow], q2_s.at[1, tlow], n1m)
    go(u1p, u1m, u2p, u2m)

    def vp_copy(g):
        frame_part = pl.ds(pl.multiple_of(g * 128, 128), 128)
        return pltpu.make_async_copy(
            x_s.at[frame_part], vp_hbm.at[frame_part], out_sem.at[g]
        )

    def value_part(g, carry):
        frame_part = pl.ds(pl.multiple_of(g * 128, 128), 128)
        clip_part = pl.ds(pl.multiple_of(g * GROUP, GROUP), GROUP)
        for cols in columns:
            q = pq_s[:, clip_part, cols]
            q = q.reshape(lanes, q.shape[2])
            x_s[frame_part, cols] = nn(a_s[frame_part, :], q).astype(BF)
        vp_copy(g).start()
        return carry

    lax.fori_loop(0, groups // 2, value_part, 0, unroll=4)
    u1p.wait_recv()
    u1m.wait_recv()
    tr_s[b1, tlow] = (tr_s[b1, tlow].astype(F32) + q1_s[0].astype(F32)).astype(BF)
    u3p = remote(tr_s.at[b1, tlow], q2_s.at[0, tlow], n1p)
    tr_s[b3, thigh] = (tr_s[b3, thigh].astype(F32) + q1_s[1].astype(F32)).astype(BF)
    u3m = remote(tr_s.at[b3, thigh], q2_s.at[1, thigh], n1m)
    go(u3p, u3m)

    lax.fori_loop(groups // 2, groups, value_part, 0, unroll=4)

    for copy in (u2p, u2m, u3p, u3m):
        copy.wait_recv()
    gt_ref[...] = (
        tr_s[p1].astype(F32) + q2_s[0].astype(F32) + q2_s[1].astype(F32)
    ) * out_scale
    gt_out = pltpu.make_async_copy(gt_ref, gt_hbm, load_sem.at[8])
    gt_out.start()

    uc.wait()
    u_send[...] = u_send[...] + u_recv[...]

    def score_grads(g, carry):
        frame_part = pl.ds(pl.multiple_of(g * 128, 128), 128)
        centred = t_s[frame_part, :] - u_send[pl.ds(g, 1), :]
        sg_s[frame_part, :] = (e_s[frame_part, :] * centred * root).astype(BF)
        return carry

    sg_out = []
    for i in range(2):
        lax.fori_loop(i * groups // 2, (i + 1) * groups // 2, score_grads, 0, unroll=4)
        part = pl.ds(i * rows // 2, rows // 2)
        sg_out.append(pltpu.make_async_copy(sg_s.at[part], sg_hbm.at[part], load_sem.at[9 + i]))
        sg_out[i].start()

    for copy in sent:
        copy.wait_send()

    def drain(rr, carry):
        sib_copy(rr, ordered(p2, rr)).wait_send()
        return carry

    lax.fori_loop(0, 4, drain, 0)

    def drain_vp(g, carry):
        vp_copy(g).wait()
        return carry

    lax.fori_loop(0, groups, drain_vp, 0)
    for copy in sg_out:
        copy.wait()
    gt_out.wait()


def final_kernel(
    vp_hbm, sg_hbm, key_hbm, texts_hbm, tg_hbm, out_hbm, gt_hbm,
    vp_s, sg_s, key_in, key_s, texts_s, tg_s, gt_s, vp_sem, sg_sem, out_sem, small_sem,
):
    rows, width = vp_s.shape
    steps = 8
    step = rows // steps
    parts = [pl.ds(i * step, step) for i in range(steps)]
    load_key = pltpu.make_async_copy(key_hbm, key_in, small_sem.at[0])
    load_texts = pltpu.make_async_copy(texts_hbm, texts_s, small_sem.at[1])
    load_tg = pltpu.make_async_copy(tg_hbm, tg_s, small_sem.at[2])
    load_key.start()
    load_vp, load_sg, outs = [], [], []
    for i, part in enumerate(parts):
        load_sg.append(pltpu.make_async_copy(sg_hbm.at[part], sg_s.at[part], sg_sem.at[i]))
        load_vp.append(pltpu.make_async_copy(vp_hbm.at[part], vp_s.at[part], vp_sem.at[i]))
        outs.append(pltpu.make_async_copy(vp_s.at[part], out_hbm.at[part], out_sem.at[i]))
        load_sg[i].start()
        load_vp[i].start()
        if i == 1:
            load_texts.start()
            load_tg.start()
    load_key.wait()
    repeat_heads(key_in, key_s)
    for i, part in enumerate(parts):
        load_sg[i].wait()
        load_vp[i].wait()
        for start in range(0, width, 256):
            cols = slice(start, min(start + 256, width))
            total = vp_s[part, cols].astype(F32) + nn(sg_s[part, :], key_s[:, cols])
            vp_s[part, cols] = total.astype(BF)
        outs[i].start()
        if i == 2:
            load_texts.wait()
            load_tg.wait()
            text_full = texts_s[...].astype(F32)
            text_norm = jnp.sqrt(jnp.sum(text_full * text_full, axis=1, keepdims=True) + EPSILON)
            text_unit = text_full / text_norm
            text_grad = tg_s[...]
            inner = jnp.sum(text_grad * text_unit, axis=1, keepdims=True)
            gt_s[...] = (text_grad - text_unit * inner) / text_norm
            gt_out = pltpu.make_async_copy(gt_s, gt_hbm, small_sem.at[3])
            gt_out.start()
    for copy in outs:
        copy.wait()
    gt_out.wait()


def local(frames, key_proj, value_weight, out_weight, texts, logit_scale, logit_bias):
    clips, frames_here, width = frames.shape
    heads = key_proj.shape[1]
    head = width // heads
    emb = out_weight.shape[1]
    all_clips = clips * lax.axis_size("clip")
    rows = clips * frames_here
    half = clips // 2
    frame_rows = frames.reshape(rows, width)
    key_t = key_proj.T
    V = pltpu.VMEM
    copies = 48
    scratch = [
        V((heads, width), BF),
        V((128, emb), BF),
        V((128, emb), F32),
        V((rows, width), BF),
        V((width, width), BF),
        V((width, emb), BF),
        V((heads * GROUP, width), BF),
        V((heads, clips, width), BF),
        V((rows, heads * GROUP), F32),
        V((2, clips // GROUP, heads * GROUP), F32),
        V((2, clips // GROUP, heads * GROUP), F32),
        V((clips // GROUP, heads * GROUP), F32),
        V((clips, width), F32),
        V((rows, heads * GROUP), BF),
        V((rows, heads * GROUP), BF),
        V((rows, heads * GROUP), F32),
        V((2, 4, 4, 128, emb), BF),
        V((2, 4, 4, 128, emb), BF),
        V((4, 4, 128, emb), BF),
        V((2, 2, 128, emb), BF),
        V((2, 4, 128, emb), BF),
        V((4, 128, emb), BF),
        V((2, 64, emb), BF),
        V((2, 128, emb), BF),
        V((2, 4, 2, 4 * half, 256), BF),
        V((2, half, emb), BF),
        V((2, half, emb), BF),
        V((half, emb), F32),
        V((half, 128), F32),
        V((4, half, emb), BF),
        V((4 * half, emb), F32),
        V((4, half, emb), BF),
        V((2, half // 2, emb), BF),
        V((2, half, emb), BF),
        V((half, emb), BF),
        V((2, half, emb), BF),
        V((clips, width), BF),
        V((clips // GROUP, heads * GROUP), F32),
        V((clips // GROUP, heads * GROUP), F32),
        pltpu.SemaphoreType.DMA((11,)),
        pltpu.SemaphoreType.DMA((clips // GROUP,)),
        pltpu.SemaphoreType.DMA((copies,)),
        pltpu.SemaphoreType.DMA((copies,)),
    ]
    anywhere = pl.BlockSpec(memory_space=pl.ANY)
    smem = pl.BlockSpec(memory_space=pltpu.SMEM)
    value_part, score_grad, text_grad = pl.pallas_call(
        functools.partial(main_kernel, (clips, width, head, emb, all_clips)),
        out_shape=(
            jax.ShapeDtypeStruct((rows, width), BF),
            jax.ShapeDtypeStruct((rows, heads * GROUP), BF),
            jax.ShapeDtypeStruct((128, emb), F32),
        ),
        in_specs=[anywhere] * 5 + [smem] * 2,
        out_specs=(anywhere, anywhere, anywhere),
        scratch_shapes=scratch,
        compiler_params=pltpu.CompilerParams(
            collective_id=0, has_side_effects=True, vmem_limit_bytes=60 * 1024 * 1024
        ),
        name="pool_pair_back",
    )(frame_rows, key_t, value_weight, out_weight, texts, logit_scale, logit_bias)
    steps = 8
    grad_frames, grad_texts = pl.pallas_call(
        final_kernel,
        in_specs=[anywhere] * 5,
        out_specs=(anywhere, anywhere),
        out_shape=(
            jax.ShapeDtypeStruct((rows, width), BF),
            jax.ShapeDtypeStruct((128, emb), F32),
        ),
        scratch_shapes=[
            V((rows, width), BF),
            V((rows, heads * GROUP), BF),
            V((heads, width), BF),
            V((heads * GROUP, width), BF),
            V((128, emb), BF),
            V((128, emb), F32),
            V((128, emb), F32),
            pltpu.SemaphoreType.DMA((steps,)),
            pltpu.SemaphoreType.DMA((steps,)),
            pltpu.SemaphoreType.DMA((steps,)),
            pltpu.SemaphoreType.DMA((4,)),
        ],
        compiler_params=pltpu.CompilerParams(vmem_limit_bytes=60 * 1024 * 1024),
        name="frame_grads",
    )(value_part, score_grad, key_t, texts, text_grad)
    return (grad_frames.reshape(clips, frames_here, width), grad_texts)


def solution(mesh):
    in_specs = (P("clip", "tm", None), P(), P(), P(), P(("tm", "clip"), None), P(), P())
    out_specs = (P("clip", "tm", None), P(("tm", "clip"), None))
    return jax.shard_map(local, mesh=mesh, in_specs=in_specs, out_specs=out_specs, check_vma=False)
```

```python
import functools
import math

import jax
import jax.numpy as jnp
from jax import lax
from jax.experimental import pallas as pl
from jax.experimental.pallas import tpu as pltpu
from jax.sharding import PartitionSpec as P

EPSILON = 1e-06
MESH = pl.DeviceIdType.MESH
BF = jnp.bfloat16
F32 = jnp.float32
NT = (((1,), (1,)), ((), ()))
TN = (((0,), (0,)), ((), ()))
HEADS = 16
GROUP = 16


def nt(a, b):
    return lax.dot_general(a, b, NT, preferred_element_type=F32)


def tn(a, b):
    return lax.dot_general(a, b, TN, preferred_element_type=F32)


def nn(a, b):
    return jnp.dot(a, b, preferred_element_type=F32)


def own_clip_mask(rows_per_clip):
    shape = (GROUP * rows_per_clip, HEADS * GROUP)
    row = lax.broadcasted_iota(jnp.int32, shape, 0)
    lane = lax.broadcasted_iota(jnp.int32, shape, 1) & (GROUP - 1)
    start = lane * rows_per_clip
    return jnp.where((row >= start) & (row < start + rows_per_clip), 1.0, 0.0)


def repeat_heads(key_ref, out_ref):
    for h in range(HEADS):
        row = key_ref[h : h + 1, :].astype(F32)
        wide = jnp.broadcast_to(row, (GROUP, row.shape[1])).astype(BF)
        out_ref[h * GROUP : (h + 1) * GROUP, :] = wide


def main_kernel(
    dims,
    frames_hbm, key_hbm, value_hbm, out_hbm, texts_hbm, scale_ref, bias_ref,
    vp_hbm, sg_hbm, gt_hbm,
    key_ref, texts_ref, gt_ref,
    x_s, w_s, ow_s, key_s, pq_s, e_s, ms_send, ms_recv, alpha_s, acc_s, a_s, sg_s, t_s,
    tt_s, tg_s, rsib_s, r1_s, r2_s, tr_s, q1_s, q2_s, g_s,
    embp_s, embr_s, vu_s, vn_s, v_s, vg_s, vgb_s, g1_s, g2_s, eg_s, egr_s, pg_s, u_send, u_recv,
    load_sem, out_sem, send_sem, recv_sem,
):
    clips, width, head, emb, all_clips = dims
    frames_here = 8
    rows = clips * frames_here
    groups = clips // GROUP
    half_clips = clips // 2
    root = 1.0 / math.sqrt(width)

    tm = lax.axis_index("tm")
    ci = lax.axis_index("clip")
    core = lax.rem(ci, 2)
    y = lax.rem(ci // 2, 4)
    x = lax.rem(ci // 8, 4)
    z_lo = ci // 32
    z = tm * 2 + z_lo

    def at(xx, yy, zz, cc):
        return (zz // 2, ((lax.rem(zz, 2) * 4 + xx) * 4 + yy) * 2 + cc)

    def up(a, n):
        return lax.rem(a + n, 4)

    p1 = x * (1 - core) + y * core
    p2 = y * (1 - core) + x * core

    def plane(a1, a2):
        return at(a1 * (1 - core) + a2 * core, a2 * (1 - core) + a1 * core, z, core)

    n1p, n1m = plane(up(p1, 1), p2), plane(up(p1, 3), p2)
    n2p, n2m = plane(p1, up(p2, 1)), plane(p1, up(p2, 3))
    zp, zm = at(x, y, up(z, 1), core), at(x, y, up(z, 3), core)
    partner = (1 - tm, ci)
    sibling = at(x, y, z, 1 - core)

    counter = [0]

    def remote(src, dst, device):
        k = counter[0]
        counter[0] += 1
        return pltpu.make_async_remote_copy(
            src_ref=src, dst_ref=dst, send_sem=send_sem.at[k], recv_sem=recv_sem.at[k],
            device_id=device, device_id_type=MESH,
        )

    chunk = rows // 4
    loads = [
        pltpu.make_async_copy(
            frames_hbm.at[pl.ds(i * chunk, chunk)], x_s.at[pl.ds(i * chunk, chunk)], load_sem.at[i]
        )
        for i in range(4)
    ]
    load_w = pltpu.make_async_copy(value_hbm, w_s, load_sem.at[4])
    load_ow = pltpu.make_async_copy(out_hbm, ow_s, load_sem.at[5])
    load_key = pltpu.make_async_copy(key_hbm, key_ref, load_sem.at[6])
    load_texts = pltpu.make_async_copy(texts_hbm, texts_ref, load_sem.at[7])
    load_texts.start()
    load_key.start()
    for load in loads:
        load.start()
    load_w.start()
    load_ow.start()

    barrier = pltpu.get_barrier_semaphore()
    greet = (n1p, n1m, n2p, n2m, zp, zm, partner, sibling)
    for device in greet:
        pl.semaphore_signal(barrier, inc=1, device_id=device, device_id_type=MESH)

    load_texts.wait()
    text_full = texts_ref[...].astype(F32)
    text_norm = jnp.sqrt(jnp.sum(text_full * text_full, axis=1, keepdims=True) + EPSILON)
    tt_s[1, p2, p1] = (text_full / text_norm).astype(BF)
    load_key.wait()
    repeat_heads(key_ref, key_s)

    pl.semaphore_wait(barrier, len(greet))

    sent = []

    def go(*copies):
        for copy in copies:
            copy.start()
            sent.append(copy)

    own = tt_s.at[1]
    a0p = remote(own.at[p2, p1], own.at[p2, p1], n1p)
    a0m = remote(own.at[p2, p1], own.at[p2, p1], n1m)
    go(a0p, a0m)

    mask = own_clip_mask(frames_here)
    clip_mask = own_clip_mask(1)
    lanes = HEADS * GROUP

    def own_lane(per_clip):
        picked = per_clip.reshape(per_clip.shape[0] // GROUP, GROUP, lanes) * clip_mask[None]
        return jnp.sum(picked, axis=1)

    for i in range(4):
        loads[i].wait()
        part = pl.ds(i * chunk, chunk)
        s = nt(x_s[part, :], key_s[...]) * root
        s3 = s.reshape(chunk // frames_here, frames_here, lanes)
        top = jnp.max(s3, axis=1)
        e3 = jnp.exp(s3 - top[:, None, :])
        e_s[part, :] = e3.reshape(chunk, lanes)
        group_part = pl.ds(i * groups // 4, groups // 4)
        ms_send[0, group_part, :] = own_lane(top)
        ms_send[1, group_part, :] = own_lane(jnp.sum(e3, axis=1))
    ms = remote(ms_send, ms_recv, partner)
    go(ms)

    def a1():
        a0p.wait_recv()
        a0m.wait_recv()
        low, high = pl.ds(0, 64), pl.ds(64, 64)
        b1, b3 = up(p1, 3), up(p1, 1)
        cp = remote(own.at[p2, b1, low], own.at[p2, b1, low], n1p)
        cm = remote(own.at[p2, b3, high], own.at[p2, b3, high], n1m)
        go(cp, cm)
        return cp, cm

    def sib_row(row):
        copy = remote(own.at[row], tt_s.at[0, row], sibling)
        go(copy)
        return copy

    fwd1 = a1()

    columns = [slice(at, min(at + 256, width)) for at in range(0, width, 256)]

    def pool_group(g, carry):
        frame_part = pl.ds(pl.multiple_of(g * 128, 128), 128)
        clip_part = pl.ds(pl.multiple_of(g * GROUP, GROUP), GROUP)
        weight = jnp.transpose(e_s[frame_part, :] * mask).astype(BF)
        for cols in columns:
            pooled = nn(weight, x_s[frame_part, cols]).astype(BF)
            pq_s[:, clip_part, cols] = pooled.reshape(HEADS, GROUP, pooled.shape[1])
        return carry

    lax.fori_loop(0, groups // 2, pool_group, 0, unroll=4)

    for copy in fwd1:
        copy.wait_recv()
    row_p = remote(own.at[p2], own.at[p2], n2p)
    row_m = remote(own.at[p2], own.at[p2], n2m)
    go(row_p, row_m)
    sib0 = sib_row(p2)

    lax.fori_loop(groups // 2, groups, pool_group, 0, unroll=4)

    load_w.wait()
    load_ow.wait()
    acc_s[...] = jnp.zeros_like(acc_s)

    pairs = []
    for h in range(0, HEADS, 2):
        first = min(h * head // 128, width // 128 - 2) * 128
        wide = 256 if (h + 2) * head <= first + 256 else 384
        pairs.append((h, first, wide))

    def window_mask(h, first, wide):
        lane = lax.broadcasted_iota(jnp.int32, (1, wide), 1)
        offset = h * head - first
        return (lane >= offset) & (lane < offset + head)

    for h, first, wide in pairs:
        cols = slice(first, first + wide)
        part = nn(pq_s[h : h + 2].reshape(2 * clips, width), w_s[:, cols])
        acc_s[:, cols] += jnp.where(window_mask(h, first, wide), part[:clips], 0.0) + jnp.where(
            window_mask(h + 1, first, wide), part[clips:], 0.0
        )

    ms.wait_recv()
    mine, theirs = ms_send[0], ms_recv[0]
    top = jnp.maximum(mine, theirs)
    mine_f, theirs_f = jnp.exp(mine - top), jnp.exp(theirs - top)
    alpha = mine_f / (ms_send[1] * mine_f + ms_recv[1] * theirs_f)
    alpha_s[...] = alpha
    spread = (alpha[:, None, :] * clip_mask[None]).reshape(clips, lanes)
    head_start = (lax.broadcasted_iota(jnp.int32, (lanes, width), 0) // GROUP) * head
    head_lane = lax.broadcasted_iota(jnp.int32, (lanes, width), 1)
    in_head = (head_lane >= head_start) & (head_lane < head_start + head)
    pooled = (acc_s[...] * nn(spread.astype(BF), jnp.where(in_head, 1.0, 0.0).astype(BF))).astype(BF)
    embp_s[...] = nn(pooled, ow_s[...]).astype(BF).reshape(2, half_clips, emb)
    er_p = remote(embp_s.at[up(z, 1) // 2], embr_s.at[0], zp)
    er_m = remote(embp_s.at[up(z, 3) // 2], embr_s.at[1], zm)
    go(er_p, er_m)

    row_p.wait_recv()
    row_m.wait_recv()
    r1, r3 = up(p2, 3), up(p2, 1)
    low, high = pl.ds(0, 2), pl.ds(2, 2)
    fwd_p = remote(own.at[r1, low], own.at[r1, low], n2p)
    fwd_m = remote(own.at[r3, high], own.at[r3, high], n2m)
    go(fwd_p, fwd_m)
    sib1 = sib_row(r3)
    sib2 = sib_row(r1)

    def weights(g, carry):
        frame_part = pl.ds(pl.multiple_of(g * 128, 128), 128)
        wide = e_s[frame_part, :] * mask * alpha_s[pl.ds(g, 1), :]
        e_s[frame_part, :] = wide
        a_s[frame_part, :] = wide.astype(BF)
        return carry

    lax.fori_loop(0, groups // 2, weights, 0, unroll=4)

    er_p.wait_recv()
    er_m.wait_recv()
    embedding = embr_s[0].astype(F32) + embr_s[1].astype(F32)
    vis_norm = jnp.sqrt(jnp.sum(embedding * embedding, axis=1, keepdims=True) + EPSILON)
    vis_unit = embedding / vis_norm
    vu_s[...] = vis_unit
    vn_s[...] = jnp.broadcast_to(vis_norm, vn_s.shape)
    v_s[z] = vis_unit.astype(BF)
    hlow, hhigh = pl.ds(0, half_clips // 2), pl.ds(half_clips // 2, half_clips // 2)

    def send_vis(at_z, half, device):
        copy = remote(v_s.at[at_z, half], v_s.at[at_z, half], device)
        go(copy)
        return copy

    v_first = send_vis(z, hlow, zp), send_vis(z, hhigh, zm)
    v_second = send_vis(z, hhigh, zp), send_vis(z, hlow, zm)
    lax.fori_loop(groups // 2, groups, weights, 0, unroll=4)
    z1, z2, z3 = up(z, 1), up(z, 2), up(z, 3)
    for copy in v_first:
        copy.wait_recv()
    v_far = send_vis(z3, hlow, zp), send_vis(z1, hhigh, zm)

    fwd_p.wait_recv()
    fwd_m.wait_recv()
    sib3 = sib_row(up(p2, 2))
    for copy in v_second + v_far:
        copy.wait_recv()

    vg_s[...] = jnp.zeros_like(vg_s)
    slope = 0.5 * scale_ref[0]
    shift = 0.5 * bias_ref[0]
    diff = lax.broadcasted_iota(jnp.int32, (128, 128), 0) - lax.broadcasted_iota(
        jnp.int32, (128, 128), 1
    )
    vis_base = [
        (((1 - zz % 2) * 4 + x) * 4 + y) * 2 * clips + core * clips + (zz // 2) * half_clips
        for zz in range(4)
    ]

    def text_base(whose, a2, a1):
        c = core * whose + (1 - core) * (1 - whose)
        xx = a1 * (1 - c) + a2 * c
        yy = a2 * (1 - c) + a1 * c
        return (tm * 64 + ((z_lo * 4 + xx) * 4 + yy) * 2 + c) * 128

    def pair_row(whose, row):
        vis = v_s[...].reshape(4 * half_clips, emb)
        total = None
        for hh in range(2):
            texts = tt_s[whose, row, pl.ds(2 * hh, 2)].reshape(256, emb)
            curve = jnp.tanh(nt(vis, texts) * slope + shift) * 0.5
            tall = []
            for zz in range(4):
                wide = []
                for b in range(2):
                    gap = text_base(whose, row, 2 * hh + b) - vis_base[zz]
                    block = curve[zz * 128 : (zz + 1) * 128, b * 128 : (b + 1) * 128]
                    wide.append(block + jnp.where(diff == gap, -0.5, 0.5))
                tall.append(jnp.concatenate(wide, axis=1))
            grad = jnp.concatenate(tall, axis=0).astype(BF)
            g_s[whose, row, hh] = grad
            part = nn(grad, texts)
            total = part if total is None else total + part
        vg_s[...] += total

    def pair_rows(whose):
        def body(row, carry):
            pair_row(whose, row)
            return carry

        lax.fori_loop(0, 4, body, 0)

    pair_rows(1)
    for copy in (sib0, sib1, sib2, sib3):
        copy.wait_recv()
    pair_rows(0)

    vgb_s[...] = vg_s[...].astype(BF).reshape(4, half_clips, emb)
    g1p = remote(vgb_s.at[z2, hlow], g1_s.at[0], zp)
    g1m = remote(vgb_s.at[z2, hhigh], g1_s.at[1], zm)
    g2p = remote(vgb_s.at[z1, hhigh], g2_s.at[0, hhigh], zp)
    g2m = remote(vgb_s.at[z3, hlow], g2_s.at[1, hlow], zm)
    go(g1p, g1m, g2p, g2m)

    sib_base = counter[0]
    counter[0] += 4

    def sib_copy(rr, row):
        return pltpu.make_async_remote_copy(
            src_ref=tg_s.at[0, row], dst_ref=rsib_s.at[row],
            send_sem=send_sem.at[sib_base + rr], recv_sem=recv_sem.at[sib_base + rr],
            device_id=sibling, device_id_type=MESH,
        )

    def ordered(p, rr):
        return lax.rem(p + 2 + 3 * rr + 3 * (rr // 2) + 2 * (rr // 3), 4)

    def text_terms(whose, row):
        vis = v_s[...].reshape(4 * half_clips, emb)
        grad = jnp.concatenate([g_s[whose, row, 0], g_s[whose, row, 1]], axis=1)
        return tn(grad, vis).reshape(4, 128, emb)

    def sib_rows(rr, carry):
        row = ordered(p1, rr)
        tg_s[0, row] = text_terms(0, row).astype(BF)
        sib_copy(rr, row).start()
        return carry

    lax.fori_loop(0, 4, sib_rows, 0)

    g1p.wait_recv()
    g1m.wait_recv()
    vgb_s[z1, hlow] = (vgb_s[z1, hlow].astype(F32) + g1_s[0].astype(F32)).astype(BF)
    g3p = remote(vgb_s.at[z1, hlow], g2_s.at[0, hlow], zp)
    vgb_s[z3, hhigh] = (vgb_s[z3, hhigh].astype(F32) + g1_s[1].astype(F32)).astype(BF)
    g3m = remote(vgb_s.at[z3, hhigh], g2_s.at[1, hhigh], zm)
    go(g3p, g3m)

    def own_rows(rr, carry):
        row = ordered(p2, rr)
        sib_copy(rr, row).wait_recv()
        tg_s[1, row] = (text_terms(1, row) + rsib_s[row].astype(F32)).astype(BF)
        return carry

    tg = tg_s.at[1]
    lax.fori_loop(0, 1, own_rows, 0)
    s1p = remote(tg.at[up(p2, 2), low], r1_s.at[0], n2p)
    s1m = remote(tg.at[up(p2, 2), high], r1_s.at[1], n2m)
    go(s1p, s1m)
    lax.fori_loop(1, 2, own_rows, 0)
    s2p = remote(tg.at[r3, high], r2_s.at[0, high], n2p)
    go(s2p)
    lax.fori_loop(2, 3, own_rows, 0)
    s2m = remote(tg.at[r1, low], r2_s.at[1, low], n2m)
    go(s2m)

    for copy in (g2p, g2m, g3p, g3m):
        copy.wait_recv()
    out_scale = scale_ref[0] * (1.0 / all_clips)
    vis_grad = (
        vg_s[pl.ds(pl.multiple_of(z * half_clips, 128), half_clips), :]
        + g2_s[0].astype(F32)
        + g2_s[1].astype(F32)
    ) * out_scale
    unit = vu_s[...]
    inner = jnp.sum(vis_grad * unit, axis=1, keepdims=True)
    eg_s[...] = ((vis_grad - unit * inner) / vn_s[:, :1]).astype(BF)
    eg_p = remote(eg_s, egr_s.at[tm], zp)
    eg_m = remote(eg_s, egr_s.at[tm], zm)
    go(eg_p, eg_m)

    lax.fori_loop(3, 4, own_rows, 0)
    eg_p.wait_recv()
    eg_m.wait_recv()
    pg_s[...] = nt(egr_s[...].reshape(clips, emb), ow_s[...]).astype(BF)

    for h, first, wide in pairs:
        if h == HEADS // 2:
            s1p.wait_recv()
            s1m.wait_recv()
            tg_s[1, r3, low] = (tg_s[1, r3, low].astype(F32) + r1_s[0].astype(F32)).astype(BF)
            s3p = remote(tg.at[r3, low], r2_s.at[0, low], n2p)
            go(s3p)
            tg_s[1, r1, high] = (tg_s[1, r1, high].astype(F32) + r1_s[1].astype(F32)).astype(BF)
            s3m = remote(tg.at[r1, high], r2_s.at[1, high], n2m)
            go(s3m)

        grads = pg_s[:, first : first + wide].astype(F32)
        part = jnp.concatenate(
            [jnp.where(window_mask(h + i, first, wide), grads, 0.0).astype(BF) for i in range(2)],
            axis=0,
        )
        for cols in columns:
            q = nt(part, w_s[cols, first : first + wide]).astype(BF)
            pq_s[h : h + 2, :, cols] = q.reshape(2, clips, q.shape[1])

    def score_terms(g, carry):
        frame_part = pl.ds(pl.multiple_of(g * 128, 128), 128)
        clip_part = pl.ds(pl.multiple_of(g * GROUP, GROUP), GROUP)
        q = pq_s[:, clip_part, :].reshape(lanes, width)
        prod = jnp.transpose(nt(q, x_s[frame_part, :]))
        t_s[frame_part, :] = prod
        u_send[pl.ds(g, 1), :] = jnp.sum(prod * e_s[frame_part, :], axis=0, keepdims=True)
        return carry

    lax.fori_loop(0, groups, score_terms, 0, unroll=4)
    uc = remote(u_send, u_recv, partner)
    uc.start()

    def vp_copy(g):
        frame_part = pl.ds(pl.multiple_of(g * 128, 128), 128)
        return pltpu.make_async_copy(
            x_s.at[frame_part], vp_hbm.at[frame_part], out_sem.at[g]
        )

    def value_part(g, carry):
        frame_part = pl.ds(pl.multiple_of(g * 128, 128), 128)
        clip_part = pl.ds(pl.multiple_of(g * GROUP, GROUP), GROUP)
        for cols in columns:
            q = pq_s[:, clip_part, cols]
            q = q.reshape(lanes, q.shape[2])
            x_s[frame_part, cols] = nn(a_s[frame_part, :], q).astype(BF)
        vp_copy(g).start()
        return carry

    lax.fori_loop(0, groups // 4, value_part, 0, unroll=4)

    for copy in (s2p, s2m, s3p, s3m):
        copy.wait_recv()
    for b in range(4):
        total = tg_s[1, p2, b].astype(F32) + r2_s[0, b].astype(F32) + r2_s[1, b].astype(F32)
        tr_s[b] = total.astype(BF)
    b1, b2, b3 = up(p1, 1), up(p1, 2), up(p1, 3)
    tlow, thigh = pl.ds(0, 64), pl.ds(64, 64)
    u1p = remote(tr_s.at[b2, tlow], q1_s.at[0], n1p)
    u1m = remote(tr_s.at[b2, thigh], q1_s.at[1], n1m)
    u2p = remote(tr_s.at[b1, thigh], q2_s.at[0, thigh], n1p)
    u2m = remote(tr_s.at[b3, tlow], q2_s.at[1, tlow], n1m)
    go(u1p, u1m, u2p, u2m)

    lax.fori_loop(groups // 4, 3 * groups // 4, value_part, 0, unroll=4)
    u1p.wait_recv()
    u1m.wait_recv()
    tr_s[b1, tlow] = (tr_s[b1, tlow].astype(F32) + q1_s[0].astype(F32)).astype(BF)
    u3p = remote(tr_s.at[b1, tlow], q2_s.at[0, tlow], n1p)
    tr_s[b3, thigh] = (tr_s[b3, thigh].astype(F32) + q1_s[1].astype(F32)).astype(BF)
    u3m = remote(tr_s.at[b3, thigh], q2_s.at[1, thigh], n1m)
    go(u3p, u3m)

    lax.fori_loop(3 * groups // 4, groups, value_part, 0, unroll=4)

    uc.wait()
    u_send[...] = u_send[...] + u_recv[...]

    def score_grads(g, carry):
        frame_part = pl.ds(pl.multiple_of(g * 128, 128), 128)
        centred = t_s[frame_part, :] - u_send[pl.ds(g, 1), :]
        sg_s[frame_part, :] = (e_s[frame_part, :] * centred * root).astype(BF)
        return carry

    sg_out = []
    for i in range(2):
        lax.fori_loop(i * groups // 2, (i + 1) * groups // 2, score_grads, 0, unroll=4)
        part = pl.ds(i * rows // 2, rows // 2)
        sg_out.append(pltpu.make_async_copy(sg_s.at[part], sg_hbm.at[part], load_sem.at[9 + i]))
        sg_out[i].start()

    for copy in (u2p, u2m, u3p, u3m):
        copy.wait_recv()
    gt_ref[...] = (
        tr_s[p1].astype(F32) + q2_s[0].astype(F32) + q2_s[1].astype(F32)
    ) * out_scale
    gt_out = pltpu.make_async_copy(gt_ref, gt_hbm, load_sem.at[8])
    gt_out.start()

    for copy in sent:
        copy.wait_send()

    def drain(rr, carry):
        sib_copy(rr, ordered(p1, rr)).wait_send()
        return carry

    lax.fori_loop(0, 4, drain, 0)

    def drain_vp(g, carry):
        vp_copy(g).wait()
        return carry

    lax.fori_loop(0, groups, drain_vp, 0)
    for copy in sg_out:
        copy.wait()
    gt_out.wait()


def final_kernel(
    vp_hbm, sg_hbm, key_hbm, texts_hbm, tg_hbm, out_hbm, gt_hbm,
    vp_s, sg_s, key_in, key_s, texts_s, tg_s, gt_s, vp_sem, sg_sem, out_sem, small_sem,
):
    rows, width = vp_s.shape
    steps = 8
    step = rows // steps
    parts = [pl.ds(i * step, step) for i in range(steps)]
    load_key = pltpu.make_async_copy(key_hbm, key_in, small_sem.at[0])
    load_texts = pltpu.make_async_copy(texts_hbm, texts_s, small_sem.at[1])
    load_tg = pltpu.make_async_copy(tg_hbm, tg_s, small_sem.at[2])
    load_key.start()
    load_vp, load_sg, outs = [], [], []
    for i, part in enumerate(parts):
        load_sg.append(pltpu.make_async_copy(sg_hbm.at[part], sg_s.at[part], sg_sem.at[i]))
        load_vp.append(pltpu.make_async_copy(vp_hbm.at[part], vp_s.at[part], vp_sem.at[i]))
        outs.append(pltpu.make_async_copy(vp_s.at[part], out_hbm.at[part], out_sem.at[i]))
        load_sg[i].start()
        load_vp[i].start()
        if i == 1:
            load_texts.start()
            load_tg.start()
    load_key.wait()
    repeat_heads(key_in, key_s)
    for i, part in enumerate(parts):
        load_sg[i].wait()
        load_vp[i].wait()
        for start in range(0, width, 256):
            cols = slice(start, min(start + 256, width))
            total = vp_s[part, cols].astype(F32) + nn(sg_s[part, :], key_s[:, cols])
            vp_s[part, cols] = total.astype(BF)
        outs[i].start()
        if i == 2:
            load_texts.wait()
            load_tg.wait()
            text_full = texts_s[...].astype(F32)
            text_norm = jnp.sqrt(jnp.sum(text_full * text_full, axis=1, keepdims=True) + EPSILON)
            text_unit = text_full / text_norm
            text_grad = tg_s[...]
            inner = jnp.sum(text_grad * text_unit, axis=1, keepdims=True)
            gt_s[...] = (text_grad - text_unit * inner) / text_norm
            gt_out = pltpu.make_async_copy(gt_s, gt_hbm, small_sem.at[3])
            gt_out.start()
    for copy in outs:
        copy.wait()
    gt_out.wait()


def local(frames, key_proj, value_weight, out_weight, texts, logit_scale, logit_bias):
    clips, frames_here, width = frames.shape
    heads = key_proj.shape[1]
    head = width // heads
    emb = out_weight.shape[1]
    all_clips = clips * lax.axis_size("clip")
    rows = clips * frames_here
    half = clips // 2
    frame_rows = frames.reshape(rows, width)
    key_t = key_proj.T
    V = pltpu.VMEM
    copies = 48
    scratch = [
        V((heads, width), BF),
        V((128, emb), BF),
        V((128, emb), F32),
        V((rows, width), BF),
        V((width, width), BF),
        V((width, emb), BF),
        V((heads * GROUP, width), BF),
        V((heads, clips, width), BF),
        V((rows, heads * GROUP), F32),
        V((2, clips // GROUP, heads * GROUP), F32),
        V((2, clips // GROUP, heads * GROUP), F32),
        V((clips // GROUP, heads * GROUP), F32),
        V((clips, width), F32),
        V((rows, heads * GROUP), BF),
        V((rows, heads * GROUP), BF),
        V((rows, heads * GROUP), F32),
        V((2, 4, 4, 128, emb), BF),
        V((2, 4, 4, 128, emb), BF),
        V((4, 4, 128, emb), BF),
        V((2, 2, 128, emb), BF),
        V((2, 4, 128, emb), BF),
        V((4, 128, emb), BF),
        V((2, 64, emb), BF),
        V((2, 128, emb), BF),
        V((2, 4, 2, 4 * half, 256), BF),
        V((2, half, emb), BF),
        V((2, half, emb), BF),
        V((half, emb), F32),
        V((half, 128), F32),
        V((4, half, emb), BF),
        V((4 * half, emb), F32),
        V((4, half, emb), BF),
        V((2, half // 2, emb), BF),
        V((2, half, emb), BF),
        V((half, emb), BF),
        V((2, half, emb), BF),
        V((clips, width), BF),
        V((clips // GROUP, heads * GROUP), F32),
        V((clips // GROUP, heads * GROUP), F32),
        pltpu.SemaphoreType.DMA((11,)),
        pltpu.SemaphoreType.DMA((clips // GROUP,)),
        pltpu.SemaphoreType.DMA((copies,)),
        pltpu.SemaphoreType.DMA((copies,)),
    ]
    anywhere = pl.BlockSpec(memory_space=pl.ANY)
    smem = pl.BlockSpec(memory_space=pltpu.SMEM)
    value_part, score_grad, text_grad = pl.pallas_call(
        functools.partial(main_kernel, (clips, width, head, emb, all_clips)),
        out_shape=(
            jax.ShapeDtypeStruct((rows, width), BF),
            jax.ShapeDtypeStruct((rows, heads * GROUP), BF),
            jax.ShapeDtypeStruct((128, emb), F32),
        ),
        in_specs=[anywhere] * 5 + [smem] * 2,
        out_specs=(anywhere, anywhere, anywhere),
        scratch_shapes=scratch,
        compiler_params=pltpu.CompilerParams(
            collective_id=0, has_side_effects=True, vmem_limit_bytes=60 * 1024 * 1024
        ),
        name="pool_pair_back",
    )(frame_rows, key_t, value_weight, out_weight, texts, logit_scale, logit_bias)
    steps = 8
    grad_frames, grad_texts = pl.pallas_call(
        final_kernel,
        in_specs=[anywhere] * 5,
        out_specs=(anywhere, anywhere),
        out_shape=(
            jax.ShapeDtypeStruct((rows, width), BF),
            jax.ShapeDtypeStruct((128, emb), F32),
        ),
        scratch_shapes=[
            V((rows, width), BF),
            V((rows, heads * GROUP), BF),
            V((heads, width), BF),
            V((heads * GROUP, width), BF),
            V((128, emb), BF),
            V((128, emb), F32),
            V((128, emb), F32),
            pltpu.SemaphoreType.DMA((steps,)),
            pltpu.SemaphoreType.DMA((steps,)),
            pltpu.SemaphoreType.DMA((steps,)),
            pltpu.SemaphoreType.DMA((4,)),
        ],
        compiler_params=pltpu.CompilerParams(vmem_limit_bytes=60 * 1024 * 1024),
        name="frame_grads",
    )(value_part, score_grad, key_t, texts, text_grad)
    return (grad_frames.reshape(clips, frames_here, width), grad_texts)


def solution(mesh):
    in_specs = (P("clip", "tm", None), P(), P(), P(), P(("tm", "clip"), None), P(), P())
    out_specs = (P("clip", "tm", None), P(("tm", "clip"), None))
    return jax.shard_map(local, mesh=mesh, in_specs=in_specs, out_specs=out_specs, check_vma=False)
```

```python
import functools
import math

import jax
import jax.numpy as jnp
from jax import lax
from jax.experimental import pallas as pl
from jax.experimental.pallas import tpu as pltpu
from jax.sharding import PartitionSpec as P

EPSILON = 1e-06
MESH = pl.DeviceIdType.MESH
BF = jnp.bfloat16
F32 = jnp.float32
NT = (((1,), (1,)), ((), ()))
TN = (((0,), (0,)), ((), ()))
HEADS = 16
GROUP = 16


def nt(a, b):
    return lax.dot_general(a, b, NT, preferred_element_type=F32)


def tn(a, b):
    return lax.dot_general(a, b, TN, preferred_element_type=F32)


def nn(a, b):
    return jnp.dot(a, b, preferred_element_type=F32)


def own_clip_mask(rows_per_clip):
    shape = (GROUP * rows_per_clip, HEADS * GROUP)
    row = lax.broadcasted_iota(jnp.int32, shape, 0)
    lane = lax.broadcasted_iota(jnp.int32, shape, 1) & (GROUP - 1)
    start = lane * rows_per_clip
    return jnp.where((row >= start) & (row < start + rows_per_clip), 1.0, 0.0)


def repeat_heads(key_ref, out_ref):
    for h in range(HEADS):
        row = key_ref[h : h + 1, :].astype(F32)
        wide = jnp.broadcast_to(row, (GROUP, row.shape[1])).astype(BF)
        out_ref[h * GROUP : (h + 1) * GROUP, :] = wide


def main_kernel(
    dims,
    frames_hbm, key_hbm, value_hbm, out_hbm, texts_hbm, scale_ref, bias_ref,
    vp_hbm, sg_hbm, gt_hbm,
    key_ref, texts_ref, gt_ref,
    x_s, w_s, ow_s, key_s, pq_s, e_s, ms_send, ms_recv, alpha_s, acc_s, a_s, sg_s, t_s,
    tt_s, tg_s, rsib_s, r1_s, r2_s, tr_s, q1_s, q2_s, g_s,
    embp_s, embr_s, vu_s, vn_s, v_s, vg_s, vgb_s, g1_s, g2_s, eg_s, egr_s, pg_s, u_send, u_recv,
    load_sem, out_sem, send_sem, recv_sem,
):
    clips, width, head, emb, all_clips = dims
    frames_here = 8
    rows = clips * frames_here
    groups = clips // GROUP
    half_clips = clips // 2
    root = 1.0 / math.sqrt(width)

    tm = lax.axis_index("tm")
    ci = lax.axis_index("clip")
    core = lax.rem(ci, 2)
    y = lax.rem(ci // 2, 4)
    x = lax.rem(ci // 8, 4)
    z_lo = ci // 32
    z = tm * 2 + z_lo

    def at(xx, yy, zz, cc):
        return (zz // 2, ((lax.rem(zz, 2) * 4 + xx) * 4 + yy) * 2 + cc)

    def up(a, n):
        return lax.rem(a + n, 4)

    p1 = x * (1 - core) + y * core
    p2 = y * (1 - core) + x * core

    def plane(a1, a2):
        return at(a1 * (1 - core) + a2 * core, a2 * (1 - core) + a1 * core, z, core)

    n1p, n1m = plane(up(p1, 1), p2), plane(up(p1, 3), p2)
    n2p, n2m = plane(p1, up(p2, 1)), plane(p1, up(p2, 3))
    zp, zm = at(x, y, up(z, 1), core), at(x, y, up(z, 3), core)
    partner = (1 - tm, ci)
    sibling = at(x, y, z, 1 - core)

    counter = [0]

    def remote(src, dst, device):
        k = counter[0]
        counter[0] += 1
        return pltpu.make_async_remote_copy(
            src_ref=src, dst_ref=dst, send_sem=send_sem.at[k], recv_sem=recv_sem.at[k],
            device_id=device, device_id_type=MESH,
        )

    chunk = rows // 4
    loads = [
        pltpu.make_async_copy(
            frames_hbm.at[pl.ds(i * chunk, chunk)], x_s.at[pl.ds(i * chunk, chunk)], load_sem.at[i]
        )
        for i in range(4)
    ]
    load_w = pltpu.make_async_copy(value_hbm, w_s, load_sem.at[4])
    load_ow = pltpu.make_async_copy(out_hbm, ow_s, load_sem.at[5])
    load_key = pltpu.make_async_copy(key_hbm, key_ref, load_sem.at[6])
    load_texts = pltpu.make_async_copy(texts_hbm, texts_ref, load_sem.at[7])
    load_texts.start()
    load_key.start()
    for load in loads:
        load.start()
    load_w.start()
    load_ow.start()

    barrier = pltpu.get_barrier_semaphore()
    greet = (n1p, n1m, n2p, n2m, zp, zm, partner, sibling)
    for device in greet:
        pl.semaphore_signal(barrier, inc=1, device_id=device, device_id_type=MESH)

    load_texts.wait()
    text_full = texts_ref[...].astype(F32)
    text_norm = jnp.sqrt(jnp.sum(text_full * text_full, axis=1, keepdims=True) + EPSILON)
    tt_s[1, p2, p1] = (text_full / text_norm).astype(BF)
    load_key.wait()
    repeat_heads(key_ref, key_s)

    pl.semaphore_wait(barrier, len(greet))

    sent = []

    def go(*copies):
        for copy in copies:
            copy.start()
            sent.append(copy)

    own = tt_s.at[1]
    a0p = remote(own.at[p2, p1], own.at[p2, p1], n1p)
    a0m = remote(own.at[p2, p1], own.at[p2, p1], n1m)
    go(a0p, a0m)

    mask = own_clip_mask(frames_here)
    clip_mask = own_clip_mask(1)
    lanes = HEADS * GROUP

    def own_lane(per_clip):
        picked = per_clip.reshape(per_clip.shape[0] // GROUP, GROUP, lanes) * clip_mask[None]
        return jnp.sum(picked, axis=1)

    for i in range(4):
        loads[i].wait()
        part = pl.ds(i * chunk, chunk)
        s = nt(x_s[part, :], key_s[...]) * root
        s3 = s.reshape(chunk // frames_here, frames_here, lanes)
        top = jnp.max(s3, axis=1)
        e3 = jnp.exp(s3 - top[:, None, :])
        e_s[part, :] = e3.reshape(chunk, lanes)
        group_part = pl.ds(i * groups // 4, groups // 4)
        ms_send[0, group_part, :] = own_lane(top)
        ms_send[1, group_part, :] = own_lane(jnp.sum(e3, axis=1))
    ms = remote(ms_send, ms_recv, partner)
    go(ms)

    def a1():
        a0p.wait_recv()
        a0m.wait_recv()
        low, high = pl.ds(0, 64), pl.ds(64, 64)
        b1, b3 = up(p1, 3), up(p1, 1)
        cp = remote(own.at[p2, b1, low], own.at[p2, b1, low], n1p)
        cm = remote(own.at[p2, b3, high], own.at[p2, b3, high], n1m)
        go(cp, cm)
        return cp, cm

    def sib_row(row):
        copy = remote(own.at[row], tt_s.at[0, row], sibling)
        go(copy)
        return copy

    fwd1 = a1()

    columns = [slice(at, min(at + 256, width)) for at in range(0, width, 256)]

    def pool_group(g, carry):
        frame_part = pl.ds(pl.multiple_of(g * 128, 128), 128)
        clip_part = pl.ds(pl.multiple_of(g * GROUP, GROUP), GROUP)
        weight = jnp.transpose(e_s[frame_part, :] * mask).astype(BF)
        for cols in columns:
            pooled = nn(weight, x_s[frame_part, cols]).astype(BF)
            pq_s[:, clip_part, cols] = pooled.reshape(HEADS, GROUP, pooled.shape[1])
        return carry

    lax.fori_loop(0, groups // 2, pool_group, 0, unroll=4)

    for copy in fwd1:
        copy.wait_recv()
    row_p = remote(own.at[p2], own.at[p2], n2p)
    row_m = remote(own.at[p2], own.at[p2], n2m)
    go(row_p, row_m)
    sib0 = sib_row(p2)

    lax.fori_loop(groups // 2, groups, pool_group, 0, unroll=4)

    load_w.wait()
    load_ow.wait()
    acc_s[...] = jnp.zeros_like(acc_s)

    pairs = []
    for h in range(0, HEADS, 2):
        first = min(h * head // 128, width // 128 - 2) * 128
        wide = 256 if (h + 2) * head <= first + 256 else 384
        pairs.append((h, first, wide))

    def window_mask(h, first, wide):
        lane = lax.broadcasted_iota(jnp.int32, (1, wide), 1)
        offset = h * head - first
        return (lane >= offset) & (lane < offset + head)

    for h, first, wide in pairs:
        cols = slice(first, first + wide)
        part = nn(pq_s[h : h + 2].reshape(2 * clips, width), w_s[:, cols])
        acc_s[:, cols] += jnp.where(window_mask(h, first, wide), part[:clips], 0.0) + jnp.where(
            window_mask(h + 1, first, wide), part[clips:], 0.0
        )

    ms.wait_recv()
    mine, theirs = ms_send[0], ms_recv[0]
    top = jnp.maximum(mine, theirs)
    mine_f, theirs_f = jnp.exp(mine - top), jnp.exp(theirs - top)
    alpha = mine_f / (ms_send[1] * mine_f + ms_recv[1] * theirs_f)
    alpha_s[...] = alpha
    spread = (alpha[:, None, :] * clip_mask[None]).reshape(clips, lanes)
    head_start = (lax.broadcasted_iota(jnp.int32, (lanes, width), 0) // GROUP) * head
    head_lane = lax.broadcasted_iota(jnp.int32, (lanes, width), 1)
    in_head = (head_lane >= head_start) & (head_lane < head_start + head)
    pooled = (acc_s[...] * nn(spread.astype(BF), jnp.where(in_head, 1.0, 0.0).astype(BF))).astype(BF)
    embp_s[...] = nn(pooled, ow_s[...]).astype(BF).reshape(2, half_clips, emb)
    er_p = remote(embp_s.at[up(z, 1) // 2], embr_s.at[0], zp)
    er_m = remote(embp_s.at[up(z, 3) // 2], embr_s.at[1], zm)
    go(er_p, er_m)

    row_p.wait_recv()
    row_m.wait_recv()
    r1, r3 = up(p2, 3), up(p2, 1)
    low, high = pl.ds(0, 2), pl.ds(2, 2)
    fwd_p = remote(own.at[r1, low], own.at[r1, low], n2p)
    fwd_m = remote(own.at[r3, high], own.at[r3, high], n2m)
    go(fwd_p, fwd_m)
    sib1 = sib_row(r3)
    sib2 = sib_row(r1)

    def weights(g, carry):
        frame_part = pl.ds(pl.multiple_of(g * 128, 128), 128)
        wide = e_s[frame_part, :] * mask * alpha_s[pl.ds(g, 1), :]
        e_s[frame_part, :] = wide
        a_s[frame_part, :] = wide.astype(BF)
        return carry

    lax.fori_loop(0, groups // 2, weights, 0, unroll=4)

    er_p.wait_recv()
    er_m.wait_recv()
    embedding = embr_s[0].astype(F32) + embr_s[1].astype(F32)
    vis_norm = jnp.sqrt(jnp.sum(embedding * embedding, axis=1, keepdims=True) + EPSILON)
    vis_unit = embedding / vis_norm
    vu_s[...] = vis_unit
    vn_s[...] = jnp.broadcast_to(vis_norm, vn_s.shape)
    v_s[z] = vis_unit.astype(BF)
    hlow, hhigh = pl.ds(0, half_clips // 2), pl.ds(half_clips // 2, half_clips // 2)

    def send_vis(at_z, half, device):
        copy = remote(v_s.at[at_z, half], v_s.at[at_z, half], device)
        go(copy)
        return copy

    v_first = send_vis(z, hlow, zp), send_vis(z, hhigh, zm)
    v_second = send_vis(z, hhigh, zp), send_vis(z, hlow, zm)
    lax.fori_loop(groups // 2, groups, weights, 0, unroll=4)
    z1, z2, z3 = up(z, 1), up(z, 2), up(z, 3)
    for copy in v_first:
        copy.wait_recv()
    v_far = send_vis(z3, hlow, zp), send_vis(z1, hhigh, zm)

    fwd_p.wait_recv()
    fwd_m.wait_recv()
    sib3 = sib_row(up(p2, 2))
    for copy in v_second + v_far:
        copy.wait_recv()

    vg_s[...] = jnp.zeros_like(vg_s)
    slope = 0.5 * scale_ref[0]
    shift = 0.5 * bias_ref[0]
    diff = lax.broadcasted_iota(jnp.int32, (128, 128), 0) - lax.broadcasted_iota(
        jnp.int32, (128, 128), 1
    )
    vis_base = [
        (((1 - zz % 2) * 4 + x) * 4 + y) * 2 * clips + core * clips + (zz // 2) * half_clips
        for zz in range(4)
    ]

    def text_base(whose, a2, a1):
        c = core * whose + (1 - core) * (1 - whose)
        xx = a1 * (1 - c) + a2 * c
        yy = a2 * (1 - c) + a1 * c
        return (tm * 64 + ((z_lo * 4 + xx) * 4 + yy) * 2 + c) * 128

    def pair_row(whose, row):
        vis = v_s[...].reshape(4 * half_clips, emb)
        total = None
        for hh in range(2):
            texts = tt_s[whose, row, pl.ds(2 * hh, 2)].reshape(256, emb)
            curve = jnp.tanh(nt(vis, texts) * slope + shift) * 0.5
            tall = []
            for zz in range(4):
                wide = []
                for b in range(2):
                    gap = text_base(whose, row, 2 * hh + b) - vis_base[zz]
                    block = curve[zz * 128 : (zz + 1) * 128, b * 128 : (b + 1) * 128]
                    wide.append(block + jnp.where(diff == gap, -0.5, 0.5))
                tall.append(jnp.concatenate(wide, axis=1))
            grad = jnp.concatenate(tall, axis=0).astype(BF)
            g_s[whose, row, hh] = grad
            part = nn(grad, texts)
            total = part if total is None else total + part
        vg_s[...] += total

    def pair_rows(whose):
        def body(row, carry):
            pair_row(whose, row)
            return carry

        lax.fori_loop(0, 4, body, 0)

    pair_rows(1)
    for copy in (sib0, sib1, sib2, sib3):
        copy.wait_recv()
    pair_rows(0)

    vgb_s[...] = vg_s[...].astype(BF).reshape(4, half_clips, emb)
    g1p = remote(vgb_s.at[z2, hlow], g1_s.at[0], zp)
    g1m = remote(vgb_s.at[z2, hhigh], g1_s.at[1], zm)
    g2p = remote(vgb_s.at[z1, hhigh], g2_s.at[0, hhigh], zp)
    g2m = remote(vgb_s.at[z3, hlow], g2_s.at[1, hlow], zm)
    go(g1p, g1m, g2p, g2m)

    sib_base = counter[0]
    counter[0] += 4

    def sib_copy(rr, row):
        return pltpu.make_async_remote_copy(
            src_ref=tg_s.at[0, row], dst_ref=rsib_s.at[row],
            send_sem=send_sem.at[sib_base + rr], recv_sem=recv_sem.at[sib_base + rr],
            device_id=sibling, device_id_type=MESH,
        )

    def ordered(p, rr):
        return lax.rem(p + 2 + 3 * rr + 3 * (rr // 2) + 2 * (rr // 3), 4)

    def text_terms(whose, row):
        vis = v_s[...].reshape(4 * half_clips, emb)
        grad = jnp.concatenate([g_s[whose, row, 0], g_s[whose, row, 1]], axis=1)
        return tn(grad, vis).reshape(4, 128, emb)

    def sib_rows(rr, carry):
        row = ordered(p1, rr)
        tg_s[0, row] = text_terms(0, row).astype(BF)
        return carry

    lax.fori_loop(0, 4, sib_rows, 0)

    g1p.wait_recv()
    g1m.wait_recv()
    vgb_s[z1, hlow] = (vgb_s[z1, hlow].astype(F32) + g1_s[0].astype(F32)).astype(BF)
    g3p = remote(vgb_s.at[z1, hlow], g2_s.at[0, hlow], zp)
    vgb_s[z3, hhigh] = (vgb_s[z3, hhigh].astype(F32) + g1_s[1].astype(F32)).astype(BF)
    g3m = remote(vgb_s.at[z3, hhigh], g2_s.at[1, hhigh], zm)
    go(g3p, g3m)

    def sib_send(rr, carry):
        sib_copy(rr, ordered(p1, rr)).start()
        return carry

    lax.fori_loop(0, 4, sib_send, 0)

    def own_rows(row, carry):
        tg_s[1, row] = text_terms(1, row).astype(BF)
        return carry

    lax.fori_loop(0, 4, own_rows, 0)

    for copy in (g2p, g2m, g3p, g3m):
        copy.wait_recv()
    out_scale = scale_ref[0] * (1.0 / all_clips)
    vis_grad = (
        vg_s[pl.ds(pl.multiple_of(z * half_clips, 128), half_clips), :]
        + g2_s[0].astype(F32)
        + g2_s[1].astype(F32)
    ) * out_scale
    unit = vu_s[...]
    inner = jnp.sum(vis_grad * unit, axis=1, keepdims=True)
    eg_s[...] = ((vis_grad - unit * inner) / vn_s[:, :1]).astype(BF)
    eg_p = remote(eg_s, egr_s.at[tm], zp)
    eg_m = remote(eg_s, egr_s.at[tm], zm)
    go(eg_p, eg_m)

    def add_sibling(rr, carry):
        row = ordered(p2, rr)
        sib_copy(rr, row).wait_recv()
        tg_s[1, row] = (tg_s[1, row].astype(F32) + rsib_s[row].astype(F32)).astype(BF)
        return carry

    tg = tg_s.at[1]
    lax.fori_loop(0, 1, add_sibling, 0)
    s1p = remote(tg.at[up(p2, 2), low], r1_s.at[0], n2p)
    s1m = remote(tg.at[up(p2, 2), high], r1_s.at[1], n2m)
    go(s1p, s1m)
    lax.fori_loop(1, 3, add_sibling, 0)
    s2p = remote(tg.at[r3, high], r2_s.at[0, high], n2p)
    s2m = remote(tg.at[r1, low], r2_s.at[1, low], n2m)
    go(s2p, s2m)
    lax.fori_loop(3, 4, add_sibling, 0)
    eg_p.wait_recv()
    eg_m.wait_recv()
    pg_s[...] = nt(egr_s[...].reshape(clips, emb), ow_s[...]).astype(BF)

    for h, first, wide in pairs:
        if h == HEADS // 2:
            s1p.wait_recv()
            s1m.wait_recv()
            tg_s[1, r3, low] = (tg_s[1, r3, low].astype(F32) + r1_s[0].astype(F32)).astype(BF)
            s3p = remote(tg.at[r3, low], r2_s.at[0, low], n2p)
            go(s3p)
            tg_s[1, r1, high] = (tg_s[1, r1, high].astype(F32) + r1_s[1].astype(F32)).astype(BF)
            s3m = remote(tg.at[r1, high], r2_s.at[1, high], n2m)
            go(s3m)

        grads = pg_s[:, first : first + wide].astype(F32)
        part = jnp.concatenate(
            [jnp.where(window_mask(h + i, first, wide), grads, 0.0).astype(BF) for i in range(2)],
            axis=0,
        )
        for cols in columns:
            q = nt(part, w_s[cols, first : first + wide]).astype(BF)
            pq_s[h : h + 2, :, cols] = q.reshape(2, clips, q.shape[1])

    def score_terms(g, carry):
        frame_part = pl.ds(pl.multiple_of(g * 128, 128), 128)
        clip_part = pl.ds(pl.multiple_of(g * GROUP, GROUP), GROUP)
        q = pq_s[:, clip_part, :].reshape(lanes, width)
        prod = jnp.transpose(nt(q, x_s[frame_part, :]))
        t_s[frame_part, :] = prod
        u_send[pl.ds(g, 1), :] = jnp.sum(prod * e_s[frame_part, :], axis=0, keepdims=True)
        return carry

    lax.fori_loop(0, groups, score_terms, 0, unroll=4)
    uc = remote(u_send, u_recv, partner)
    uc.start()

    def vp_copy(g):
        frame_part = pl.ds(pl.multiple_of(g * 128, 128), 128)
        return pltpu.make_async_copy(
            x_s.at[frame_part], vp_hbm.at[frame_part], out_sem.at[g]
        )

    def value_part(g, carry):
        frame_part = pl.ds(pl.multiple_of(g * 128, 128), 128)
        clip_part = pl.ds(pl.multiple_of(g * GROUP, GROUP), GROUP)
        for cols in columns:
            q = pq_s[:, clip_part, cols]
            q = q.reshape(lanes, q.shape[2])
            x_s[frame_part, cols] = nn(a_s[frame_part, :], q).astype(BF)
        vp_copy(g).start()
        return carry

    lax.fori_loop(0, groups // 4, value_part, 0, unroll=4)

    for copy in (s2p, s2m, s3p, s3m):
        copy.wait_recv()
    for b in range(4):
        total = tg_s[1, p2, b].astype(F32) + r2_s[0, b].astype(F32) + r2_s[1, b].astype(F32)
        tr_s[b] = total.astype(BF)
    b1, b2, b3 = up(p1, 1), up(p1, 2), up(p1, 3)
    tlow, thigh = pl.ds(0, 64), pl.ds(64, 64)
    u1p = remote(tr_s.at[b2, tlow], q1_s.at[0], n1p)
    u1m = remote(tr_s.at[b2, thigh], q1_s.at[1], n1m)
    u2p = remote(tr_s.at[b1, thigh], q2_s.at[0, thigh], n1p)
    u2m = remote(tr_s.at[b3, tlow], q2_s.at[1, tlow], n1m)
    go(u1p, u1m, u2p, u2m)

    lax.fori_loop(groups // 4, 3 * groups // 4, value_part, 0, unroll=4)
    u1p.wait_recv()
    u1m.wait_recv()
    tr_s[b1, tlow] = (tr_s[b1, tlow].astype(F32) + q1_s[0].astype(F32)).astype(BF)
    u3p = remote(tr_s.at[b1, tlow], q2_s.at[0, tlow], n1p)
    tr_s[b3, thigh] = (tr_s[b3, thigh].astype(F32) + q1_s[1].astype(F32)).astype(BF)
    u3m = remote(tr_s.at[b3, thigh], q2_s.at[1, thigh], n1m)
    go(u3p, u3m)

    lax.fori_loop(3 * groups // 4, groups, value_part, 0, unroll=4)

    uc.wait()
    u_send[...] = u_send[...] + u_recv[...]

    def score_grads(g, carry):
        frame_part = pl.ds(pl.multiple_of(g * 128, 128), 128)
        centred = t_s[frame_part, :] - u_send[pl.ds(g, 1), :]
        sg_s[frame_part, :] = (e_s[frame_part, :] * centred * root).astype(BF)
        return carry

    sg_out = []
    for i in range(2):
        lax.fori_loop(i * groups // 2, (i + 1) * groups // 2, score_grads, 0, unroll=4)
        part = pl.ds(i * rows // 2, rows // 2)
        sg_out.append(pltpu.make_async_copy(sg_s.at[part], sg_hbm.at[part], load_sem.at[9 + i]))
        sg_out[i].start()

    for copy in (u2p, u2m, u3p, u3m):
        copy.wait_recv()
    gt_ref[...] = (
        tr_s[p1].astype(F32) + q2_s[0].astype(F32) + q2_s[1].astype(F32)
    ) * out_scale
    gt_out = pltpu.make_async_copy(gt_ref, gt_hbm, load_sem.at[8])
    gt_out.start()

    for copy in sent:
        copy.wait_send()

    def drain(rr, carry):
        sib_copy(rr, ordered(p1, rr)).wait_send()
        return carry

    lax.fori_loop(0, 4, drain, 0)

    def drain_vp(g, carry):
        vp_copy(g).wait()
        return carry

    lax.fori_loop(0, groups, drain_vp, 0)
    for copy in sg_out:
        copy.wait()
    gt_out.wait()


def final_kernel(
    vp_hbm, sg_hbm, key_hbm, texts_hbm, tg_hbm, out_hbm, gt_hbm,
    vp_s, sg_s, key_in, key_s, texts_s, tg_s, gt_s, vp_sem, sg_sem, out_sem, small_sem,
):
    rows, width = vp_s.shape
    steps = 8
    step = rows // steps
    parts = [pl.ds(i * step, step) for i in range(steps)]
    load_key = pltpu.make_async_copy(key_hbm, key_in, small_sem.at[0])
    load_texts = pltpu.make_async_copy(texts_hbm, texts_s, small_sem.at[1])
    load_tg = pltpu.make_async_copy(tg_hbm, tg_s, small_sem.at[2])
    load_key.start()
    load_vp, load_sg, outs = [], [], []
    for i, part in enumerate(parts):
        load_sg.append(pltpu.make_async_copy(sg_hbm.at[part], sg_s.at[part], sg_sem.at[i]))
        load_vp.append(pltpu.make_async_copy(vp_hbm.at[part], vp_s.at[part], vp_sem.at[i]))
        outs.append(pltpu.make_async_copy(vp_s.at[part], out_hbm.at[part], out_sem.at[i]))
        load_sg[i].start()
        load_vp[i].start()
        if i == 1:
            load_texts.start()
            load_tg.start()
    load_key.wait()
    repeat_heads(key_in, key_s)
    for i, part in enumerate(parts):
        load_sg[i].wait()
        load_vp[i].wait()
        for start in range(0, width, 256):
            cols = slice(start, min(start + 256, width))
            total = vp_s[part, cols].astype(F32) + nn(sg_s[part, :], key_s[:, cols])
            vp_s[part, cols] = total.astype(BF)
        outs[i].start()
        if i == 2:
            load_texts.wait()
            load_tg.wait()
            text_full = texts_s[...].astype(F32)
            text_norm = jnp.sqrt(jnp.sum(text_full * text_full, axis=1, keepdims=True) + EPSILON)
            text_unit = text_full / text_norm
            text_grad = tg_s[...]
            inner = jnp.sum(text_grad * text_unit, axis=1, keepdims=True)
            gt_s[...] = (text_grad - text_unit * inner) / text_norm
            gt_out = pltpu.make_async_copy(gt_s, gt_hbm, small_sem.at[3])
            gt_out.start()
    for copy in outs:
        copy.wait()
    gt_out.wait()


def local(frames, key_proj, value_weight, out_weight, texts, logit_scale, logit_bias):
    clips, frames_here, width = frames.shape
    heads = key_proj.shape[1]
    head = width // heads
    emb = out_weight.shape[1]
    all_clips = clips * lax.axis_size("clip")
    rows = clips * frames_here
    half = clips // 2
    frame_rows = frames.reshape(rows, width)
    key_t = key_proj.T
    V = pltpu.VMEM
    copies = 48
    scratch = [
        V((heads, width), BF),
        V((128, emb), BF),
        V((128, emb), F32),
        V((rows, width), BF),
        V((width, width), BF),
        V((width, emb), BF),
        V((heads * GROUP, width), BF),
        V((heads, clips, width), BF),
        V((rows, heads * GROUP), F32),
        V((2, clips // GROUP, heads * GROUP), F32),
        V((2, clips // GROUP, heads * GROUP), F32),
        V((clips // GROUP, heads * GROUP), F32),
        V((clips, width), F32),
        V((rows, heads * GROUP), BF),
        V((rows, heads * GROUP), BF),
        V((rows, heads * GROUP), F32),
        V((2, 4, 4, 128, emb), BF),
        V((2, 4, 4, 128, emb), BF),
        V((4, 4, 128, emb), BF),
        V((2, 2, 128, emb), BF),
        V((2, 4, 128, emb), BF),
        V((4, 128, emb), BF),
        V((2, 64, emb), BF),
        V((2, 128, emb), BF),
        V((2, 4, 2, 4 * half, 256), BF),
        V((2, half, emb), BF),
        V((2, half, emb), BF),
        V((half, emb), F32),
        V((half, 128), F32),
        V((4, half, emb), BF),
        V((4 * half, emb), F32),
        V((4, half, emb), BF),
        V((2, half // 2, emb), BF),
        V((2, half, emb), BF),
        V((half, emb), BF),
        V((2, half, emb), BF),
        V((clips, width), BF),
        V((clips // GROUP, heads * GROUP), F32),
        V((clips // GROUP, heads * GROUP), F32),
        pltpu.SemaphoreType.DMA((11,)),
        pltpu.SemaphoreType.DMA((clips // GROUP,)),
        pltpu.SemaphoreType.DMA((copies,)),
        pltpu.SemaphoreType.DMA((copies,)),
    ]
    anywhere = pl.BlockSpec(memory_space=pl.ANY)
    smem = pl.BlockSpec(memory_space=pltpu.SMEM)
    value_part, score_grad, text_grad = pl.pallas_call(
        functools.partial(main_kernel, (clips, width, head, emb, all_clips)),
        out_shape=(
            jax.ShapeDtypeStruct((rows, width), BF),
            jax.ShapeDtypeStruct((rows, heads * GROUP), BF),
            jax.ShapeDtypeStruct((128, emb), F32),
        ),
        in_specs=[anywhere] * 5 + [smem] * 2,
        out_specs=(anywhere, anywhere, anywhere),
        scratch_shapes=scratch,
        compiler_params=pltpu.CompilerParams(
            collective_id=0, has_side_effects=True, vmem_limit_bytes=60 * 1024 * 1024
        ),
        name="pool_pair_back",
    )(frame_rows, key_t, value_weight, out_weight, texts, logit_scale, logit_bias)
    steps = 8
    grad_frames, grad_texts = pl.pallas_call(
        final_kernel,
        in_specs=[anywhere] * 5,
        out_specs=(anywhere, anywhere),
        out_shape=(
            jax.ShapeDtypeStruct((rows, width), BF),
            jax.ShapeDtypeStruct((128, emb), F32),
        ),
        scratch_shapes=[
            V((rows, width), BF),
            V((rows, heads * GROUP), BF),
            V((heads, width), BF),
            V((heads * GROUP, width), BF),
            V((128, emb), BF),
            V((128, emb), F32),
            V((128, emb), F32),
            pltpu.SemaphoreType.DMA((steps,)),
            pltpu.SemaphoreType.DMA((steps,)),
            pltpu.SemaphoreType.DMA((steps,)),
            pltpu.SemaphoreType.DMA((4,)),
        ],
        compiler_params=pltpu.CompilerParams(vmem_limit_bytes=60 * 1024 * 1024),
        name="frame_grads",
    )(value_part, score_grad, key_t, texts, text_grad)
    return (grad_frames.reshape(clips, frames_here, width), grad_texts)


def solution(mesh):
    in_specs = (P("clip", "tm", None), P(), P(), P(), P(("tm", "clip"), None), P(), P())
    out_specs = (P("clip", "tm", None), P(("tm", "clip"), None))
    return jax.shard_map(local, mesh=mesh, in_specs=in_specs, out_specs=out_specs, check_vma=False)
```

```python
import functools
import math

import jax
import jax.numpy as jnp
from jax import lax
from jax.experimental import pallas as pl
from jax.experimental.pallas import tpu as pltpu
from jax.sharding import PartitionSpec as P

EPSILON = 1e-06
MESH = pl.DeviceIdType.MESH
BF = jnp.bfloat16
F32 = jnp.float32
NT = (((1,), (1,)), ((), ()))
TN = (((0,), (0,)), ((), ()))
HEADS = 16
GROUP = 16


def nt(a, b):
    return lax.dot_general(a, b, NT, preferred_element_type=F32)


def tn(a, b):
    return lax.dot_general(a, b, TN, preferred_element_type=F32)


def nn(a, b):
    return jnp.dot(a, b, preferred_element_type=F32)


def own_clip_mask(rows_per_clip):
    shape = (GROUP * rows_per_clip, HEADS * GROUP)
    row = lax.broadcasted_iota(jnp.int32, shape, 0)
    lane = lax.broadcasted_iota(jnp.int32, shape, 1) & (GROUP - 1)
    start = lane * rows_per_clip
    return jnp.where((row >= start) & (row < start + rows_per_clip), 1.0, 0.0)


def repeat_heads(key_ref, out_ref):
    for h in range(HEADS):
        row = key_ref[h : h + 1, :].astype(F32)
        wide = jnp.broadcast_to(row, (GROUP, row.shape[1])).astype(BF)
        out_ref[h * GROUP : (h + 1) * GROUP, :] = wide


def main_kernel(
    dims,
    frames_hbm, key_hbm, value_hbm, out_hbm, texts_hbm, scale_ref, bias_ref,
    vp_hbm, sg_hbm, gt_hbm,
    key_ref, texts_ref, gt_ref,
    x_s, w_s, ow_s, key_s, pq_s, e_s, ms_send, ms_recv, alpha_s, acc_s, a_s, sg_s, t_s,
    tt_s, tg_s, rsib_s, r1_s, r2_s, tr_s, q1_s, q2_s, g_s,
    embp_s, embr_s, vu_s, vn_s, v_s, vg_s, vgb_s, g1_s, g2_s, eg_s, egr_s, pg_s, u_send, u_recv,
    load_sem, out_sem, send_sem, recv_sem,
):
    clips, width, head, emb, all_clips = dims
    frames_here = 8
    rows = clips * frames_here
    groups = clips // GROUP
    half_clips = clips // 2
    root = 1.0 / math.sqrt(width)

    tm = lax.axis_index("tm")
    ci = lax.axis_index("clip")
    core = lax.rem(ci, 2)
    y = lax.rem(ci // 2, 4)
    x = lax.rem(ci // 8, 4)
    z_lo = ci // 32
    z = tm * 2 + z_lo

    def at(xx, yy, zz, cc):
        return (zz // 2, ((lax.rem(zz, 2) * 4 + xx) * 4 + yy) * 2 + cc)

    def up(a, n):
        return lax.rem(a + n, 4)

    p1 = y * (1 - core) + x * core
    p2 = x * (1 - core) + y * core

    def plane(a1, a2):
        return at(a2 * (1 - core) + a1 * core, a1 * (1 - core) + a2 * core, z, core)

    n1p, n1m = plane(up(p1, 1), p2), plane(up(p1, 3), p2)
    n2p, n2m = plane(p1, up(p2, 1)), plane(p1, up(p2, 3))
    zp, zm = at(x, y, up(z, 1), core), at(x, y, up(z, 3), core)
    partner = (1 - tm, ci)
    sibling = at(x, y, z, 1 - core)

    counter = [0]

    def remote(src, dst, device):
        k = counter[0]
        counter[0] += 1
        return pltpu.make_async_remote_copy(
            src_ref=src, dst_ref=dst, send_sem=send_sem.at[k], recv_sem=recv_sem.at[k],
            device_id=device, device_id_type=MESH,
        )

    chunk = rows // 4
    loads = [
        pltpu.make_async_copy(
            frames_hbm.at[pl.ds(i * chunk, chunk)], x_s.at[pl.ds(i * chunk, chunk)], load_sem.at[i]
        )
        for i in range(4)
    ]
    load_w = pltpu.make_async_copy(value_hbm, w_s, load_sem.at[4])
    load_ow = pltpu.make_async_copy(out_hbm, ow_s, load_sem.at[5])
    load_key = pltpu.make_async_copy(key_hbm, key_ref, load_sem.at[6])
    load_texts = pltpu.make_async_copy(texts_hbm, texts_ref, load_sem.at[7])
    load_texts.start()
    load_key.start()
    for load in loads:
        load.start()
    load_w.start()
    load_ow.start()

    barrier = pltpu.get_barrier_semaphore()
    greet = (n1p, n1m, n2p, n2m, zp, zm, partner, sibling)
    for device in greet:
        pl.semaphore_signal(barrier, inc=1, device_id=device, device_id_type=MESH)

    load_texts.wait()
    text_full = texts_ref[...].astype(F32)
    text_norm = jnp.sqrt(jnp.sum(text_full * text_full, axis=1, keepdims=True) + EPSILON)
    tt_s[1, p2, p1] = (text_full / text_norm).astype(BF)
    load_key.wait()
    repeat_heads(key_ref, key_s)

    pl.semaphore_wait(barrier, len(greet))

    sent = []

    def go(*copies):
        for copy in copies:
            copy.start()
            sent.append(copy)

    own = tt_s.at[1]
    a0p = remote(own.at[p2, p1], own.at[p2, p1], n1p)
    a0m = remote(own.at[p2, p1], own.at[p2, p1], n1m)
    go(a0p, a0m)

    mask = own_clip_mask(frames_here)
    clip_mask = own_clip_mask(1)
    lanes = HEADS * GROUP

    def own_lane(per_clip):
        picked = per_clip.reshape(per_clip.shape[0] // GROUP, GROUP, lanes) * clip_mask[None]
        return jnp.sum(picked, axis=1)

    for i in range(4):
        loads[i].wait()
        part = pl.ds(i * chunk, chunk)
        s = nt(x_s[part, :], key_s[...]) * root
        s3 = s.reshape(chunk // frames_here, frames_here, lanes)
        top = jnp.max(s3, axis=1)
        e3 = jnp.exp(s3 - top[:, None, :])
        e_s[part, :] = e3.reshape(chunk, lanes)
        group_part = pl.ds(i * groups // 4, groups // 4)
        ms_send[0, group_part, :] = own_lane(top)
        ms_send[1, group_part, :] = own_lane(jnp.sum(e3, axis=1))
    ms = remote(ms_send, ms_recv, partner)
    go(ms)

    def a1():
        a0p.wait_recv()
        a0m.wait_recv()
        low, high = pl.ds(0, 64), pl.ds(64, 64)
        b1, b3 = up(p1, 3), up(p1, 1)
        cp = remote(own.at[p2, b1, low], own.at[p2, b1, low], n1p)
        cm = remote(own.at[p2, b3, high], own.at[p2, b3, high], n1m)
        go(cp, cm)
        return cp, cm

    def sib_row(row):
        copy = remote(own.at[row], tt_s.at[0, row], sibling)
        go(copy)
        return copy

    fwd1 = a1()

    columns = [slice(at, min(at + 256, width)) for at in range(0, width, 256)]

    def pool_group(g, carry):
        frame_part = pl.ds(pl.multiple_of(g * 128, 128), 128)
        clip_part = pl.ds(pl.multiple_of(g * GROUP, GROUP), GROUP)
        weight = jnp.transpose(e_s[frame_part, :] * mask).astype(BF)
        for cols in columns:
            pooled = nn(weight, x_s[frame_part, cols]).astype(BF)
            pq_s[:, clip_part, cols] = pooled.reshape(HEADS, GROUP, pooled.shape[1])
        return carry

    lax.fori_loop(0, groups // 2, pool_group, 0, unroll=8)

    for copy in fwd1:
        copy.wait_recv()
    row_p = remote(own.at[p2], own.at[p2], n2p)
    row_m = remote(own.at[p2], own.at[p2], n2m)
    go(row_p, row_m)
    sib0 = sib_row(p2)

    lax.fori_loop(groups // 2, groups, pool_group, 0, unroll=8)

    load_w.wait()
    load_ow.wait()
    acc_s[...] = jnp.zeros_like(acc_s)

    pairs = []
    for h in range(0, HEADS, 2):
        first = min(h * head // 128, width // 128 - 2) * 128
        wide = 256 if (h + 2) * head <= first + 256 else 384
        pairs.append((h, first, wide))

    def window_mask(h, first, wide):
        lane = lax.broadcasted_iota(jnp.int32, (1, wide), 1)
        offset = h * head - first
        return (lane >= offset) & (lane < offset + head)

    for h, first, wide in pairs:
        cols = slice(first, first + wide)
        part = nn(pq_s[h : h + 2].reshape(2 * clips, width), w_s[:, cols])
        acc_s[:, cols] += jnp.where(window_mask(h, first, wide), part[:clips], 0.0) + jnp.where(
            window_mask(h + 1, first, wide), part[clips:], 0.0
        )

    ms.wait_recv()
    mine, theirs = ms_send[0], ms_recv[0]
    top = jnp.maximum(mine, theirs)
    mine_f, theirs_f = jnp.exp(mine - top), jnp.exp(theirs - top)
    alpha = mine_f / (ms_send[1] * mine_f + ms_recv[1] * theirs_f)
    alpha_s[...] = alpha
    spread = (alpha[:, None, :] * clip_mask[None]).reshape(clips, lanes)
    head_start = (lax.broadcasted_iota(jnp.int32, (lanes, width), 0) // GROUP) * head
    head_lane = lax.broadcasted_iota(jnp.int32, (lanes, width), 1)
    in_head = (head_lane >= head_start) & (head_lane < head_start + head)
    pooled = (acc_s[...] * nn(spread.astype(BF), jnp.where(in_head, 1.0, 0.0).astype(BF))).astype(BF)
    embp_s[...] = nn(pooled, ow_s[...]).astype(BF).reshape(2, half_clips, emb)
    er_p = remote(embp_s.at[up(z, 1) // 2], embr_s.at[0], zp)
    er_m = remote(embp_s.at[up(z, 3) // 2], embr_s.at[1], zm)
    go(er_p, er_m)

    row_p.wait_recv()
    row_m.wait_recv()
    r1, r3 = up(p2, 3), up(p2, 1)
    low, high = pl.ds(0, 2), pl.ds(2, 2)
    fwd_p = remote(own.at[r1, low], own.at[r1, low], n2p)
    fwd_m = remote(own.at[r3, high], own.at[r3, high], n2m)
    go(fwd_p, fwd_m)
    sib1 = sib_row(r3)
    sib2 = sib_row(r1)

    def weights(g, carry):
        frame_part = pl.ds(pl.multiple_of(g * 128, 128), 128)
        wide = e_s[frame_part, :] * mask * alpha_s[pl.ds(g, 1), :]
        e_s[frame_part, :] = wide
        a_s[frame_part, :] = wide.astype(BF)
        return carry

    lax.fori_loop(0, groups // 2, weights, 0, unroll=4)

    er_p.wait_recv()
    er_m.wait_recv()
    embedding = embr_s[0].astype(F32) + embr_s[1].astype(F32)
    vis_norm = jnp.sqrt(jnp.sum(embedding * embedding, axis=1, keepdims=True) + EPSILON)
    vis_unit = embedding / vis_norm
    vu_s[...] = vis_unit
    vn_s[...] = jnp.broadcast_to(vis_norm, vn_s.shape)
    v_s[z] = vis_unit.astype(BF)
    hlow, hhigh = pl.ds(0, half_clips // 2), pl.ds(half_clips // 2, half_clips // 2)

    def send_vis(at_z, half, device):
        copy = remote(v_s.at[at_z, half], v_s.at[at_z, half], device)
        go(copy)
        return copy

    v_first = send_vis(z, hlow, zp), send_vis(z, hhigh, zm)
    v_second = send_vis(z, hhigh, zp), send_vis(z, hlow, zm)
    lax.fori_loop(groups // 2, groups, weights, 0, unroll=4)
    z1, z2, z3 = up(z, 1), up(z, 2), up(z, 3)
    for copy in v_first:
        copy.wait_recv()
    v_far = send_vis(z3, hlow, zp), send_vis(z1, hhigh, zm)

    fwd_p.wait_recv()
    fwd_m.wait_recv()
    sib3 = sib_row(up(p2, 2))
    for copy in v_second + v_far:
        copy.wait_recv()

    vg_s[...] = jnp.zeros_like(vg_s)
    slope = 0.5 * scale_ref[0]
    shift = 0.5 * bias_ref[0]
    diff = lax.broadcasted_iota(jnp.int32, (128, 128), 0) - lax.broadcasted_iota(
        jnp.int32, (128, 128), 1
    )
    vis_base = [
        (((1 - zz % 2) * 4 + x) * 4 + y) * 2 * clips + core * clips + (zz // 2) * half_clips
        for zz in range(4)
    ]

    def text_base(whose, a2, a1):
        c = core * whose + (1 - core) * (1 - whose)
        xx = a2 * (1 - c) + a1 * c
        yy = a1 * (1 - c) + a2 * c
        return (tm * 64 + ((z_lo * 4 + xx) * 4 + yy) * 2 + c) * 128

    def pair_row(whose, row):
        vis = v_s[...].reshape(4 * half_clips, emb)
        total = None
        for hh in range(2):
            texts = tt_s[whose, row, pl.ds(2 * hh, 2)].reshape(256, emb)
            curve = jnp.tanh(nt(vis, texts) * slope + shift) * 0.5
            tall = []
            for zz in range(4):
                wide = []
                for b in range(2):
                    gap = text_base(whose, row, 2 * hh + b) - vis_base[zz]
                    block = curve[zz * 128 : (zz + 1) * 128, b * 128 : (b + 1) * 128]
                    wide.append(block + jnp.where(diff == gap, -0.5, 0.5))
                tall.append(jnp.concatenate(wide, axis=1))
            grad = jnp.concatenate(tall, axis=0).astype(BF)
            g_s[whose, row, hh] = grad
            part = nn(grad, texts)
            total = part if total is None else total + part
        vg_s[...] += total

    def pair_rows(whose):
        def body(row, carry):
            pair_row(whose, row)
            return carry

        lax.fori_loop(0, 4, body, 0)

    pair_rows(1)
    for copy in (sib0, sib1, sib2, sib3):
        copy.wait_recv()
    pair_rows(0)

    vgb_s[...] = vg_s[...].astype(BF).reshape(4, half_clips, emb)
    g1p = remote(vgb_s.at[z2, hlow], g1_s.at[0], zp)
    g1m = remote(vgb_s.at[z2, hhigh], g1_s.at[1], zm)
    g2p = remote(vgb_s.at[z1, hhigh], g2_s.at[0, hhigh], zp)
    g2m = remote(vgb_s.at[z3, hlow], g2_s.at[1, hlow], zm)
    go(g1p, g1m, g2p, g2m)

    sib_base = counter[0]
    counter[0] += 4

    def sib_copy(rr, row):
        return pltpu.make_async_remote_copy(
            src_ref=tg_s.at[0, row], dst_ref=rsib_s.at[row],
            send_sem=send_sem.at[sib_base + rr], recv_sem=recv_sem.at[sib_base + rr],
            device_id=sibling, device_id_type=MESH,
        )

    def ordered(p, rr):
        return lax.rem(p + 2 + 3 * rr + 3 * (rr // 2) + 2 * (rr // 3), 4)

    def text_terms(whose, row):
        vis = v_s[...].reshape(4 * half_clips, emb)
        grad = jnp.concatenate([g_s[whose, row, 0], g_s[whose, row, 1]], axis=1)
        return tn(grad, vis).reshape(4, 128, emb)

    def sib_rows(rr, carry):
        row = ordered(p1, rr)
        tg_s[0, row] = text_terms(0, row).astype(BF)
        return carry

    lax.fori_loop(0, 4, sib_rows, 0)

    g1p.wait_recv()
    g1m.wait_recv()
    vgb_s[z1, hlow] = (vgb_s[z1, hlow].astype(F32) + g1_s[0].astype(F32)).astype(BF)
    g3p = remote(vgb_s.at[z1, hlow], g2_s.at[0, hlow], zp)
    vgb_s[z3, hhigh] = (vgb_s[z3, hhigh].astype(F32) + g1_s[1].astype(F32)).astype(BF)
    g3m = remote(vgb_s.at[z3, hhigh], g2_s.at[1, hhigh], zm)
    go(g3p, g3m)

    def sib_send(rr, carry):
        sib_copy(rr, ordered(p1, rr)).start()
        return carry

    lax.fori_loop(0, 4, sib_send, 0)

    def own_rows(row, carry):
        tg_s[1, row] = text_terms(1, row).astype(BF)
        return carry

    lax.fori_loop(0, 4, own_rows, 0)

    for copy in (g2p, g2m, g3p, g3m):
        copy.wait_recv()
    out_scale = scale_ref[0] * (1.0 / all_clips)
    vis_grad = (
        vg_s[pl.ds(pl.multiple_of(z * half_clips, 128), half_clips), :]
        + g2_s[0].astype(F32)
        + g2_s[1].astype(F32)
    ) * out_scale
    unit = vu_s[...]
    inner = jnp.sum(vis_grad * unit, axis=1, keepdims=True)
    eg_s[...] = ((vis_grad - unit * inner) / vn_s[:, :1]).astype(BF)
    eg_p = remote(eg_s, egr_s.at[tm], zp)
    eg_m = remote(eg_s, egr_s.at[tm], zm)
    go(eg_p, eg_m)

    def add_sibling(rr, carry):
        row = ordered(p2, rr)
        sib_copy(rr, row).wait_recv()
        tg_s[1, row] = (tg_s[1, row].astype(F32) + rsib_s[row].astype(F32)).astype(BF)
        return carry

    tg = tg_s.at[1]
    lax.fori_loop(0, 1, add_sibling, 0)
    s1p = remote(tg.at[up(p2, 2), low], r1_s.at[0], n2p)
    s1m = remote(tg.at[up(p2, 2), high], r1_s.at[1], n2m)
    go(s1p, s1m)
    lax.fori_loop(1, 3, add_sibling, 0)
    s2p = remote(tg.at[r3, high], r2_s.at[0, high], n2p)
    s2m = remote(tg.at[r1, low], r2_s.at[1, low], n2m)
    go(s2p, s2m)
    lax.fori_loop(3, 4, add_sibling, 0)
    eg_p.wait_recv()
    eg_m.wait_recv()
    pg_s[...] = nt(egr_s[...].reshape(clips, emb), ow_s[...]).astype(BF)

    for h, first, wide in pairs:
        if h == HEADS // 2:
            s1p.wait_recv()
            s1m.wait_recv()
            tg_s[1, r3, low] = (tg_s[1, r3, low].astype(F32) + r1_s[0].astype(F32)).astype(BF)
            s3p = remote(tg.at[r3, low], r2_s.at[0, low], n2p)
            go(s3p)
            tg_s[1, r1, high] = (tg_s[1, r1, high].astype(F32) + r1_s[1].astype(F32)).astype(BF)
            s3m = remote(tg.at[r1, high], r2_s.at[1, high], n2m)
            go(s3m)

        grads = pg_s[:, first : first + wide].astype(F32)
        part = jnp.concatenate(
            [jnp.where(window_mask(h + i, first, wide), grads, 0.0).astype(BF) for i in range(2)],
            axis=0,
        )
        for cols in columns:
            q = nt(part, w_s[cols, first : first + wide]).astype(BF)
            pq_s[h : h + 2, :, cols] = q.reshape(2, clips, q.shape[1])

    def score_terms(g, carry):
        frame_part = pl.ds(pl.multiple_of(g * 128, 128), 128)
        clip_part = pl.ds(pl.multiple_of(g * GROUP, GROUP), GROUP)
        q = pq_s[:, clip_part, :].reshape(lanes, width)
        prod = jnp.transpose(nt(q, x_s[frame_part, :]))
        t_s[frame_part, :] = prod
        u_send[pl.ds(g, 1), :] = jnp.sum(prod * e_s[frame_part, :], axis=0, keepdims=True)
        return carry

    lax.fori_loop(0, groups, score_terms, 0, unroll=8)
    uc = remote(u_send, u_recv, partner)
    uc.start()

    def vp_copy(g):
        frame_part = pl.ds(pl.multiple_of(g * 128, 128), 128)
        return pltpu.make_async_copy(
            x_s.at[frame_part], vp_hbm.at[frame_part], out_sem.at[g]
        )

    def value_part(g, carry):
        frame_part = pl.ds(pl.multiple_of(g * 128, 128), 128)
        clip_part = pl.ds(pl.multiple_of(g * GROUP, GROUP), GROUP)
        for cols in columns:
            q = pq_s[:, clip_part, cols]
            q = q.reshape(lanes, q.shape[2])
            x_s[frame_part, cols] = nn(a_s[frame_part, :], q).astype(BF)
        vp_copy(g).start()
        return carry

    lax.fori_loop(0, groups // 4, value_part, 0, unroll=4)

    for copy in (s2p, s2m, s3p, s3m):
        copy.wait_recv()
    for b in range(4):
        total = tg_s[1, p2, b].astype(F32) + r2_s[0, b].astype(F32) + r2_s[1, b].astype(F32)
        tr_s[b] = total.astype(BF)
    b1, b2, b3 = up(p1, 1), up(p1, 2), up(p1, 3)
    tlow, thigh = pl.ds(0, 64), pl.ds(64, 64)
    u1p = remote(tr_s.at[b2, tlow], q1_s.at[0], n1p)
    u1m = remote(tr_s.at[b2, thigh], q1_s.at[1], n1m)
    u2p = remote(tr_s.at[b1, thigh], q2_s.at[0, thigh], n1p)
    u2m = remote(tr_s.at[b3, tlow], q2_s.at[1, tlow], n1m)
    go(u1p, u1m, u2p, u2m)

    lax.fori_loop(groups // 4, 3 * groups // 4, value_part, 0, unroll=8)
    u1p.wait_recv()
    u1m.wait_recv()
    tr_s[b1, tlow] = (tr_s[b1, tlow].astype(F32) + q1_s[0].astype(F32)).astype(BF)
    u3p = remote(tr_s.at[b1, tlow], q2_s.at[0, tlow], n1p)
    tr_s[b3, thigh] = (tr_s[b3, thigh].astype(F32) + q1_s[1].astype(F32)).astype(BF)
    u3m = remote(tr_s.at[b3, thigh], q2_s.at[1, thigh], n1m)
    go(u3p, u3m)

    lax.fori_loop(3 * groups // 4, groups, value_part, 0, unroll=4)

    uc.wait()
    u_send[...] = u_send[...] + u_recv[...]

    def score_grads(g, carry):
        frame_part = pl.ds(pl.multiple_of(g * 128, 128), 128)
        centred = t_s[frame_part, :] - u_send[pl.ds(g, 1), :]
        sg_s[frame_part, :] = (e_s[frame_part, :] * centred * root).astype(BF)
        return carry

    sg_out = []
    for i in range(2):
        lax.fori_loop(i * groups // 2, (i + 1) * groups // 2, score_grads, 0, unroll=4)
        part = pl.ds(i * rows // 2, rows // 2)
        sg_out.append(pltpu.make_async_copy(sg_s.at[part], sg_hbm.at[part], load_sem.at[9 + i]))
        sg_out[i].start()

    for copy in (u2p, u2m, u3p, u3m):
        copy.wait_recv()
    gt_ref[...] = (
        tr_s[p1].astype(F32) + q2_s[0].astype(F32) + q2_s[1].astype(F32)
    ) * out_scale
    gt_out = pltpu.make_async_copy(gt_ref, gt_hbm, load_sem.at[8])
    gt_out.start()

    for copy in sent:
        copy.wait_send()

    def drain(rr, carry):
        sib_copy(rr, ordered(p1, rr)).wait_send()
        return carry

    lax.fori_loop(0, 4, drain, 0)

    def drain_vp(g, carry):
        vp_copy(g).wait()
        return carry

    lax.fori_loop(0, groups, drain_vp, 0)
    for copy in sg_out:
        copy.wait()
    gt_out.wait()


def final_kernel(
    vp_hbm, sg_hbm, key_hbm, texts_hbm, tg_hbm, out_hbm, gt_hbm,
    vp_s, sg_s, key_in, key_s, texts_s, tg_s, gt_s, vp_sem, sg_sem, out_sem, small_sem,
):
    rows, width = vp_s.shape
    steps = 8
    step = rows // steps
    parts = [pl.ds(i * step, step) for i in range(steps)]
    load_key = pltpu.make_async_copy(key_hbm, key_in, small_sem.at[0])
    load_texts = pltpu.make_async_copy(texts_hbm, texts_s, small_sem.at[1])
    load_tg = pltpu.make_async_copy(tg_hbm, tg_s, small_sem.at[2])
    load_key.start()
    load_vp, load_sg, outs = [], [], []
    for i, part in enumerate(parts):
        load_sg.append(pltpu.make_async_copy(sg_hbm.at[part], sg_s.at[part], sg_sem.at[i]))
        load_vp.append(pltpu.make_async_copy(vp_hbm.at[part], vp_s.at[part], vp_sem.at[i]))
        outs.append(pltpu.make_async_copy(vp_s.at[part], out_hbm.at[part], out_sem.at[i]))
        load_sg[i].start()
        load_vp[i].start()
        if i == 1:
            load_texts.start()
            load_tg.start()
    load_key.wait()
    repeat_heads(key_in, key_s)
    for i, part in enumerate(parts):
        load_sg[i].wait()
        load_vp[i].wait()
        for start in range(0, width, 256):
            cols = slice(start, min(start + 256, width))
            total = vp_s[part, cols].astype(F32) + nn(sg_s[part, :], key_s[:, cols])
            vp_s[part, cols] = total.astype(BF)
        outs[i].start()
        if i == 2:
            load_texts.wait()
            load_tg.wait()
            text_full = texts_s[...].astype(F32)
            text_norm = jnp.sqrt(jnp.sum(text_full * text_full, axis=1, keepdims=True) + EPSILON)
            text_unit = text_full / text_norm
            text_grad = tg_s[...]
            inner = jnp.sum(text_grad * text_unit, axis=1, keepdims=True)
            gt_s[...] = (text_grad - text_unit * inner) / text_norm
            gt_out = pltpu.make_async_copy(gt_s, gt_hbm, small_sem.at[3])
            gt_out.start()
    for copy in outs:
        copy.wait()
    gt_out.wait()


def local(frames, key_proj, value_weight, out_weight, texts, logit_scale, logit_bias):
    clips, frames_here, width = frames.shape
    heads = key_proj.shape[1]
    head = width // heads
    emb = out_weight.shape[1]
    all_clips = clips * lax.axis_size("clip")
    rows = clips * frames_here
    half = clips // 2
    frame_rows = frames.reshape(rows, width)
    key_t = key_proj.T
    V = pltpu.VMEM
    copies = 48
    scratch = [
        V((heads, width), BF),
        V((128, emb), BF),
        V((128, emb), F32),
        V((rows, width), BF),
        V((width, width), BF),
        V((width, emb), BF),
        V((heads * GROUP, width), BF),
        V((heads, clips, width), BF),
        V((rows, heads * GROUP), F32),
        V((2, clips // GROUP, heads * GROUP), F32),
        V((2, clips // GROUP, heads * GROUP), F32),
        V((clips // GROUP, heads * GROUP), F32),
        V((clips, width), F32),
        V((rows, heads * GROUP), BF),
        V((rows, heads * GROUP), BF),
        V((rows, heads * GROUP), F32),
        V((2, 4, 4, 128, emb), BF),
        V((2, 4, 4, 128, emb), BF),
        V((4, 4, 128, emb), BF),
        V((2, 2, 128, emb), BF),
        V((2, 4, 128, emb), BF),
        V((4, 128, emb), BF),
        V((2, 64, emb), BF),
        V((2, 128, emb), BF),
        V((2, 4, 2, 4 * half, 256), BF),
        V((2, half, emb), BF),
        V((2, half, emb), BF),
        V((half, emb), F32),
        V((half, 128), F32),
        V((4, half, emb), BF),
        V((4 * half, emb), F32),
        V((4, half, emb), BF),
        V((2, half // 2, emb), BF),
        V((2, half, emb), BF),
        V((half, emb), BF),
        V((2, half, emb), BF),
        V((clips, width), BF),
        V((clips // GROUP, heads * GROUP), F32),
        V((clips // GROUP, heads * GROUP), F32),
        pltpu.SemaphoreType.DMA((11,)),
        pltpu.SemaphoreType.DMA((clips // GROUP,)),
        pltpu.SemaphoreType.DMA((copies,)),
        pltpu.SemaphoreType.DMA((copies,)),
    ]
    anywhere = pl.BlockSpec(memory_space=pl.ANY)
    smem = pl.BlockSpec(memory_space=pltpu.SMEM)
    value_part, score_grad, text_grad = pl.pallas_call(
        functools.partial(main_kernel, (clips, width, head, emb, all_clips)),
        out_shape=(
            jax.ShapeDtypeStruct((rows, width), BF),
            jax.ShapeDtypeStruct((rows, heads * GROUP), BF),
            jax.ShapeDtypeStruct((128, emb), F32),
        ),
        in_specs=[anywhere] * 5 + [smem] * 2,
        out_specs=(anywhere, anywhere, anywhere),
        scratch_shapes=scratch,
        compiler_params=pltpu.CompilerParams(
            collective_id=0, has_side_effects=True, vmem_limit_bytes=60 * 1024 * 1024
        ),
        name="pool_pair_back",
    )(frame_rows, key_t, value_weight, out_weight, texts, logit_scale, logit_bias)
    steps = 8
    grad_frames, grad_texts = pl.pallas_call(
        final_kernel,
        in_specs=[anywhere] * 5,
        out_specs=(anywhere, anywhere),
        out_shape=(
            jax.ShapeDtypeStruct((rows, width), BF),
            jax.ShapeDtypeStruct((128, emb), F32),
        ),
        scratch_shapes=[
            V((rows, width), BF),
            V((rows, heads * GROUP), BF),
            V((heads, width), BF),
            V((heads * GROUP, width), BF),
            V((128, emb), BF),
            V((128, emb), F32),
            V((128, emb), F32),
            pltpu.SemaphoreType.DMA((steps,)),
            pltpu.SemaphoreType.DMA((steps,)),
            pltpu.SemaphoreType.DMA((steps,)),
            pltpu.SemaphoreType.DMA((4,)),
        ],
        compiler_params=pltpu.CompilerParams(vmem_limit_bytes=60 * 1024 * 1024),
        name="frame_grads",
    )(value_part, score_grad, key_t, texts, text_grad)
    return (grad_frames.reshape(clips, frames_here, width), grad_texts)


def solution(mesh):
    in_specs = (P("clip", "tm", None), P(), P(), P(), P(("tm", "clip"), None), P(), P())
    out_specs = (P("clip", "tm", None), P(("tm", "clip"), None))
    return jax.shard_map(local, mesh=mesh, in_specs=in_specs, out_specs=out_specs, check_vma=False)
```

```python
import functools
import math

import jax
import jax.numpy as jnp
from jax import lax
from jax.experimental import pallas as pl
from jax.experimental.pallas import tpu as pltpu
from jax.sharding import PartitionSpec as P

EPSILON = 1e-06
MESH = pl.DeviceIdType.MESH
BF = jnp.bfloat16
F32 = jnp.float32
NT = (((1,), (1,)), ((), ()))
TN = (((0,), (0,)), ((), ()))
HEADS = 16
GROUP = 16


def nt(a, b):
    return lax.dot_general(a, b, NT, preferred_element_type=F32)


def tn(a, b):
    return lax.dot_general(a, b, TN, preferred_element_type=F32)


def nn(a, b):
    return jnp.dot(a, b, preferred_element_type=F32)


def own_clip_mask(rows_per_clip):
    shape = (GROUP * rows_per_clip, HEADS * GROUP)
    row = lax.broadcasted_iota(jnp.int32, shape, 0)
    lane = lax.broadcasted_iota(jnp.int32, shape, 1) & (GROUP - 1)
    start = lane * rows_per_clip
    return jnp.where((row >= start) & (row < start + rows_per_clip), 1.0, 0.0)


def repeat_heads(key_ref, out_ref):
    for h in range(HEADS):
        row = key_ref[h : h + 1, :].astype(F32)
        wide = jnp.broadcast_to(row, (GROUP, row.shape[1])).astype(BF)
        out_ref[h * GROUP : (h + 1) * GROUP, :] = wide


def main_kernel(
    dims,
    frames_hbm, key_hbm, value_hbm, out_hbm, texts_hbm, scale_ref, bias_ref,
    vp_hbm, sg_hbm, gt_hbm,
    key_ref, texts_ref, gt_ref,
    x_s, w_s, ow_s, key_s, pq_s, e_s, ms_send, ms_recv, alpha_s, acc_s, a_s, sg_s, t_s,
    tt_s, tg_s, rsib_s, r1_s, r2_s, tr_s, q1_s, q2_s, g_s,
    embp_s, embr_s, vu_s, vn_s, v_s, vg_s, vgb_s, g1_s, g2_s, eg_s, egr_s, pg_s, u_send, u_recv,
    load_sem, out_sem, send_sem, recv_sem,
):
    clips, width, head, emb, all_clips = dims
    frames_here = 8
    rows = clips * frames_here
    groups = clips // GROUP
    half_clips = clips // 2
    root = 1.0 / math.sqrt(width)

    tm = lax.axis_index("tm")
    ci = lax.axis_index("clip")
    core = lax.rem(ci, 2)
    y = lax.rem(ci // 2, 4)
    x = lax.rem(ci // 8, 4)
    z_lo = ci // 32
    z = tm * 2 + z_lo

    def at(xx, yy, zz, cc):
        return (zz // 2, ((lax.rem(zz, 2) * 4 + xx) * 4 + yy) * 2 + cc)

    def up(a, n):
        return lax.rem(a + n, 4)

    p1 = y * (1 - core) + x * core
    p2 = x * (1 - core) + y * core

    def plane(a1, a2):
        return at(a2 * (1 - core) + a1 * core, a1 * (1 - core) + a2 * core, z, core)

    n1p, n1m = plane(up(p1, 1), p2), plane(up(p1, 3), p2)
    n2p, n2m = plane(p1, up(p2, 1)), plane(p1, up(p2, 3))
    z1, z2, z3 = up(z, 1 + 2 * core), up(z, 2), up(z, 3 - 2 * core)
    zp, zm = at(x, y, z1, core), at(x, y, z3, core)
    partner = (1 - tm, ci)
    sibling = at(x, y, z, 1 - core)

    counter = [0]

    def remote(src, dst, device):
        k = counter[0]
        counter[0] += 1
        return pltpu.make_async_remote_copy(
            src_ref=src, dst_ref=dst, send_sem=send_sem.at[k], recv_sem=recv_sem.at[k],
            device_id=device, device_id_type=MESH,
        )

    chunk = rows // 4
    loads = [
        pltpu.make_async_copy(
            frames_hbm.at[pl.ds(i * chunk, chunk)], x_s.at[pl.ds(i * chunk, chunk)], load_sem.at[i]
        )
        for i in range(4)
    ]
    load_w = pltpu.make_async_copy(value_hbm, w_s, load_sem.at[4])
    load_ow = pltpu.make_async_copy(out_hbm, ow_s, load_sem.at[5])
    load_key = pltpu.make_async_copy(key_hbm, key_ref, load_sem.at[6])
    load_texts = pltpu.make_async_copy(texts_hbm, texts_ref, load_sem.at[7])
    load_texts.start()
    load_key.start()
    for load in loads:
        load.start()
    load_w.start()
    load_ow.start()

    barrier = pltpu.get_barrier_semaphore()
    greet = (n1p, n1m, n2p, n2m, zp, zm, partner, sibling)
    for device in greet:
        pl.semaphore_signal(barrier, inc=1, device_id=device, device_id_type=MESH)

    load_texts.wait()
    text_full = texts_ref[...].astype(F32)
    text_norm = jnp.sqrt(jnp.sum(text_full * text_full, axis=1, keepdims=True) + EPSILON)
    tt_s[1, p2, p1] = (text_full / text_norm).astype(BF)
    load_key.wait()
    repeat_heads(key_ref, key_s)

    pl.semaphore_wait(barrier, len(greet))

    sent = []

    def go(*copies):
        for copy in copies:
            copy.start()
            sent.append(copy)

    own = tt_s.at[1]
    a0p = remote(own.at[p2, p1], own.at[p2, p1], n1p)
    a0m = remote(own.at[p2, p1], own.at[p2, p1], n1m)
    go(a0p, a0m)

    mask = own_clip_mask(frames_here)
    clip_mask = own_clip_mask(1)
    lanes = HEADS * GROUP

    def own_lane(per_clip):
        picked = per_clip.reshape(per_clip.shape[0] // GROUP, GROUP, lanes) * clip_mask[None]
        return jnp.sum(picked, axis=1)

    for i in range(4):
        loads[i].wait()
        part = pl.ds(i * chunk, chunk)
        s = nt(x_s[part, :], key_s[...]) * root
        s3 = s.reshape(chunk // frames_here, frames_here, lanes)
        top = jnp.max(s3, axis=1)
        e3 = jnp.exp(s3 - top[:, None, :])
        e_s[part, :] = e3.reshape(chunk, lanes)
        group_part = pl.ds(i * groups // 4, groups // 4)
        ms_send[0, group_part, :] = own_lane(top)
        ms_send[1, group_part, :] = own_lane(jnp.sum(e3, axis=1))
    ms = remote(ms_send, ms_recv, partner)
    go(ms)

    def a1():
        a0p.wait_recv()
        a0m.wait_recv()
        low, high = pl.ds(0, 64), pl.ds(64, 64)
        b1, b3 = up(p1, 3), up(p1, 1)
        cp = remote(own.at[p2, b1, low], own.at[p2, b1, low], n1p)
        cm = remote(own.at[p2, b3, high], own.at[p2, b3, high], n1m)
        go(cp, cm)
        return cp, cm

    def sib_row(row):
        copy = remote(own.at[row], tt_s.at[0, row], sibling)
        go(copy)
        return copy

    fwd1 = a1()

    columns = [slice(at, min(at + 256, width)) for at in range(0, width, 256)]

    def pool_group(g, carry):
        frame_part = pl.ds(pl.multiple_of(g * 128, 128), 128)
        clip_part = pl.ds(pl.multiple_of(g * GROUP, GROUP), GROUP)
        weight = jnp.transpose(e_s[frame_part, :] * mask).astype(BF)
        for cols in columns:
            pooled = nn(weight, x_s[frame_part, cols]).astype(BF)
            pq_s[:, clip_part, cols] = pooled.reshape(HEADS, GROUP, pooled.shape[1])
        return carry

    lax.fori_loop(0, groups // 2, pool_group, 0, unroll=8)

    for copy in fwd1:
        copy.wait_recv()
    row_p = remote(own.at[p2], own.at[p2], n2p)
    row_m = remote(own.at[p2], own.at[p2], n2m)
    go(row_p, row_m)
    sib0 = sib_row(p2)

    lax.fori_loop(groups // 2, groups, pool_group, 0, unroll=8)

    load_w.wait()
    load_ow.wait()
    acc_s[...] = jnp.zeros_like(acc_s)

    pairs = []
    for h in range(0, HEADS, 2):
        first = min(h * head // 128, width // 128 - 2) * 128
        wide = 256 if (h + 2) * head <= first + 256 else 384
        pairs.append((h, first, wide))

    def window_mask(h, first, wide):
        lane = lax.broadcasted_iota(jnp.int32, (1, wide), 1)
        offset = h * head - first
        return (lane >= offset) & (lane < offset + head)

    for h, first, wide in pairs:
        cols = slice(first, first + wide)
        part = nn(pq_s[h : h + 2].reshape(2 * clips, width), w_s[:, cols])
        acc_s[:, cols] += jnp.where(window_mask(h, first, wide), part[:clips], 0.0) + jnp.where(
            window_mask(h + 1, first, wide), part[clips:], 0.0
        )

    ms.wait_recv()
    mine, theirs = ms_send[0], ms_recv[0]
    top = jnp.maximum(mine, theirs)
    mine_f, theirs_f = jnp.exp(mine - top), jnp.exp(theirs - top)
    alpha = mine_f / (ms_send[1] * mine_f + ms_recv[1] * theirs_f)
    alpha_s[...] = alpha
    spread = (alpha[:, None, :] * clip_mask[None]).reshape(clips, lanes)
    head_start = (lax.broadcasted_iota(jnp.int32, (lanes, width), 0) // GROUP) * head
    head_lane = lax.broadcasted_iota(jnp.int32, (lanes, width), 1)
    in_head = (head_lane >= head_start) & (head_lane < head_start + head)
    pooled = (acc_s[...] * nn(spread.astype(BF), jnp.where(in_head, 1.0, 0.0).astype(BF))).astype(BF)
    embp_s[...] = nn(pooled, ow_s[...]).astype(BF).reshape(2, half_clips, emb)
    er_p = remote(embp_s.at[z1 // 2], embr_s.at[0], zp)
    er_m = remote(embp_s.at[z3 // 2], embr_s.at[1], zm)
    go(er_p, er_m)

    row_p.wait_recv()
    row_m.wait_recv()
    r1, r3 = up(p2, 3), up(p2, 1)
    low, high = pl.ds(0, 2), pl.ds(2, 2)
    fwd_p = remote(own.at[r1, low], own.at[r1, low], n2p)
    fwd_m = remote(own.at[r3, high], own.at[r3, high], n2m)
    go(fwd_p, fwd_m)
    sib1 = sib_row(r3)
    sib2 = sib_row(r1)

    def weights(g, carry):
        frame_part = pl.ds(pl.multiple_of(g * 128, 128), 128)
        wide = e_s[frame_part, :] * mask * alpha_s[pl.ds(g, 1), :]
        e_s[frame_part, :] = wide
        a_s[frame_part, :] = wide.astype(BF)
        return carry

    lax.fori_loop(0, groups // 2, weights, 0, unroll=4)

    er_p.wait_recv()
    er_m.wait_recv()
    embedding = embr_s[0].astype(F32) + embr_s[1].astype(F32)
    vis_norm = jnp.sqrt(jnp.sum(embedding * embedding, axis=1, keepdims=True) + EPSILON)
    vis_unit = embedding / vis_norm
    vu_s[...] = vis_unit
    vn_s[...] = jnp.broadcast_to(vis_norm, vn_s.shape)
    v_s[z] = vis_unit.astype(BF)
    hlow, hhigh = pl.ds(0, half_clips // 2), pl.ds(half_clips // 2, half_clips // 2)

    def send_vis(at_z, half, device):
        copy = remote(v_s.at[at_z, half], v_s.at[at_z, half], device)
        go(copy)
        return copy

    v_first = send_vis(z, hlow, zp), send_vis(z, hhigh, zm)
    v_second = send_vis(z, hhigh, zp), send_vis(z, hlow, zm)
    lax.fori_loop(groups // 2, groups, weights, 0, unroll=4)
    for copy in v_first:
        copy.wait_recv()
    v_far = send_vis(z3, hlow, zp), send_vis(z1, hhigh, zm)

    fwd_p.wait_recv()
    fwd_m.wait_recv()
    sib3 = sib_row(up(p2, 2))
    for copy in v_second + v_far:
        copy.wait_recv()

    vg_s[...] = jnp.zeros_like(vg_s)
    slope = 0.5 * scale_ref[0]
    shift = 0.5 * bias_ref[0]
    diff = lax.broadcasted_iota(jnp.int32, (128, 128), 0) - lax.broadcasted_iota(
        jnp.int32, (128, 128), 1
    )
    vis_base = [
        (((1 - zz % 2) * 4 + x) * 4 + y) * 2 * clips + core * clips + (zz // 2) * half_clips
        for zz in range(4)
    ]

    def text_base(whose, a2, a1):
        c = core * whose + (1 - core) * (1 - whose)
        xx = a2 * (1 - c) + a1 * c
        yy = a1 * (1 - c) + a2 * c
        return (tm * 64 + ((z_lo * 4 + xx) * 4 + yy) * 2 + c) * 128

    def pair_row(whose, row):
        vis = v_s[...].reshape(4 * half_clips, emb)
        total = None
        for hh in range(2):
            texts = tt_s[whose, row, pl.ds(2 * hh, 2)].reshape(256, emb)
            curve = jnp.tanh(nt(vis, texts) * slope + shift) * 0.5
            tall = []
            for zz in range(4):
                wide = []
                for b in range(2):
                    gap = text_base(whose, row, 2 * hh + b) - vis_base[zz]
                    block = curve[zz * 128 : (zz + 1) * 128, b * 128 : (b + 1) * 128]
                    wide.append(block + jnp.where(diff == gap, -0.5, 0.5))
                tall.append(jnp.concatenate(wide, axis=1))
            grad = jnp.concatenate(tall, axis=0).astype(BF)
            g_s[whose, row, hh] = grad
            part = nn(grad, texts)
            total = part if total is None else total + part
        vg_s[...] += total

    def pair_rows(whose):
        def body(row, carry):
            pair_row(whose, row)
            return carry

        lax.fori_loop(0, 4, body, 0, unroll=2)

    pair_rows(1)
    for copy in (sib0, sib1, sib2, sib3):
        copy.wait_recv()
    pair_rows(0)

    vgb_s[...] = vg_s[...].astype(BF).reshape(4, half_clips, emb)
    g1p = remote(vgb_s.at[z2, hlow], g1_s.at[0], zp)
    g1m = remote(vgb_s.at[z2, hhigh], g1_s.at[1], zm)
    g2p = remote(vgb_s.at[z1, hhigh], g2_s.at[0, hhigh], zp)
    g2m = remote(vgb_s.at[z3, hlow], g2_s.at[1, hlow], zm)
    go(g1p, g1m, g2p, g2m)

    sib_base = counter[0]
    counter[0] += 4

    def sib_copy(rr, row):
        return pltpu.make_async_remote_copy(
            src_ref=tg_s.at[0, row], dst_ref=rsib_s.at[row],
            send_sem=send_sem.at[sib_base + rr], recv_sem=recv_sem.at[sib_base + rr],
            device_id=sibling, device_id_type=MESH,
        )

    def ordered(p, rr):
        return lax.rem(p + 2 + 3 * rr + 3 * (rr // 2) + 2 * (rr // 3), 4)

    def text_terms(whose, row):
        vis = v_s[...].reshape(4 * half_clips, emb)
        grad = jnp.concatenate([g_s[whose, row, 0], g_s[whose, row, 1]], axis=1)
        return tn(grad, vis).reshape(4, 128, emb)

    def sib_rows(rr, carry):
        row = ordered(p1, rr)
        tg_s[0, row] = text_terms(0, row).astype(BF)
        return carry

    lax.fori_loop(0, 4, sib_rows, 0, unroll=2)

    g1p.wait_recv()
    g1m.wait_recv()
    vgb_s[z1, hlow] = (vgb_s[z1, hlow].astype(F32) + g1_s[0].astype(F32)).astype(BF)
    g3p = remote(vgb_s.at[z1, hlow], g2_s.at[0, hlow], zp)
    vgb_s[z3, hhigh] = (vgb_s[z3, hhigh].astype(F32) + g1_s[1].astype(F32)).astype(BF)
    g3m = remote(vgb_s.at[z3, hhigh], g2_s.at[1, hhigh], zm)
    go(g3p, g3m)

    def sib_send(rr, carry):
        sib_copy(rr, ordered(p1, rr)).start()
        return carry

    lax.fori_loop(0, 4, sib_send, 0)

    def own_rows(row, carry):
        tg_s[1, row] = text_terms(1, row).astype(BF)
        return carry

    lax.fori_loop(0, 4, own_rows, 0, unroll=2)

    for copy in (g2p, g2m, g3p, g3m):
        copy.wait_recv()
    out_scale = scale_ref[0] * (1.0 / all_clips)
    vis_grad = (
        vg_s[pl.ds(pl.multiple_of(z * half_clips, 128), half_clips), :]
        + g2_s[0].astype(F32)
        + g2_s[1].astype(F32)
    ) * out_scale
    unit = vu_s[...]
    inner = jnp.sum(vis_grad * unit, axis=1, keepdims=True)
    eg_s[...] = ((vis_grad - unit * inner) / vn_s[:, :1]).astype(BF)
    eg_p = remote(eg_s, egr_s.at[tm], zp)
    eg_m = remote(eg_s, egr_s.at[tm], zm)
    go(eg_p, eg_m)

    def add_sibling(rr, carry):
        row = ordered(p2, rr)
        sib_copy(rr, row).wait_recv()
        tg_s[1, row] = (tg_s[1, row].astype(F32) + rsib_s[row].astype(F32)).astype(BF)
        return carry

    tg = tg_s.at[1]
    lax.fori_loop(0, 1, add_sibling, 0)
    s1p = remote(tg.at[up(p2, 2), low], r1_s.at[0], n2p)
    s1m = remote(tg.at[up(p2, 2), high], r1_s.at[1], n2m)
    go(s1p, s1m)
    lax.fori_loop(1, 3, add_sibling, 0)
    s2p = remote(tg.at[r3, high], r2_s.at[0, high], n2p)
    s2m = remote(tg.at[r1, low], r2_s.at[1, low], n2m)
    go(s2p, s2m)
    lax.fori_loop(3, 4, add_sibling, 0)
    eg_p.wait_recv()
    eg_m.wait_recv()
    pg_s[...] = nt(egr_s[...].reshape(clips, emb), ow_s[...]).astype(BF)

    for h, first, wide in pairs:
        if h == HEADS // 2:
            s1p.wait_recv()
            s1m.wait_recv()
            tg_s[1, r3, low] = (tg_s[1, r3, low].astype(F32) + r1_s[0].astype(F32)).astype(BF)
            s3p = remote(tg.at[r3, low], r2_s.at[0, low], n2p)
            go(s3p)
            tg_s[1, r1, high] = (tg_s[1, r1, high].astype(F32) + r1_s[1].astype(F32)).astype(BF)
            s3m = remote(tg.at[r1, high], r2_s.at[1, high], n2m)
            go(s3m)

        grads = pg_s[:, first : first + wide].astype(F32)
        part = jnp.concatenate(
            [jnp.where(window_mask(h + i, first, wide), grads, 0.0).astype(BF) for i in range(2)],
            axis=0,
        )
        for cols in columns:
            q = nt(part, w_s[cols, first : first + wide]).astype(BF)
            pq_s[h : h + 2, :, cols] = q.reshape(2, clips, q.shape[1])

    def score_terms(g, carry):
        frame_part = pl.ds(pl.multiple_of(g * 128, 128), 128)
        clip_part = pl.ds(pl.multiple_of(g * GROUP, GROUP), GROUP)
        q = pq_s[:, clip_part, :].reshape(lanes, width)
        prod = jnp.transpose(nt(q, x_s[frame_part, :]))
        t_s[frame_part, :] = prod
        u_send[pl.ds(g, 1), :] = jnp.sum(prod * e_s[frame_part, :], axis=0, keepdims=True)
        return carry

    lax.fori_loop(0, groups, score_terms, 0, unroll=8)
    uc = remote(u_send, u_recv, partner)
    uc.start()

    def vp_copy(g):
        frame_part = pl.ds(pl.multiple_of(g * 128, 128), 128)
        return pltpu.make_async_copy(
            x_s.at[frame_part], vp_hbm.at[frame_part], out_sem.at[g]
        )

    def value_part(g, carry):
        frame_part = pl.ds(pl.multiple_of(g * 128, 128), 128)
        clip_part = pl.ds(pl.multiple_of(g * GROUP, GROUP), GROUP)
        for cols in columns:
            q = pq_s[:, clip_part, cols]
            q = q.reshape(lanes, q.shape[2])
            x_s[frame_part, cols] = nn(a_s[frame_part, :], q).astype(BF)
        vp_copy(g).start()
        return carry

    lax.fori_loop(0, groups // 4, value_part, 0, unroll=4)

    for copy in (s2p, s2m, s3p, s3m):
        copy.wait_recv()
    for b in range(4):
        total = tg_s[1, p2, b].astype(F32) + r2_s[0, b].astype(F32) + r2_s[1, b].astype(F32)
        tr_s[b] = total.astype(BF)
    b1, b2, b3 = up(p1, 1), up(p1, 2), up(p1, 3)
    tlow, thigh = pl.ds(0, 64), pl.ds(64, 64)
    u1p = remote(tr_s.at[b2, tlow], q1_s.at[0], n1p)
    u1m = remote(tr_s.at[b2, thigh], q1_s.at[1], n1m)
    u2p = remote(tr_s.at[b1, thigh], q2_s.at[0, thigh], n1p)
    u2m = remote(tr_s.at[b3, tlow], q2_s.at[1, tlow], n1m)
    go(u1p, u1m, u2p, u2m)

    lax.fori_loop(groups // 4, 3 * groups // 4, value_part, 0, unroll=8)
    u1p.wait_recv()
    u1m.wait_recv()
    tr_s[b1, tlow] = (tr_s[b1, tlow].astype(F32) + q1_s[0].astype(F32)).astype(BF)
    u3p = remote(tr_s.at[b1, tlow], q2_s.at[0, tlow], n1p)
    tr_s[b3, thigh] = (tr_s[b3, thigh].astype(F32) + q1_s[1].astype(F32)).astype(BF)
    u3m = remote(tr_s.at[b3, thigh], q2_s.at[1, thigh], n1m)
    go(u3p, u3m)

    lax.fori_loop(3 * groups // 4, groups, value_part, 0, unroll=4)

    uc.wait()
    u_send[...] = u_send[...] + u_recv[...]

    def score_grads(g, carry):
        frame_part = pl.ds(pl.multiple_of(g * 128, 128), 128)
        centred = t_s[frame_part, :] - u_send[pl.ds(g, 1), :]
        sg_s[frame_part, :] = (e_s[frame_part, :] * centred * root).astype(BF)
        return carry

    sg_out = []
    for i in range(2):
        lax.fori_loop(i * groups // 2, (i + 1) * groups // 2, score_grads, 0, unroll=4)
        part = pl.ds(i * rows // 2, rows // 2)
        sg_out.append(pltpu.make_async_copy(sg_s.at[part], sg_hbm.at[part], load_sem.at[9 + i]))
        sg_out[i].start()

    for copy in (u2p, u2m, u3p, u3m):
        copy.wait_recv()
    gt_ref[...] = (
        tr_s[p1].astype(F32) + q2_s[0].astype(F32) + q2_s[1].astype(F32)
    ) * out_scale
    gt_out = pltpu.make_async_copy(gt_ref, gt_hbm, load_sem.at[8])
    gt_out.start()

    for copy in sent:
        copy.wait_send()

    def drain(rr, carry):
        sib_copy(rr, ordered(p1, rr)).wait_send()
        return carry

    lax.fori_loop(0, 4, drain, 0)

    def drain_vp(g, carry):
        vp_copy(g).wait()
        return carry

    lax.fori_loop(0, groups, drain_vp, 0)
    for copy in sg_out:
        copy.wait()
    gt_out.wait()


def final_kernel(
    vp_hbm, sg_hbm, key_hbm, texts_hbm, tg_hbm, out_hbm, gt_hbm,
    vp_s, sg_s, key_in, key_s, texts_s, tg_s, gt_s, vp_sem, sg_sem, out_sem, small_sem,
):
    rows, width = vp_s.shape
    steps = 8
    step = rows // steps
    parts = [pl.ds(i * step, step) for i in range(steps)]
    load_key = pltpu.make_async_copy(key_hbm, key_in, small_sem.at[0])
    load_texts = pltpu.make_async_copy(texts_hbm, texts_s, small_sem.at[1])
    load_tg = pltpu.make_async_copy(tg_hbm, tg_s, small_sem.at[2])
    load_key.start()
    load_vp, load_sg, outs = [], [], []
    for i, part in enumerate(parts):
        load_sg.append(pltpu.make_async_copy(sg_hbm.at[part], sg_s.at[part], sg_sem.at[i]))
        load_vp.append(pltpu.make_async_copy(vp_hbm.at[part], vp_s.at[part], vp_sem.at[i]))
        outs.append(pltpu.make_async_copy(vp_s.at[part], out_hbm.at[part], out_sem.at[i]))
        load_sg[i].start()
        load_vp[i].start()
        if i == 1:
            load_texts.start()
            load_tg.start()
    load_key.wait()
    repeat_heads(key_in, key_s)
    for i, part in enumerate(parts):
        load_sg[i].wait()
        load_vp[i].wait()
        for start in range(0, width, 256):
            cols = slice(start, min(start + 256, width))
            total = vp_s[part, cols].astype(F32) + nn(sg_s[part, :], key_s[:, cols])
            vp_s[part, cols] = total.astype(BF)
        outs[i].start()
        if i == 2:
            load_texts.wait()
            load_tg.wait()
            text_full = texts_s[...].astype(F32)
            text_norm = jnp.sqrt(jnp.sum(text_full * text_full, axis=1, keepdims=True) + EPSILON)
            text_unit = text_full / text_norm
            text_grad = tg_s[...]
            inner = jnp.sum(text_grad * text_unit, axis=1, keepdims=True)
            gt_s[...] = (text_grad - text_unit * inner) / text_norm
            gt_out = pltpu.make_async_copy(gt_s, gt_hbm, small_sem.at[3])
            gt_out.start()
    for copy in outs:
        copy.wait()
    gt_out.wait()


def local(frames, key_proj, value_weight, out_weight, texts, logit_scale, logit_bias):
    clips, frames_here, width = frames.shape
    heads = key_proj.shape[1]
    head = width // heads
    emb = out_weight.shape[1]
    all_clips = clips * lax.axis_size("clip")
    rows = clips * frames_here
    half = clips // 2
    frame_rows = frames.reshape(rows, width)
    key_t = key_proj.T
    V = pltpu.VMEM
    copies = 48
    scratch = [
        V((heads, width), BF),
        V((128, emb), BF),
        V((128, emb), F32),
        V((rows, width), BF),
        V((width, width), BF),
        V((width, emb), BF),
        V((heads * GROUP, width), BF),
        V((heads, clips, width), BF),
        V((rows, heads * GROUP), F32),
        V((2, clips // GROUP, heads * GROUP), F32),
        V((2, clips // GROUP, heads * GROUP), F32),
        V((clips // GROUP, heads * GROUP), F32),
        V((clips, width), F32),
        V((rows, heads * GROUP), BF),
        V((rows, heads * GROUP), BF),
        V((rows, heads * GROUP), F32),
        V((2, 4, 4, 128, emb), BF),
        V((2, 4, 4, 128, emb), BF),
        V((4, 4, 128, emb), BF),
        V((2, 2, 128, emb), BF),
        V((2, 4, 128, emb), BF),
        V((4, 128, emb), BF),
        V((2, 64, emb), BF),
        V((2, 128, emb), BF),
        V((2, 4, 2, 4 * half, 256), BF),
        V((2, half, emb), BF),
        V((2, half, emb), BF),
        V((half, emb), F32),
        V((half, 128), F32),
        V((4, half, emb), BF),
        V((4 * half, emb), F32),
        V((4, half, emb), BF),
        V((2, half // 2, emb), BF),
        V((2, half, emb), BF),
        V((half, emb), BF),
        V((2, half, emb), BF),
        V((clips, width), BF),
        V((clips // GROUP, heads * GROUP), F32),
        V((clips // GROUP, heads * GROUP), F32),
        pltpu.SemaphoreType.DMA((11,)),
        pltpu.SemaphoreType.DMA((clips // GROUP,)),
        pltpu.SemaphoreType.DMA((copies,)),
        pltpu.SemaphoreType.DMA((copies,)),
    ]
    anywhere = pl.BlockSpec(memory_space=pl.ANY)
    smem = pl.BlockSpec(memory_space=pltpu.SMEM)
    value_part, score_grad, text_grad = pl.pallas_call(
        functools.partial(main_kernel, (clips, width, head, emb, all_clips)),
        out_shape=(
            jax.ShapeDtypeStruct((rows, width), BF),
            jax.ShapeDtypeStruct((rows, heads * GROUP), BF),
            jax.ShapeDtypeStruct((128, emb), F32),
        ),
        in_specs=[anywhere] * 5 + [smem] * 2,
        out_specs=(anywhere, anywhere, anywhere),
        scratch_shapes=scratch,
        compiler_params=pltpu.CompilerParams(
            collective_id=0, has_side_effects=True, vmem_limit_bytes=60 * 1024 * 1024
        ),
        name="pool_pair_back",
    )(frame_rows, key_t, value_weight, out_weight, texts, logit_scale, logit_bias)
    steps = 8
    grad_frames, grad_texts = pl.pallas_call(
        final_kernel,
        in_specs=[anywhere] * 5,
        out_specs=(anywhere, anywhere),
        out_shape=(
            jax.ShapeDtypeStruct((rows, width), BF),
            jax.ShapeDtypeStruct((128, emb), F32),
        ),
        scratch_shapes=[
            V((rows, width), BF),
            V((rows, heads * GROUP), BF),
            V((heads, width), BF),
            V((heads * GROUP, width), BF),
            V((128, emb), BF),
            V((128, emb), F32),
            V((128, emb), F32),
            pltpu.SemaphoreType.DMA((steps,)),
            pltpu.SemaphoreType.DMA((steps,)),
            pltpu.SemaphoreType.DMA((steps,)),
            pltpu.SemaphoreType.DMA((4,)),
        ],
        compiler_params=pltpu.CompilerParams(vmem_limit_bytes=60 * 1024 * 1024),
        name="frame_grads",
    )(value_part, score_grad, key_t, texts, text_grad)
    return (grad_frames.reshape(clips, frames_here, width), grad_texts)


def solution(mesh):
    in_specs = (P("clip", "tm", None), P(), P(), P(), P(("tm", "clip"), None), P(), P())
    out_specs = (P("clip", "tm", None), P(("tm", "clip"), None))
    return jax.shard_map(local, mesh=mesh, in_specs=in_specs, out_specs=out_specs, check_vma=False)
```

```python
import functools
import math

import jax
import jax.numpy as jnp
from jax import lax
from jax.experimental import pallas as pl
from jax.experimental.pallas import tpu as pltpu
from jax.sharding import PartitionSpec as P

EPSILON = 1e-06
MESH = pl.DeviceIdType.MESH
BF = jnp.bfloat16
F32 = jnp.float32
NT = (((1,), (1,)), ((), ()))
TN = (((0,), (0,)), ((), ()))
HEADS = 16
GROUP = 16


def nt(a, b):
    return lax.dot_general(a, b, NT, preferred_element_type=F32)


def tn(a, b):
    return lax.dot_general(a, b, TN, preferred_element_type=F32)


def nn(a, b):
    return jnp.dot(a, b, preferred_element_type=F32)


def own_clip_mask(rows_per_clip):
    shape = (GROUP * rows_per_clip, HEADS * GROUP)
    row = lax.broadcasted_iota(jnp.int32, shape, 0)
    lane = lax.broadcasted_iota(jnp.int32, shape, 1) & (GROUP - 1)
    start = lane * rows_per_clip
    return jnp.where((row >= start) & (row < start + rows_per_clip), 1.0, 0.0)


def repeat_heads(key_ref, out_ref):
    for h in range(HEADS):
        row = key_ref[h : h + 1, :].astype(F32)
        wide = jnp.broadcast_to(row, (GROUP, row.shape[1])).astype(BF)
        out_ref[h * GROUP : (h + 1) * GROUP, :] = wide


def main_kernel(
    dims,
    frames_hbm, key_hbm, value_hbm, out_hbm, texts_hbm, scale_ref, bias_ref,
    vp_hbm, sg_hbm, gt_hbm,
    key_ref, texts_ref, gt_ref,
    x_s, w_s, ow_s, key_s, pq_s, e_s, ms_send, ms_recv, alpha_s, acc_s, a_s, sg_s, t_s,
    tt_s, tg_s, rsib_s, r1_s, r2_s, tr_s, q1_s, q2_s, g_s,
    embp_s, embr_s, vu_s, vn_s, v_s, vg_s, vgb_s, g1_s, g2_s, eg_s, egr_s, pg_s, u_send, u_recv,
    load_sem, out_sem, send_sem, recv_sem,
):
    clips, width, head, emb, all_clips = dims
    frames_here = 8
    rows = clips * frames_here
    groups = clips // GROUP
    half_clips = clips // 2
    root = 1.0 / math.sqrt(width)

    tm = lax.axis_index("tm")
    ci = lax.axis_index("clip")
    core = lax.rem(ci, 2)
    y = lax.rem(ci // 2, 4)
    x = lax.rem(ci // 8, 4)
    z_lo = ci // 32
    z = tm * 2 + z_lo

    def at(xx, yy, zz, cc):
        return (zz // 2, ((lax.rem(zz, 2) * 4 + xx) * 4 + yy) * 2 + cc)

    def up(a, n):
        return lax.rem(a + n, 4)

    p1 = y * (1 - core) + x * core
    p2 = x * (1 - core) + y * core

    def plane(a1, a2):
        return at(a2 * (1 - core) + a1 * core, a1 * (1 - core) + a2 * core, z, core)

    n1p, n1m = plane(up(p1, 1), p2), plane(up(p1, 3), p2)
    n2p, n2m = plane(p1, up(p2, 1)), plane(p1, up(p2, 3))
    z1, z2, z3 = up(z, 1 + 2 * core), up(z, 2), up(z, 3 - 2 * core)
    zp, zm = at(x, y, z1, core), at(x, y, z3, core)
    partner = (1 - tm, ci)
    sibling = at(x, y, z, 1 - core)

    counter = [0]

    def remote(src, dst, device):
        k = counter[0]
        counter[0] += 1
        return pltpu.make_async_remote_copy(
            src_ref=src, dst_ref=dst, send_sem=send_sem.at[k], recv_sem=recv_sem.at[k],
            device_id=device, device_id_type=MESH,
        )

    chunk = rows // 4
    loads = [
        pltpu.make_async_copy(
            frames_hbm.at[pl.ds(i * chunk, chunk)], x_s.at[pl.ds(i * chunk, chunk)], load_sem.at[i]
        )
        for i in range(4)
    ]
    load_w = pltpu.make_async_copy(value_hbm, w_s, load_sem.at[4])
    load_ow = pltpu.make_async_copy(out_hbm, ow_s, load_sem.at[5])
    load_key = pltpu.make_async_copy(key_hbm, key_ref, load_sem.at[6])
    load_texts = pltpu.make_async_copy(texts_hbm, texts_ref, load_sem.at[7])
    load_texts.start()
    load_key.start()
    for load in loads:
        load.start()
    load_w.start()
    load_ow.start()

    barrier = pltpu.get_barrier_semaphore()
    greet = (n1p, n1m, n2p, n2m, zp, zm, partner, sibling)
    for device in greet:
        pl.semaphore_signal(barrier, inc=1, device_id=device, device_id_type=MESH)

    load_texts.wait()
    text_full = texts_ref[...].astype(F32)
    text_norm = jnp.sqrt(jnp.sum(text_full * text_full, axis=1, keepdims=True) + EPSILON)
    tt_s[1, p2, p1] = (text_full / text_norm).astype(BF)
    load_key.wait()
    repeat_heads(key_ref, key_s)

    pl.semaphore_wait(barrier, len(greet))

    sent = []

    def go(*copies):
        for copy in copies:
            copy.start()
            sent.append(copy)

    own = tt_s.at[1]
    a0p = remote(own.at[p2, p1], own.at[p2, p1], n1p)
    a0m = remote(own.at[p2, p1], own.at[p2, p1], n1m)
    go(a0p, a0m)

    acc_s[...] = jnp.zeros_like(acc_s)
    vg_s[...] = jnp.zeros_like(vg_s)
    lanes = HEADS * GROUP
    head_start = (lax.broadcasted_iota(jnp.int32, (lanes, width), 0) // GROUP) * head
    head_lane = lax.broadcasted_iota(jnp.int32, (lanes, width), 1)
    in_head = (head_lane >= head_start) & (head_lane < head_start + head)
    pg_s[...] = jnp.where(in_head, 1.0, 0.0).astype(BF)

    mask = own_clip_mask(frames_here)
    clip_mask = own_clip_mask(1)

    def own_lane(per_clip):
        picked = per_clip.reshape(per_clip.shape[0] // GROUP, GROUP, lanes) * clip_mask[None]
        return jnp.sum(picked, axis=1)

    for i in range(4):
        loads[i].wait()
        part = pl.ds(i * chunk, chunk)
        s = nt(x_s[part, :], key_s[...]) * root
        s3 = s.reshape(chunk // frames_here, frames_here, lanes)
        top = jnp.max(s3, axis=1)
        e3 = jnp.exp(s3 - top[:, None, :])
        e_s[part, :] = e3.reshape(chunk, lanes)
        group_part = pl.ds(i * groups // 4, groups // 4)
        ms_send[0, group_part, :] = own_lane(top)
        ms_send[1, group_part, :] = own_lane(jnp.sum(e3, axis=1))
    ms = remote(ms_send, ms_recv, partner)
    go(ms)

    def a1():
        a0p.wait_recv()
        a0m.wait_recv()
        low, high = pl.ds(0, 64), pl.ds(64, 64)
        b1, b3 = up(p1, 3), up(p1, 1)
        cp = remote(own.at[p2, b1, low], own.at[p2, b1, low], n1p)
        cm = remote(own.at[p2, b3, high], own.at[p2, b3, high], n1m)
        go(cp, cm)
        return cp, cm

    def sib_row(row):
        copy = remote(own.at[row], tt_s.at[0, row], sibling)
        go(copy)
        return copy

    fwd1 = a1()

    columns = [slice(at, min(at + 256, width)) for at in range(0, width, 256)]

    def pool_group(g, carry):
        frame_part = pl.ds(pl.multiple_of(g * 128, 128), 128)
        clip_part = pl.ds(pl.multiple_of(g * GROUP, GROUP), GROUP)
        weight = jnp.transpose(e_s[frame_part, :] * mask).astype(BF)
        for cols in columns:
            pooled = nn(weight, x_s[frame_part, cols]).astype(BF)
            pq_s[:, clip_part, cols] = pooled.reshape(HEADS, GROUP, pooled.shape[1])
        return carry

    lax.fori_loop(0, groups // 2, pool_group, 0, unroll=8)

    for copy in fwd1:
        copy.wait_recv()
    row_p = remote(own.at[p2], own.at[p2], n2p)
    row_m = remote(own.at[p2], own.at[p2], n2m)
    go(row_p, row_m)
    sib0 = sib_row(p2)

    lax.fori_loop(groups // 2, groups, pool_group, 0, unroll=8)

    load_w.wait()
    load_ow.wait()

    pairs = []
    for h in range(0, HEADS, 2):
        first = min(h * head // 128, width // 128 - 2) * 128
        wide = 256 if (h + 2) * head <= first + 256 else 384
        pairs.append((h, first, wide))

    def window_mask(h, first, wide):
        lane = lax.broadcasted_iota(jnp.int32, (1, wide), 1)
        offset = h * head - first
        return (lane >= offset) & (lane < offset + head)

    for h, first, wide in pairs:
        cols = slice(first, first + wide)
        part = nn(pq_s[h : h + 2].reshape(2 * clips, width), w_s[:, cols])
        acc_s[:, cols] += jnp.where(window_mask(h, first, wide), part[:clips], 0.0) + jnp.where(
            window_mask(h + 1, first, wide), part[clips:], 0.0
        )

    ms.wait_recv()
    mine, theirs = ms_send[0], ms_recv[0]
    top = jnp.maximum(mine, theirs)
    mine_f, theirs_f = jnp.exp(mine - top), jnp.exp(theirs - top)
    alpha = mine_f / (ms_send[1] * mine_f + ms_recv[1] * theirs_f)
    alpha_s[...] = alpha
    spread = (alpha[:, None, :] * clip_mask[None]).reshape(clips, lanes)
    pooled = (acc_s[...] * nn(spread.astype(BF), pg_s[...])).astype(BF)
    embp_s[...] = nn(pooled, ow_s[...]).astype(BF).reshape(2, half_clips, emb)
    er_p = remote(embp_s.at[z1 // 2], embr_s.at[0], zp)
    er_m = remote(embp_s.at[z3 // 2], embr_s.at[1], zm)
    go(er_p, er_m)

    row_p.wait_recv()
    row_m.wait_recv()
    r1, r3 = up(p2, 3), up(p2, 1)
    low, high = pl.ds(0, 2), pl.ds(2, 2)
    fwd_p = remote(own.at[r1, low], own.at[r1, low], n2p)
    fwd_m = remote(own.at[r3, high], own.at[r3, high], n2m)
    go(fwd_p, fwd_m)
    sib1 = sib_row(r3)
    sib2 = sib_row(r1)

    def weights(g, carry):
        frame_part = pl.ds(pl.multiple_of(g * 128, 128), 128)
        wide = e_s[frame_part, :] * mask * alpha_s[pl.ds(g, 1), :]
        e_s[frame_part, :] = wide
        a_s[frame_part, :] = wide.astype(BF)
        return carry

    lax.fori_loop(0, groups // 2, weights, 0, unroll=4)

    er_p.wait_recv()
    er_m.wait_recv()
    embedding = embr_s[0].astype(F32) + embr_s[1].astype(F32)
    vis_norm = jnp.sqrt(jnp.sum(embedding * embedding, axis=1, keepdims=True) + EPSILON)
    vis_unit = embedding / vis_norm
    vu_s[...] = vis_unit
    vn_s[...] = jnp.broadcast_to(vis_norm, vn_s.shape)
    v_s[z] = vis_unit.astype(BF)
    hlow, hhigh = pl.ds(0, half_clips // 2), pl.ds(half_clips // 2, half_clips // 2)

    def send_vis(at_z, half, device):
        copy = remote(v_s.at[at_z, half], v_s.at[at_z, half], device)
        go(copy)
        return copy

    v_first = send_vis(z, hlow, zp), send_vis(z, hhigh, zm)
    v_second = send_vis(z, hhigh, zp), send_vis(z, hlow, zm)
    lax.fori_loop(groups // 2, groups, weights, 0, unroll=4)
    for copy in v_first:
        copy.wait_recv()
    v_far = send_vis(z3, hlow, zp), send_vis(z1, hhigh, zm)

    fwd_p.wait_recv()
    fwd_m.wait_recv()
    sib3 = sib_row(up(p2, 2))
    for copy in v_second + v_far:
        copy.wait_recv()

    slope = 0.5 * scale_ref[0]
    shift = 0.5 * bias_ref[0]
    diff = lax.broadcasted_iota(jnp.int32, (128, 128), 0) - lax.broadcasted_iota(
        jnp.int32, (128, 128), 1
    )
    vis_base = [
        (((1 - zz % 2) * 4 + x) * 4 + y) * 2 * clips + core * clips + (zz // 2) * half_clips
        for zz in range(4)
    ]

    def text_base(whose, a2, a1):
        c = core * whose + (1 - core) * (1 - whose)
        xx = a2 * (1 - c) + a1 * c
        yy = a1 * (1 - c) + a2 * c
        return (tm * 64 + ((z_lo * 4 + xx) * 4 + yy) * 2 + c) * 128

    def pair_row(whose, row):
        vis = v_s[...].reshape(4 * half_clips, emb)
        total = None
        for hh in range(2):
            texts = tt_s[whose, row, pl.ds(2 * hh, 2)].reshape(256, emb)
            curve = jnp.tanh(nt(vis, texts) * slope + shift) * 0.5
            tall = []
            for zz in range(4):
                wide = []
                for b in range(2):
                    gap = text_base(whose, row, 2 * hh + b) - vis_base[zz]
                    block = curve[zz * 128 : (zz + 1) * 128, b * 128 : (b + 1) * 128]
                    wide.append(block + jnp.where(diff == gap, -0.5, 0.5))
                tall.append(jnp.concatenate(wide, axis=1))
            grad = jnp.concatenate(tall, axis=0).astype(BF)
            g_s[whose, row, hh] = grad
            part = nn(grad, texts)
            total = part if total is None else total + part
        vg_s[...] += total

    def pair_rows(whose):
        def body(row, carry):
            pair_row(whose, row)
            return carry

        lax.fori_loop(0, 4, body, 0, unroll=2)

    pair_rows(1)
    for copy in (sib0, sib1, sib2, sib3):
        copy.wait_recv()
    pair_rows(0)

    vgb_s[...] = vg_s[...].astype(BF).reshape(4, half_clips, emb)
    g1p = remote(vgb_s.at[z2, hlow], g1_s.at[0], zp)
    g1m = remote(vgb_s.at[z2, hhigh], g1_s.at[1], zm)
    g2p = remote(vgb_s.at[z1, hhigh], g2_s.at[0, hhigh], zp)
    g2m = remote(vgb_s.at[z3, hlow], g2_s.at[1, hlow], zm)
    go(g1p, g1m, g2p, g2m)

    sib_base = counter[0]
    counter[0] += 4

    def sib_copy(rr, row):
        return pltpu.make_async_remote_copy(
            src_ref=tg_s.at[0, row], dst_ref=rsib_s.at[row],
            send_sem=send_sem.at[sib_base + rr], recv_sem=recv_sem.at[sib_base + rr],
            device_id=sibling, device_id_type=MESH,
        )

    def ordered(p, rr):
        return lax.rem(p + 2 + 3 * rr + 3 * (rr // 2) + 2 * (rr // 3), 4)

    def text_terms(whose, row):
        vis = v_s[...].reshape(4 * half_clips, emb)
        grad = jnp.concatenate([g_s[whose, row, 0], g_s[whose, row, 1]], axis=1)
        return tn(grad, vis).reshape(4, 128, emb)

    def sib_rows(rr, carry):
        row = ordered(p1, rr)
        tg_s[0, row] = text_terms(0, row).astype(BF)
        return carry

    lax.fori_loop(0, 4, sib_rows, 0, unroll=4)

    g1p.wait_recv()
    g1m.wait_recv()
    vgb_s[z1, hlow] = (vgb_s[z1, hlow].astype(F32) + g1_s[0].astype(F32)).astype(BF)
    g3p = remote(vgb_s.at[z1, hlow], g2_s.at[0, hlow], zp)
    vgb_s[z3, hhigh] = (vgb_s[z3, hhigh].astype(F32) + g1_s[1].astype(F32)).astype(BF)
    g3m = remote(vgb_s.at[z3, hhigh], g2_s.at[1, hhigh], zm)
    go(g3p, g3m)

    def sib_send(rr, carry):
        sib_copy(rr, ordered(p1, rr)).start()
        return carry

    lax.fori_loop(0, 4, sib_send, 0)

    def own_rows(row, carry):
        tg_s[1, row] = text_terms(1, row).astype(BF)
        return carry

    lax.fori_loop(0, 4, own_rows, 0, unroll=4)

    for copy in (g2p, g2m, g3p, g3m):
        copy.wait_recv()
    out_scale = scale_ref[0] * (1.0 / all_clips)
    vis_grad = (
        vg_s[pl.ds(pl.multiple_of(z * half_clips, 128), half_clips), :]
        + g2_s[0].astype(F32)
        + g2_s[1].astype(F32)
    ) * out_scale
    unit = vu_s[...]
    inner = jnp.sum(vis_grad * unit, axis=1, keepdims=True)
    eg_s[...] = ((vis_grad - unit * inner) / vn_s[:, :1]).astype(BF)
    eg_p = remote(eg_s, egr_s.at[tm], zp)
    eg_m = remote(eg_s, egr_s.at[tm], zm)
    go(eg_p, eg_m)

    def add_sibling(rr, carry):
        row = ordered(p2, rr)
        sib_copy(rr, row).wait_recv()
        tg_s[1, row] = (tg_s[1, row].astype(F32) + rsib_s[row].astype(F32)).astype(BF)
        return carry

    tg = tg_s.at[1]
    lax.fori_loop(0, 1, add_sibling, 0)
    s1p = remote(tg.at[up(p2, 2), low], r1_s.at[0], n2p)
    s1m = remote(tg.at[up(p2, 2), high], r1_s.at[1], n2m)
    go(s1p, s1m)
    lax.fori_loop(1, 3, add_sibling, 0)
    s2p = remote(tg.at[r3, high], r2_s.at[0, high], n2p)
    s2m = remote(tg.at[r1, low], r2_s.at[1, low], n2m)
    go(s2p, s2m)
    lax.fori_loop(3, 4, add_sibling, 0)
    eg_p.wait_recv()
    eg_m.wait_recv()
    pg_s[...] = nt(egr_s[...].reshape(clips, emb), ow_s[...]).astype(BF)

    for h, first, wide in pairs:
        if h == HEADS // 2:
            s1p.wait_recv()
            s1m.wait_recv()
            tg_s[1, r3, low] = (tg_s[1, r3, low].astype(F32) + r1_s[0].astype(F32)).astype(BF)
            s3p = remote(tg.at[r3, low], r2_s.at[0, low], n2p)
            go(s3p)
            tg_s[1, r1, high] = (tg_s[1, r1, high].astype(F32) + r1_s[1].astype(F32)).astype(BF)
            s3m = remote(tg.at[r1, high], r2_s.at[1, high], n2m)
            go(s3m)

        grads = pg_s[:, first : first + wide].astype(F32)
        part = jnp.concatenate(
            [jnp.where(window_mask(h + i, first, wide), grads, 0.0).astype(BF) for i in range(2)],
            axis=0,
        )
        for cols in columns:
            q = nt(part, w_s[cols, first : first + wide]).astype(BF)
            pq_s[h : h + 2, :, cols] = q.reshape(2, clips, q.shape[1])

    def score_terms(g, carry):
        frame_part = pl.ds(pl.multiple_of(g * 128, 128), 128)
        clip_part = pl.ds(pl.multiple_of(g * GROUP, GROUP), GROUP)
        q = pq_s[:, clip_part, :].reshape(lanes, width)
        prod = jnp.transpose(nt(q, x_s[frame_part, :]))
        t_s[frame_part, :] = prod
        u_send[pl.ds(g, 1), :] = jnp.sum(prod * e_s[frame_part, :], axis=0, keepdims=True)
        return carry

    lax.fori_loop(0, groups, score_terms, 0, unroll=8)
    uc = remote(u_send, u_recv, partner)
    uc.start()

    def vp_copy(g):
        frame_part = pl.ds(pl.multiple_of(g * 128, 128), 128)
        return pltpu.make_async_copy(
            x_s.at[frame_part], vp_hbm.at[frame_part], out_sem.at[g]
        )

    def value_part(g, carry):
        frame_part = pl.ds(pl.multiple_of(g * 128, 128), 128)
        clip_part = pl.ds(pl.multiple_of(g * GROUP, GROUP), GROUP)
        for cols in columns:
            q = pq_s[:, clip_part, cols]
            q = q.reshape(lanes, q.shape[2])
            x_s[frame_part, cols] = nn(a_s[frame_part, :], q).astype(BF)
        vp_copy(g).start()
        return carry

    lax.fori_loop(0, groups // 4, value_part, 0, unroll=4)

    for copy in (s2p, s2m, s3p, s3m):
        copy.wait_recv()
    for b in range(4):
        total = tg_s[1, p2, b].astype(F32) + r2_s[0, b].astype(F32) + r2_s[1, b].astype(F32)
        tr_s[b] = total.astype(BF)
    b1, b2, b3 = up(p1, 1), up(p1, 2), up(p1, 3)
    tlow, thigh = pl.ds(0, 64), pl.ds(64, 64)
    u1p = remote(tr_s.at[b2, tlow], q1_s.at[0], n1p)
    u1m = remote(tr_s.at[b2, thigh], q1_s.at[1], n1m)
    u2p = remote(tr_s.at[b1, thigh], q2_s.at[0, thigh], n1p)
    u2m = remote(tr_s.at[b3, tlow], q2_s.at[1, tlow], n1m)
    go(u1p, u1m, u2p, u2m)

    lax.fori_loop(groups // 4, 3 * groups // 4, value_part, 0, unroll=8)
    u1p.wait_recv()
    u1m.wait_recv()
    tr_s[b1, tlow] = (tr_s[b1, tlow].astype(F32) + q1_s[0].astype(F32)).astype(BF)
    u3p = remote(tr_s.at[b1, tlow], q2_s.at[0, tlow], n1p)
    tr_s[b3, thigh] = (tr_s[b3, thigh].astype(F32) + q1_s[1].astype(F32)).astype(BF)
    u3m = remote(tr_s.at[b3, thigh], q2_s.at[1, thigh], n1m)
    go(u3p, u3m)


    uc.wait()
    u_send[...] = u_send[...] + u_recv[...]

    def score_grads(g, carry):
        frame_part = pl.ds(pl.multiple_of(g * 128, 128), 128)
        centred = t_s[frame_part, :] - u_send[pl.ds(g, 1), :]
        sg_s[frame_part, :] = (e_s[frame_part, :] * centred * root).astype(BF)
        return carry

    sg_out = []
    for i in range(2):
        lax.fori_loop(i * groups // 2, (i + 1) * groups // 2, score_grads, 0, unroll=8)
        part = pl.ds(i * rows // 2, rows // 2)
        sg_out.append(pltpu.make_async_copy(sg_s.at[part], sg_hbm.at[part], load_sem.at[9 + i]))
        sg_out[i].start()

    lax.fori_loop(3 * groups // 4, groups, value_part, 0, unroll=4)

    for copy in (u2p, u2m, u3p, u3m):
        copy.wait_recv()
    gt_ref[...] = (
        tr_s[p1].astype(F32) + q2_s[0].astype(F32) + q2_s[1].astype(F32)
    ) * out_scale
    gt_out = pltpu.make_async_copy(gt_ref, gt_hbm, load_sem.at[8])
    gt_out.start()

    for copy in sent:
        copy.wait_send()

    def drain(rr, carry):
        sib_copy(rr, ordered(p1, rr)).wait_send()
        return carry

    lax.fori_loop(0, 4, drain, 0)

    def drain_vp(g, carry):
        vp_copy(g).wait()
        return carry

    lax.fori_loop(0, groups, drain_vp, 0)
    for copy in sg_out:
        copy.wait()
    gt_out.wait()


def final_kernel(
    vp_hbm, sg_hbm, key_hbm, texts_hbm, tg_hbm, out_hbm, gt_hbm,
    vp_s, sg_s, key_in, key_s, texts_s, tg_s, gt_s, vp_sem, sg_sem, out_sem, small_sem,
):
    rows, width = vp_s.shape
    steps = 8
    step = rows // steps
    parts = [pl.ds(i * step, step) for i in range(steps)]
    load_key = pltpu.make_async_copy(key_hbm, key_in, small_sem.at[0])
    load_texts = pltpu.make_async_copy(texts_hbm, texts_s, small_sem.at[1])
    load_tg = pltpu.make_async_copy(tg_hbm, tg_s, small_sem.at[2])
    load_key.start()
    load_vp, load_sg, outs = [], [], []
    for i, part in enumerate(parts):
        load_sg.append(pltpu.make_async_copy(sg_hbm.at[part], sg_s.at[part], sg_sem.at[i]))
        load_vp.append(pltpu.make_async_copy(vp_hbm.at[part], vp_s.at[part], vp_sem.at[i]))
        outs.append(pltpu.make_async_copy(vp_s.at[part], out_hbm.at[part], out_sem.at[i]))
        load_sg[i].start()
        load_vp[i].start()
        if i == 1:
            load_texts.start()
            load_tg.start()
    load_key.wait()
    repeat_heads(key_in, key_s)
    for i, part in enumerate(parts):
        load_sg[i].wait()
        load_vp[i].wait()
        for start in range(0, width, 256):
            cols = slice(start, min(start + 256, width))
            total = vp_s[part, cols].astype(F32) + nn(sg_s[part, :], key_s[:, cols])
            vp_s[part, cols] = total.astype(BF)
        outs[i].start()
        if i == 2:
            load_texts.wait()
            load_tg.wait()
            text_full = texts_s[...].astype(F32)
            text_norm = jnp.sqrt(jnp.sum(text_full * text_full, axis=1, keepdims=True) + EPSILON)
            text_unit = text_full / text_norm
            text_grad = tg_s[...]
            inner = jnp.sum(text_grad * text_unit, axis=1, keepdims=True)
            gt_s[...] = (text_grad - text_unit * inner) / text_norm
            gt_out = pltpu.make_async_copy(gt_s, gt_hbm, small_sem.at[3])
            gt_out.start()
    for copy in outs:
        copy.wait()
    gt_out.wait()


def local(frames, key_proj, value_weight, out_weight, texts, logit_scale, logit_bias):
    clips, frames_here, width = frames.shape
    heads = key_proj.shape[1]
    head = width // heads
    emb = out_weight.shape[1]
    all_clips = clips * lax.axis_size("clip")
    rows = clips * frames_here
    half = clips // 2
    frame_rows = frames.reshape(rows, width)
    key_t = key_proj.T
    V = pltpu.VMEM
    copies = 48
    scratch = [
        V((heads, width), BF),
        V((128, emb), BF),
        V((128, emb), F32),
        V((rows, width), BF),
        V((width, width), BF),
        V((width, emb), BF),
        V((heads * GROUP, width), BF),
        V((heads, clips, width), BF),
        V((rows, heads * GROUP), F32),
        V((2, clips // GROUP, heads * GROUP), F32),
        V((2, clips // GROUP, heads * GROUP), F32),
        V((clips // GROUP, heads * GROUP), F32),
        V((clips, width), F32),
        V((rows, heads * GROUP), BF),
        V((rows, heads * GROUP), BF),
        V((rows, heads * GROUP), F32),
        V((2, 4, 4, 128, emb), BF),
        V((2, 4, 4, 128, emb), BF),
        V((4, 4, 128, emb), BF),
        V((2, 2, 128, emb), BF),
        V((2, 4, 128, emb), BF),
        V((4, 128, emb), BF),
        V((2, 64, emb), BF),
        V((2, 128, emb), BF),
        V((2, 4, 2, 4 * half, 256), BF),
        V((2, half, emb), BF),
        V((2, half, emb), BF),
        V((half, emb), F32),
        V((half, 128), F32),
        V((4, half, emb), BF),
        V((4 * half, emb), F32),
        V((4, half, emb), BF),
        V((2, half // 2, emb), BF),
        V((2, half, emb), BF),
        V((half, emb), BF),
        V((2, half, emb), BF),
        V((clips, width), BF),
        V((clips // GROUP, heads * GROUP), F32),
        V((clips // GROUP, heads * GROUP), F32),
        pltpu.SemaphoreType.DMA((11,)),
        pltpu.SemaphoreType.DMA((clips // GROUP,)),
        pltpu.SemaphoreType.DMA((copies,)),
        pltpu.SemaphoreType.DMA((copies,)),
    ]
    anywhere = pl.BlockSpec(memory_space=pl.ANY)
    smem = pl.BlockSpec(memory_space=pltpu.SMEM)
    value_part, score_grad, text_grad = pl.pallas_call(
        functools.partial(main_kernel, (clips, width, head, emb, all_clips)),
        out_shape=(
            jax.ShapeDtypeStruct((rows, width), BF),
            jax.ShapeDtypeStruct((rows, heads * GROUP), BF),
            jax.ShapeDtypeStruct((128, emb), F32),
        ),
        in_specs=[anywhere] * 5 + [smem] * 2,
        out_specs=(anywhere, anywhere, anywhere),
        scratch_shapes=scratch,
        compiler_params=pltpu.CompilerParams(
            collective_id=0, has_side_effects=True, vmem_limit_bytes=60 * 1024 * 1024
        ),
        name="pool_pair_back",
    )(frame_rows, key_t, value_weight, out_weight, texts, logit_scale, logit_bias)
    steps = 8
    grad_frames, grad_texts = pl.pallas_call(
        final_kernel,
        in_specs=[anywhere] * 5,
        out_specs=(anywhere, anywhere),
        out_shape=(
            jax.ShapeDtypeStruct((rows, width), BF),
            jax.ShapeDtypeStruct((128, emb), F32),
        ),
        scratch_shapes=[
            V((rows, width), BF),
            V((rows, heads * GROUP), BF),
            V((heads, width), BF),
            V((heads * GROUP, width), BF),
            V((128, emb), BF),
            V((128, emb), F32),
            V((128, emb), F32),
            pltpu.SemaphoreType.DMA((steps,)),
            pltpu.SemaphoreType.DMA((steps,)),
            pltpu.SemaphoreType.DMA((steps,)),
            pltpu.SemaphoreType.DMA((4,)),
        ],
        compiler_params=pltpu.CompilerParams(vmem_limit_bytes=60 * 1024 * 1024),
        name="frame_grads",
    )(value_part, score_grad, key_t, texts, text_grad)
    return (grad_frames.reshape(clips, frames_here, width), grad_texts)


def solution(mesh):
    in_specs = (P("clip", "tm", None), P(), P(), P(), P(("tm", "clip"), None), P(), P())
    out_specs = (P("clip", "tm", None), P(("tm", "clip"), None))
    return jax.shard_map(local, mesh=mesh, in_specs=in_specs, out_specs=out_specs, check_vma=False)
```

```python
import functools
import math

import jax
import jax.numpy as jnp
from jax import lax
from jax.experimental import pallas as pl
from jax.experimental.pallas import tpu as pltpu
from jax.sharding import PartitionSpec as P

EPSILON = 1e-06
MESH = pl.DeviceIdType.MESH
BF = jnp.bfloat16
F32 = jnp.float32
NT = (((1,), (1,)), ((), ()))
TN = (((0,), (0,)), ((), ()))
HEADS = 16
GROUP = 16


def nt(a, b):
    return lax.dot_general(a, b, NT, preferred_element_type=F32)


def tn(a, b):
    return lax.dot_general(a, b, TN, preferred_element_type=F32)


def nn(a, b):
    return jnp.dot(a, b, preferred_element_type=F32)


def own_clip_mask(rows_per_clip):
    shape = (GROUP * rows_per_clip, HEADS * GROUP)
    row = lax.broadcasted_iota(jnp.int32, shape, 0)
    lane = lax.broadcasted_iota(jnp.int32, shape, 1) & (GROUP - 1)
    start = lane * rows_per_clip
    return jnp.where((row >= start) & (row < start + rows_per_clip), 1.0, 0.0)


def repeat_heads(key_ref, out_ref):
    for h in range(HEADS):
        row = key_ref[h : h + 1, :].astype(F32)
        wide = jnp.broadcast_to(row, (GROUP, row.shape[1])).astype(BF)
        out_ref[h * GROUP : (h + 1) * GROUP, :] = wide


def main_kernel(
    dims,
    frames_hbm, key_hbm, value_hbm, out_hbm, texts_hbm, scale_ref, bias_ref,
    vp_hbm, sg_hbm, gt_hbm,
    key_ref, texts_ref, gt_ref,
    x_s, w_s, ow_s, key_s, pq_s, e_s, ms_send, ms_recv, alpha_s, acc_s, a_s, sg_s, t_s,
    tt_s, tg_s, rsib_s, r1_s, r2_s, tr_s, q1_s, q2_s, g_s,
    embp_s, embr_s, vu_s, vn_s, v_s, vg_s, vgb_s, g1_s, g2_s, eg_s, egr_s, pg_s, u_send, u_recv,
    load_sem, out_sem, send_sem, recv_sem,
):
    clips, width, head, emb, all_clips = dims
    frames_here = 8
    rows = clips * frames_here
    groups = clips // GROUP
    half_clips = clips // 2
    root = 1.0 / math.sqrt(width)

    tm = lax.axis_index("tm")
    ci = lax.axis_index("clip")
    core = lax.rem(ci, 2)
    y = lax.rem(ci // 2, 4)
    x = lax.rem(ci // 8, 4)
    z_lo = ci // 32
    z = tm * 2 + z_lo

    def at(xx, yy, zz, cc):
        return (zz // 2, ((lax.rem(zz, 2) * 4 + xx) * 4 + yy) * 2 + cc)

    def up(a, n):
        return lax.rem(a + n, 4)

    p1 = y * (1 - core) + x * core
    p2 = x * (1 - core) + y * core

    def plane(a1, a2):
        return at(a2 * (1 - core) + a1 * core, a1 * (1 - core) + a2 * core, z, core)

    n1p, n1m = plane(up(p1, 1), p2), plane(up(p1, 3), p2)
    n2p, n2m = plane(p1, up(p2, 1)), plane(p1, up(p2, 3))
    z1, z2, z3 = up(z, 1 + 2 * core), up(z, 2), up(z, 3 - 2 * core)
    zp, zm = at(x, y, z1, core), at(x, y, z3, core)
    partner = (1 - tm, ci)
    sibling = at(x, y, z, 1 - core)

    counter = [0]

    def remote(src, dst, device):
        k = counter[0]
        counter[0] += 1
        return pltpu.make_async_remote_copy(
            src_ref=src, dst_ref=dst, send_sem=send_sem.at[k], recv_sem=recv_sem.at[k],
            device_id=device, device_id_type=MESH,
        )

    chunk = rows // 4
    loads = [
        pltpu.make_async_copy(
            frames_hbm.at[pl.ds(i * chunk, chunk)], x_s.at[pl.ds(i * chunk, chunk)], load_sem.at[i]
        )
        for i in range(4)
    ]
    load_w = pltpu.make_async_copy(value_hbm, w_s, load_sem.at[4])
    load_ow = pltpu.make_async_copy(out_hbm, ow_s, load_sem.at[5])
    load_key = pltpu.make_async_copy(key_hbm, key_ref, load_sem.at[6])
    load_texts = pltpu.make_async_copy(texts_hbm, texts_ref, load_sem.at[7])
    load_texts.start()
    load_key.start()
    for load in loads:
        load.start()
    load_w.start()
    load_ow.start()

    barrier = pltpu.get_barrier_semaphore()
    greet = (n1p, n1m, n2p, n2m, zp, zm, partner, sibling)
    for device in greet:
        pl.semaphore_signal(barrier, inc=1, device_id=device, device_id_type=MESH)

    load_texts.wait()
    text_full = texts_ref[...].astype(F32)
    text_norm = jnp.sqrt(jnp.sum(text_full * text_full, axis=1, keepdims=True) + EPSILON)
    tt_s[1, p2, p1] = (text_full / text_norm).astype(BF)
    load_key.wait()
    repeat_heads(key_ref, key_s)

    pl.semaphore_wait(barrier, len(greet))

    sent = []

    def go(*copies):
        for copy in copies:
            copy.start()
            sent.append(copy)

    own = tt_s.at[1]
    a0p = remote(own.at[p2, p1], own.at[p2, p1], n1p)
    a0m = remote(own.at[p2, p1], own.at[p2, p1], n1m)
    go(a0p, a0m)

    acc_s[...] = jnp.zeros_like(acc_s)
    vg_s[...] = jnp.zeros_like(vg_s)
    lanes = HEADS * GROUP
    head_start = (lax.broadcasted_iota(jnp.int32, (lanes, width), 0) // GROUP) * head
    head_lane = lax.broadcasted_iota(jnp.int32, (lanes, width), 1)
    in_head = (head_lane >= head_start) & (head_lane < head_start + head)
    pg_s[...] = jnp.where(in_head, 1.0, 0.0).astype(BF)

    mask = own_clip_mask(frames_here)
    clip_mask = own_clip_mask(1)

    def own_lane(per_clip):
        picked = per_clip.reshape(per_clip.shape[0] // GROUP, GROUP, lanes) * clip_mask[None]
        return jnp.sum(picked, axis=1)

    for i in range(4):
        loads[i].wait()
        part = pl.ds(i * chunk, chunk)
        s = nt(x_s[part, :], key_s[...]) * root
        s3 = s.reshape(chunk // frames_here, frames_here, lanes)
        top = jnp.max(s3, axis=1)
        e3 = jnp.exp(s3 - top[:, None, :])
        e_s[part, :] = e3.reshape(chunk, lanes)
        group_part = pl.ds(i * groups // 4, groups // 4)
        ms_send[0, group_part, :] = own_lane(top)
        ms_send[1, group_part, :] = own_lane(jnp.sum(e3, axis=1))
    ms = remote(ms_send, ms_recv, partner)
    go(ms)

    def a1():
        a0p.wait_recv()
        a0m.wait_recv()
        low, high = pl.ds(0, 64), pl.ds(64, 64)
        b1, b3 = up(p1, 3), up(p1, 1)
        cp = remote(own.at[p2, b1, low], own.at[p2, b1, low], n1p)
        cm = remote(own.at[p2, b3, high], own.at[p2, b3, high], n1m)
        go(cp, cm)
        return cp, cm

    def sib_row(row):
        copy = remote(own.at[row], tt_s.at[0, row], sibling)
        go(copy)
        return copy

    fwd1 = a1()

    columns = [slice(at, min(at + 256, width)) for at in range(0, width, 256)]

    def pool_group(g, carry):
        frame_part = pl.ds(pl.multiple_of(g * 128, 128), 128)
        clip_part = pl.ds(pl.multiple_of(g * GROUP, GROUP), GROUP)
        weight = jnp.transpose(e_s[frame_part, :] * mask).astype(BF)
        for cols in columns:
            pooled = nn(weight, x_s[frame_part, cols]).astype(BF)
            pq_s[:, clip_part, cols] = pooled.reshape(HEADS, GROUP, pooled.shape[1])
        return carry

    lax.fori_loop(0, groups // 2, pool_group, 0, unroll=8)

    for copy in fwd1:
        copy.wait_recv()
    row_p = remote(own.at[p2], own.at[p2], n2p)
    row_m = remote(own.at[p2], own.at[p2], n2m)
    go(row_p, row_m)
    sib0 = sib_row(p2)

    lax.fori_loop(groups // 2, groups, pool_group, 0, unroll=8)

    load_w.wait()
    load_ow.wait()

    pairs = []
    for h in range(0, HEADS, 2):
        first = min(h * head // 128, width // 128 - 2) * 128
        wide = 256 if (h + 2) * head <= first + 256 else 384
        pairs.append((h, first, wide))

    def window_mask(h, first, wide):
        lane = lax.broadcasted_iota(jnp.int32, (1, wide), 1)
        offset = h * head - first
        return (lane >= offset) & (lane < offset + head)

    for h, first, wide in pairs:
        cols = slice(first, first + wide)
        part = nn(pq_s[h : h + 2].reshape(2 * clips, width), w_s[:, cols])
        acc_s[:, cols] += jnp.where(window_mask(h, first, wide), part[:clips], 0.0) + jnp.where(
            window_mask(h + 1, first, wide), part[clips:], 0.0
        )

    ms.wait_recv()
    mine, theirs = ms_send[0], ms_recv[0]
    top = jnp.maximum(mine, theirs)
    mine_f, theirs_f = jnp.exp(mine - top), jnp.exp(theirs - top)
    alpha = mine_f / (ms_send[1] * mine_f + ms_recv[1] * theirs_f)
    alpha_s[...] = alpha
    spread = (alpha[:, None, :] * clip_mask[None]).reshape(clips, lanes)
    pooled = (acc_s[...] * nn(spread.astype(BF), pg_s[...])).astype(BF)
    embp_s[...] = nn(pooled, ow_s[...]).astype(BF).reshape(2, half_clips, emb)
    er_p = remote(embp_s.at[z1 // 2], embr_s.at[0], zp)
    er_m = remote(embp_s.at[z3 // 2], embr_s.at[1], zm)
    go(er_p, er_m)

    row_p.wait_recv()
    row_m.wait_recv()
    r1, r3 = up(p2, 3), up(p2, 1)
    low, high = pl.ds(0, 2), pl.ds(2, 2)
    fwd_p = remote(own.at[r1, low], own.at[r1, low], n2p)
    fwd_m = remote(own.at[r3, high], own.at[r3, high], n2m)
    go(fwd_p, fwd_m)
    sib1 = sib_row(r3)
    sib2 = sib_row(r1)

    def weights(g, carry):
        frame_part = pl.ds(pl.multiple_of(g * 128, 128), 128)
        wide = e_s[frame_part, :] * mask * alpha_s[pl.ds(g, 1), :]
        e_s[frame_part, :] = wide
        a_s[frame_part, :] = wide.astype(BF)
        return carry

    lax.fori_loop(0, groups // 2, weights, 0, unroll=4)

    er_p.wait_recv()
    er_m.wait_recv()
    embedding = embr_s[0].astype(F32) + embr_s[1].astype(F32)
    vis_norm = jnp.sqrt(jnp.sum(embedding * embedding, axis=1, keepdims=True) + EPSILON)
    vis_unit = embedding / vis_norm
    vu_s[...] = vis_unit
    vn_s[...] = jnp.broadcast_to(vis_norm, vn_s.shape)
    v_s[z] = vis_unit.astype(BF)
    hlow, hhigh = pl.ds(0, half_clips // 2), pl.ds(half_clips // 2, half_clips // 2)

    def send_vis(at_z, half, device):
        copy = remote(v_s.at[at_z, half], v_s.at[at_z, half], device)
        go(copy)
        return copy

    v_first = send_vis(z, hlow, zp), send_vis(z, hhigh, zm)
    v_second = send_vis(z, hhigh, zp), send_vis(z, hlow, zm)
    lax.fori_loop(groups // 2, groups, weights, 0, unroll=4)
    for copy in v_first:
        copy.wait_recv()
    v_far = send_vis(z3, hlow, zp), send_vis(z1, hhigh, zm)

    fwd_p.wait_recv()
    fwd_m.wait_recv()
    sib3 = sib_row(up(p2, 2))
    for copy in v_second + v_far:
        copy.wait_recv()

    slope = 0.5 * scale_ref[0]
    shift = 0.5 * bias_ref[0]
    diff = lax.broadcasted_iota(jnp.int32, (128, 128), 0) - lax.broadcasted_iota(
        jnp.int32, (128, 128), 1
    )
    vis_base = [
        (((1 - zz % 2) * 4 + x) * 4 + y) * 2 * clips + core * clips + (zz // 2) * half_clips
        for zz in range(4)
    ]

    def text_base(whose, a2, a1):
        c = core * whose + (1 - core) * (1 - whose)
        xx = a2 * (1 - c) + a1 * c
        yy = a1 * (1 - c) + a2 * c
        return (tm * 64 + ((z_lo * 4 + xx) * 4 + yy) * 2 + c) * 128

    def pair_row(whose, row):
        vis = v_s[...].reshape(4 * half_clips, emb)
        total = None
        for hh in range(2):
            texts = tt_s[whose, row, pl.ds(2 * hh, 2)].reshape(256, emb)
            curve = jnp.tanh(nt(vis, texts) * slope + shift) * 0.5
            tall = []
            for zz in range(4):
                wide = []
                for b in range(2):
                    gap = text_base(whose, row, 2 * hh + b) - vis_base[zz]
                    block = curve[zz * 128 : (zz + 1) * 128, b * 128 : (b + 1) * 128]
                    wide.append(block + jnp.where(diff == gap, -0.5, 0.5))
                tall.append(jnp.concatenate(wide, axis=1))
            grad = jnp.concatenate(tall, axis=0).astype(BF)
            g_s[whose, row, hh] = grad
            part = nn(grad, texts)
            total = part if total is None else total + part
        vg_s[...] += total

    def pair_rows(whose):
        def body(row, carry):
            pair_row(whose, row)
            return carry

        lax.fori_loop(0, 4, body, 0, unroll=4)

    pair_rows(1)
    for copy in (sib0, sib1, sib2, sib3):
        copy.wait_recv()
    pair_rows(0)

    vgb_s[...] = vg_s[...].astype(BF).reshape(4, half_clips, emb)
    g1p = remote(vgb_s.at[z2, hlow], g1_s.at[0], zp)
    g1m = remote(vgb_s.at[z2, hhigh], g1_s.at[1], zm)
    g2p = remote(vgb_s.at[z1, hhigh], g2_s.at[0, hhigh], zp)
    g2m = remote(vgb_s.at[z3, hlow], g2_s.at[1, hlow], zm)
    go(g1p, g1m, g2p, g2m)

    sib_base = counter[0]
    counter[0] += 4

    def sib_copy(rr, row):
        return pltpu.make_async_remote_copy(
            src_ref=tg_s.at[0, row], dst_ref=rsib_s.at[row],
            send_sem=send_sem.at[sib_base + rr], recv_sem=recv_sem.at[sib_base + rr],
            device_id=sibling, device_id_type=MESH,
        )

    def ordered(p, rr):
        return lax.rem(p + 2 + 3 * rr + 3 * (rr // 2) + 2 * (rr // 3), 4)

    def text_terms(whose, row):
        vis = v_s[...].reshape(4 * half_clips, emb)
        grad = jnp.concatenate([g_s[whose, row, 0], g_s[whose, row, 1]], axis=1)
        return tn(grad, vis).reshape(4, 128, emb)

    def sib_rows(rr, carry):
        row = ordered(p1, rr)
        tg_s[0, row] = text_terms(0, row).astype(BF)
        return carry

    lax.fori_loop(0, 4, sib_rows, 0, unroll=4)

    g1p.wait_recv()
    g1m.wait_recv()
    vgb_s[z1, hlow] = (vgb_s[z1, hlow].astype(F32) + g1_s[0].astype(F32)).astype(BF)
    g3p = remote(vgb_s.at[z1, hlow], g2_s.at[0, hlow], zp)
    vgb_s[z3, hhigh] = (vgb_s[z3, hhigh].astype(F32) + g1_s[1].astype(F32)).astype(BF)
    g3m = remote(vgb_s.at[z3, hhigh], g2_s.at[1, hhigh], zm)
    go(g3p, g3m)

    def sib_send(rr, carry):
        sib_copy(rr, ordered(p1, rr)).start()
        return carry

    lax.fori_loop(0, 4, sib_send, 0)

    def own_rows(row, carry):
        tg_s[1, row] = text_terms(1, row).astype(BF)
        return carry

    lax.fori_loop(0, 4, own_rows, 0, unroll=4)

    for copy in (g2p, g2m, g3p, g3m):
        copy.wait_recv()
    out_scale = scale_ref[0] * (1.0 / all_clips)
    vis_grad = (
        vg_s[pl.ds(pl.multiple_of(z * half_clips, 128), half_clips), :]
        + g2_s[0].astype(F32)
        + g2_s[1].astype(F32)
    ) * out_scale
    unit = vu_s[...]
    inner = jnp.sum(vis_grad * unit, axis=1, keepdims=True)
    eg_s[...] = ((vis_grad - unit * inner) / vn_s[:, :1]).astype(BF)
    eg_p = remote(eg_s, egr_s.at[tm], zp)
    eg_m = remote(eg_s, egr_s.at[tm], zm)
    go(eg_p, eg_m)

    def add_sibling(rr, carry):
        row = ordered(p2, rr)
        sib_copy(rr, row).wait_recv()
        tg_s[1, row] = (tg_s[1, row].astype(F32) + rsib_s[row].astype(F32)).astype(BF)
        return carry

    tg = tg_s.at[1]
    lax.fori_loop(0, 1, add_sibling, 0)
    s1p = remote(tg.at[up(p2, 2), low], r1_s.at[0], n2p)
    s1m = remote(tg.at[up(p2, 2), high], r1_s.at[1], n2m)
    go(s1p, s1m)
    lax.fori_loop(1, 3, add_sibling, 0)
    s2p = remote(tg.at[r3, high], r2_s.at[0, high], n2p)
    s2m = remote(tg.at[r1, low], r2_s.at[1, low], n2m)
    go(s2p, s2m)
    lax.fori_loop(3, 4, add_sibling, 0)
    eg_p.wait_recv()
    eg_m.wait_recv()
    pg_s[...] = nt(egr_s[...].reshape(clips, emb), ow_s[...]).astype(BF)

    for h, first, wide in pairs:
        if h == HEADS // 2:
            s1p.wait_recv()
            s1m.wait_recv()
            tg_s[1, r3, low] = (tg_s[1, r3, low].astype(F32) + r1_s[0].astype(F32)).astype(BF)
            s3p = remote(tg.at[r3, low], r2_s.at[0, low], n2p)
            go(s3p)
            tg_s[1, r1, high] = (tg_s[1, r1, high].astype(F32) + r1_s[1].astype(F32)).astype(BF)
            s3m = remote(tg.at[r1, high], r2_s.at[1, high], n2m)
            go(s3m)

        grads = pg_s[:, first : first + wide].astype(F32)
        part = jnp.concatenate(
            [jnp.where(window_mask(h + i, first, wide), grads, 0.0).astype(BF) for i in range(2)],
            axis=0,
        )
        for cols in columns:
            q = nt(part, w_s[cols, first : first + wide]).astype(BF)
            pq_s[h : h + 2, :, cols] = q.reshape(2, clips, q.shape[1])

    def score_terms(g, carry):
        frame_part = pl.ds(pl.multiple_of(g * 128, 128), 128)
        clip_part = pl.ds(pl.multiple_of(g * GROUP, GROUP), GROUP)
        q = pq_s[:, clip_part, :].reshape(lanes, width)
        prod = jnp.transpose(nt(q, x_s[frame_part, :]))
        t_s[frame_part, :] = prod
        u_send[pl.ds(g, 1), :] = jnp.sum(prod * e_s[frame_part, :], axis=0, keepdims=True)
        return carry

    lax.fori_loop(0, groups, score_terms, 0, unroll=8)
    uc = remote(u_send, u_recv, partner)
    uc.start()

    def vp_copy(g):
        frame_part = pl.ds(pl.multiple_of(g * 128, 128), 128)
        return pltpu.make_async_copy(
            x_s.at[frame_part], vp_hbm.at[frame_part], out_sem.at[g]
        )

    def value_part(g, carry):
        frame_part = pl.ds(pl.multiple_of(g * 128, 128), 128)
        clip_part = pl.ds(pl.multiple_of(g * GROUP, GROUP), GROUP)
        for cols in columns:
            q = pq_s[:, clip_part, cols]
            q = q.reshape(lanes, q.shape[2])
            x_s[frame_part, cols] = nn(a_s[frame_part, :], q).astype(BF)
        vp_copy(g).start()
        return carry

    lax.fori_loop(0, groups // 4, value_part, 0, unroll=4)

    for copy in (s2p, s2m, s3p, s3m):
        copy.wait_recv()
    for b in range(4):
        total = tg_s[1, p2, b].astype(F32) + r2_s[0, b].astype(F32) + r2_s[1, b].astype(F32)
        tr_s[b] = total.astype(BF)
    b1, b2, b3 = up(p1, 1), up(p1, 2), up(p1, 3)
    tlow, thigh = pl.ds(0, 64), pl.ds(64, 64)
    u1p = remote(tr_s.at[b2, tlow], q1_s.at[0], n1p)
    u1m = remote(tr_s.at[b2, thigh], q1_s.at[1], n1m)
    u2p = remote(tr_s.at[b1, thigh], q2_s.at[0, thigh], n1p)
    u2m = remote(tr_s.at[b3, tlow], q2_s.at[1, tlow], n1m)
    go(u1p, u1m, u2p, u2m)

    lax.fori_loop(groups // 4, 3 * groups // 4, value_part, 0, unroll=8)
    u1p.wait_recv()
    u1m.wait_recv()
    tr_s[b1, tlow] = (tr_s[b1, tlow].astype(F32) + q1_s[0].astype(F32)).astype(BF)
    u3p = remote(tr_s.at[b1, tlow], q2_s.at[0, tlow], n1p)
    tr_s[b3, thigh] = (tr_s[b3, thigh].astype(F32) + q1_s[1].astype(F32)).astype(BF)
    u3m = remote(tr_s.at[b3, thigh], q2_s.at[1, thigh], n1m)
    go(u3p, u3m)


    uc.wait()
    u_send[...] = u_send[...] + u_recv[...]

    def score_grads(g, carry):
        frame_part = pl.ds(pl.multiple_of(g * 128, 128), 128)
        centred = t_s[frame_part, :] - u_send[pl.ds(g, 1), :]
        sg_s[frame_part, :] = (e_s[frame_part, :] * centred * root).astype(BF)
        return carry

    sg_out = []
    for i in range(2):
        lax.fori_loop(i * groups // 2, (i + 1) * groups // 2, score_grads, 0, unroll=8)
        part = pl.ds(i * rows // 2, rows // 2)
        sg_out.append(pltpu.make_async_copy(sg_s.at[part], sg_hbm.at[part], load_sem.at[9 + i]))
        sg_out[i].start()

    lax.fori_loop(3 * groups // 4, groups, value_part, 0, unroll=4)

    for copy in (u2p, u2m, u3p, u3m):
        copy.wait_recv()
    gt_ref[...] = (
        tr_s[p1].astype(F32) + q2_s[0].astype(F32) + q2_s[1].astype(F32)
    ) * out_scale
    gt_out = pltpu.make_async_copy(gt_ref, gt_hbm, load_sem.at[8])
    gt_out.start()

    for copy in sent:
        copy.wait_send()

    def drain(rr, carry):
        sib_copy(rr, ordered(p1, rr)).wait_send()
        return carry

    lax.fori_loop(0, 4, drain, 0)

    def drain_vp(g, carry):
        vp_copy(g).wait()
        return carry

    lax.fori_loop(0, groups, drain_vp, 0)
    for copy in sg_out:
        copy.wait()
    gt_out.wait()


def final_kernel(
    vp_hbm, sg_hbm, key_hbm, texts_hbm, tg_hbm, out_hbm, gt_hbm,
    vp_s, sg_s, key_in, key_s, texts_s, tg_s, gt_s, vp_sem, sg_sem, out_sem, small_sem,
):
    rows, width = vp_s.shape
    steps = 8
    step = rows // steps
    parts = [pl.ds(i * step, step) for i in range(steps)]
    load_key = pltpu.make_async_copy(key_hbm, key_in, small_sem.at[0])
    load_texts = pltpu.make_async_copy(texts_hbm, texts_s, small_sem.at[1])
    load_tg = pltpu.make_async_copy(tg_hbm, tg_s, small_sem.at[2])
    load_key.start()
    load_vp, load_sg, outs = [], [], []
    for i, part in enumerate(parts):
        load_sg.append(pltpu.make_async_copy(sg_hbm.at[part], sg_s.at[part], sg_sem.at[i]))
        load_vp.append(pltpu.make_async_copy(vp_hbm.at[part], vp_s.at[part], vp_sem.at[i]))
        outs.append(pltpu.make_async_copy(vp_s.at[part], out_hbm.at[part], out_sem.at[i]))
        load_sg[i].start()
        load_vp[i].start()
        if i == 1:
            load_texts.start()
            load_tg.start()
    load_key.wait()
    repeat_heads(key_in, key_s)
    for i, part in enumerate(parts):
        load_sg[i].wait()
        load_vp[i].wait()
        for start in range(0, width, 256):
            cols = slice(start, min(start + 256, width))
            total = vp_s[part, cols].astype(F32) + nn(sg_s[part, :], key_s[:, cols])
            vp_s[part, cols] = total.astype(BF)
        outs[i].start()
        if i == 2:
            load_texts.wait()
            load_tg.wait()
            text_full = texts_s[...].astype(F32)
            text_norm = jnp.sqrt(jnp.sum(text_full * text_full, axis=1, keepdims=True) + EPSILON)
            text_unit = text_full / text_norm
            text_grad = tg_s[...]
            inner = jnp.sum(text_grad * text_unit, axis=1, keepdims=True)
            gt_s[...] = (text_grad - text_unit * inner) / text_norm
            gt_out = pltpu.make_async_copy(gt_s, gt_hbm, small_sem.at[3])
            gt_out.start()
    for copy in outs:
        copy.wait()
    gt_out.wait()


def local(frames, key_proj, value_weight, out_weight, texts, logit_scale, logit_bias):
    clips, frames_here, width = frames.shape
    heads = key_proj.shape[1]
    head = width // heads
    emb = out_weight.shape[1]
    all_clips = clips * lax.axis_size("clip")
    rows = clips * frames_here
    half = clips // 2
    frame_rows = frames.reshape(rows, width)
    key_t = key_proj.T
    V = pltpu.VMEM
    copies = 48
    scratch = [
        V((heads, width), BF),
        V((128, emb), BF),
        V((128, emb), F32),
        V((rows, width), BF),
        V((width, width), BF),
        V((width, emb), BF),
        V((heads * GROUP, width), BF),
        V((heads, clips, width), BF),
        V((rows, heads * GROUP), F32),
        V((2, clips // GROUP, heads * GROUP), F32),
        V((2, clips // GROUP, heads * GROUP), F32),
        V((clips // GROUP, heads * GROUP), F32),
        V((clips, width), F32),
        V((rows, heads * GROUP), BF),
        V((rows, heads * GROUP), BF),
        V((rows, heads * GROUP), F32),
        V((2, 4, 4, 128, emb), BF),
        V((2, 4, 4, 128, emb), BF),
        V((4, 4, 128, emb), BF),
        V((2, 2, 128, emb), BF),
        V((2, 4, 128, emb), BF),
        V((4, 128, emb), BF),
        V((2, 64, emb), BF),
        V((2, 128, emb), BF),
        V((2, 4, 2, 4 * half, 256), BF),
        V((2, half, emb), BF),
        V((2, half, emb), BF),
        V((half, emb), F32),
        V((half, 128), F32),
        V((4, half, emb), BF),
        V((4 * half, emb), F32),
        V((4, half, emb), BF),
        V((2, half // 2, emb), BF),
        V((2, half, emb), BF),
        V((half, emb), BF),
        V((2, half, emb), BF),
        V((clips, width), BF),
        V((clips // GROUP, heads * GROUP), F32),
        V((clips // GROUP, heads * GROUP), F32),
        pltpu.SemaphoreType.DMA((11,)),
        pltpu.SemaphoreType.DMA((clips // GROUP,)),
        pltpu.SemaphoreType.DMA((copies,)),
        pltpu.SemaphoreType.DMA((copies,)),
    ]
    anywhere = pl.BlockSpec(memory_space=pl.ANY)
    smem = pl.BlockSpec(memory_space=pltpu.SMEM)
    value_part, score_grad, text_grad = pl.pallas_call(
        functools.partial(main_kernel, (clips, width, head, emb, all_clips)),
        out_shape=(
            jax.ShapeDtypeStruct((rows, width), BF),
            jax.ShapeDtypeStruct((rows, heads * GROUP), BF),
            jax.ShapeDtypeStruct((128, emb), F32),
        ),
        in_specs=[anywhere] * 5 + [smem] * 2,
        out_specs=(anywhere, anywhere, anywhere),
        scratch_shapes=scratch,
        compiler_params=pltpu.CompilerParams(
            collective_id=0, has_side_effects=True, vmem_limit_bytes=60 * 1024 * 1024
        ),
        name="pool_pair_back",
    )(frame_rows, key_t, value_weight, out_weight, texts, logit_scale, logit_bias)
    steps = 8
    grad_frames, grad_texts = pl.pallas_call(
        final_kernel,
        in_specs=[anywhere] * 5,
        out_specs=(anywhere, anywhere),
        out_shape=(
            jax.ShapeDtypeStruct((rows, width), BF),
            jax.ShapeDtypeStruct((128, emb), F32),
        ),
        scratch_shapes=[
            V((rows, width), BF),
            V((rows, heads * GROUP), BF),
            V((heads, width), BF),
            V((heads * GROUP, width), BF),
            V((128, emb), BF),
            V((128, emb), F32),
            V((128, emb), F32),
            pltpu.SemaphoreType.DMA((steps,)),
            pltpu.SemaphoreType.DMA((steps,)),
            pltpu.SemaphoreType.DMA((steps,)),
            pltpu.SemaphoreType.DMA((4,)),
        ],
        compiler_params=pltpu.CompilerParams(vmem_limit_bytes=60 * 1024 * 1024),
        name="frame_grads",
    )(value_part, score_grad, key_t, texts, text_grad)
    return (grad_frames.reshape(clips, frames_here, width), grad_texts)


def solution(mesh):
    in_specs = (P("clip", "tm", None), P(), P(), P(), P(("tm", "clip"), None), P(), P())
    out_specs = (P("clip", "tm", None), P(("tm", "clip"), None))
    return jax.shard_map(local, mesh=mesh, in_specs=in_specs, out_specs=out_specs, check_vma=False)
```
